128 devices in a mesh: section: 4 (over y_hi, core), dp: 32 (over z, y_lo, x).
Axes of the slice: x: 4, y: 4 (y_hi: 2, y_lo: 2; y = y_hi * 2 + y_lo), z: 4, core: 2. Of those that a mesh axis runs over, the one named last changes fastest.
Arguments:
- inputs: bfloat16 [4096, 8192], P('dp'), may hold values from -6 to 6
- cotangent: bfloat16 [4096, 8192], P('dp'), may hold values from -6 to 6
- sample_ids: int32 [32, 4], P('dp'), may hold values from 0 to 4, as said below
- out_bases: bfloat16 [4, 160, 32, 8192], P('section', 'dp'), may hold values from -6 to 6
- in_bases: bfloat16 [4, 160, 32, 8192], P('section', 'dp'), may hold values from -6 to 6
- proj_in: bfloat16 [4, 8192, 256], P('section', 'dp'), may hold values from -0.0625 to 0.0625
- proj_out: bfloat16 [4, 8192, 256], P('section', 'dp'), may hold values from -0.375 to 0.375
- gains: float32 [4, 8192], P('section'), may hold values from 0.1 to 1.9
Outputs:
- out_acts: bfloat16 [4, 4096, 8192], P('section', 'dp')
- in_grads: bfloat16 [4, 4096, 8192], P('section', 'dp')
- new_out_bases: bfloat16 [4, 160, 32, 8192], P('section', 'dp')
- new_in_bases: bfloat16 [4, 160, 32, 8192], P('section', 'dp')
- grad_in: float32 [4, 8192, 256], P('section', 'dp')
- grad_out: float32 [4, 8192, 256], P('section', 'dp')
The draws below stay inside these ranges and needn't reach their ends.
Inputs may be any that keep to these rules, and one draw needn't show every extreme that they name: `sample_ids`: each row names 4 different samples of that dp row's block of 5 stored samples.
All inputs are finite; a program needn't handle non-finite values. Where the reference program divides by a largest or mean magnitude, that divisor is 1e-20 or more.
Results may differ from the reference program's by a relative error of at most 0.04.
Values may be sent and summed in bfloat16 or wider, within the bound.
No kernel may reach another device: no remote copies, remote signals or barrier semaphores. Data moves between devices by JAX's collectives and lax.ppermute only.
A program may use at most 192 MiB of HBM per device.

```python
import jax
import jax.numpy as jnp
from jax import lax

D = 8192
RANK = 256
BLOCK = 128
SEQ = 32
MICRO = 4
SAMPLES = 5
SECTIONS = 4
TOKENS = 4096
ALLSAMPLES = 160
N_DP = 32


def draw_sample_ids(key, part):
    key = jax.random.fold_in(key, 7)
    keys = jax.random.split(key, N_DP)
    orders = jax.vmap(lambda single: jax.random.permutation(single, SAMPLES))(keys)
    return orders[:, :MICRO].astype(jnp.int32)


def spiked(drawn, own_key, source, target, blocks, factor):
    def block_of(position):
        return (jnp.arange(drawn.shape[position]) // (drawn.shape[position] // blocks)).reshape((-1,) + (1,) * (drawn.ndim - 1 - position))

    near = jax.random.permutation(own_key, blocks)[block_of(target)]
    second = (block_of(target) + blocks // 2) % blocks
    return jnp.where((block_of(source) == near) | (block_of(source) == second), factor * drawn, drawn)


def level_of(stream_key, dims, shards, least, largest):
    loudness = 1.0
    for axis_at, parts in shards:
        steps = jax.random.uniform(jax.random.fold_in(jax.random.fold_in(stream_key, 6), axis_at), (parts,), jnp.float32, least / len(shards), largest / len(shards))
        loudness = loudness * jnp.repeat(jnp.exp(steps), dims[axis_at] // parts).reshape((-1,) + (1,) * (len(dims) - 1 - axis_at))
    return loudness


def gaussian(stream_key, extent, deviation, most, cuts=(), kind=jnp.bfloat16):
    entries = deviation * jax.random.normal(stream_key, extent, jnp.float32)
    if cuts:
        entries = entries * level_of(stream_key, extent, cuts, -0.22, 0.18)
    return jnp.clip(entries, -most, most).astype(kind)


def heavy_noise(own_key, extent, width, reach, cuts, heavy, kind=jnp.bfloat16):
    values = width * jax.random.normal(own_key, extent, jnp.float32)
    if cuts:
        values = values * level_of(own_key, extent, cuts, -0.22, 0.18)
    return jnp.clip(spiked(values, jax.random.fold_in(own_key, 3), *heavy), -reach, reach).astype(kind)


def setup_inputs(seed: int = 0) -> dict:
    splits = jax.random.split(jax.random.key(seed), 9)
    inputs = gaussian(splits[0], (TOKENS, D), 1.0, 6.0, ((0, 32),))
    cotangent = heavy_noise(splits[1], (TOKENS, D), 1.0, 6.0, ((0, 32),), (0, 1, 32, 2.75))
    sample_ids = draw_sample_ids(jax.random.fold_in(splits[8], 71), 0)
    out_bases = gaussian(splits[3], (SECTIONS, ALLSAMPLES, SEQ, D), 1.0, 6.0, ((0, 4), (1, 32)))
    in_bases = gaussian(splits[4], (SECTIONS, ALLSAMPLES, SEQ, D), 1.0, 6.0, ((0, 4), (1, 32)))
    proj_in = gaussian(splits[5], (SECTIONS, D, RANK), D ** -0.5, 0.0625, ((0, 4), (1, 32)))
    proj_out = gaussian(splits[6], (SECTIONS, D, RANK), RANK ** -0.5, 0.375, ((0, 4), (1, 32)))
    gains = jnp.clip(1.0 + 0.18 * jax.random.normal(splits[7], (SECTIONS, D), jnp.float32), 0.1, 1.9)
    return dict(inputs=inputs, cotangent=cotangent, sample_ids=sample_ids, out_bases=out_bases, in_bases=in_bases, proj_in=proj_in, proj_out=proj_out, gains=gains)


def block_code(values):
    blocks = values.reshape(values.shape[0], -1, BLOCK)
    scale = lax.optimization_barrier(jnp.max(jnp.abs(blocks), axis=-1)) + 1e-06
    code = (blocks / scale[..., None]).astype(jnp.bfloat16)
    return (code.reshape(values.shape), scale)

def block_value(code, scale):
    blocks = code.astype(jnp.float32).reshape(code.shape[0], -1, BLOCK)
    return (blocks * scale[..., None]).reshape(code.shape)

def forward_layer(height, gain, w_in, w_out):
    hf = height.astype(jnp.float32)
    rstd = lax.rsqrt(lax.optimization_barrier(jnp.mean(hf * hf, axis=-1, keepdims=True)) + 1e-05)
    normed = (hf * rstd * gain).astype(jnp.bfloat16)
    pre = jnp.dot(normed, w_in, preferred_element_type=jnp.float32)
    act = jax.nn.silu(pre).astype(jnp.bfloat16)
    branch = lax.dot_general(act, w_out, (((1,), (1,)), ((), ())), preferred_element_type=jnp.float32)
    return ((hf + branch).astype(jnp.bfloat16), normed, pre, act, rstd)

def backward_layer(grad, height, rstd, pre, gain, w_in, w_out):
    down = jnp.dot(grad, w_out, preferred_element_type=jnp.float32)
    sig = jax.nn.sigmoid(pre)
    dpre = (down * sig * (1.0 + pre * (1.0 - sig))).astype(jnp.bfloat16)
    dnorm = lax.dot_general(dpre, w_in, (((1,), (1,)), ((), ())), preferred_element_type=jnp.float32)
    hf = height.astype(jnp.float32)
    extra = dnorm * gain
    dh = grad.astype(jnp.float32) + rstd * extra - hf * rstd ** 3 * lax.optimization_barrier(jnp.mean(extra * hf, axis=-1, keepdims=True))
    return (dh, dpre)

def reference(inputs, cotangent, sample_ids, out_bases, in_bases, proj_in, proj_out, gains):
    table_out = out_bases.reshape(SECTIONS, N_DP, SAMPLES, SEQ, D)
    table_in = in_bases.reshape(SECTIONS, N_DP, SAMPLES, SEQ, D)
    rows = jnp.arange(N_DP, dtype=jnp.int32)[:, None]
    height = inputs
    saved = []
    acts_list = []
    for s in range(SECTIONS):
        result, normed, pre, act, rstd = forward_layer(height, gains[s], proj_in[s], proj_out[s])
        saved.append((height, normed, pre, act, rstd))
        acts_list.append(result)
        if s < SECTIONS - 1:
            base_out = table_out[s][rows, sample_ids].reshape(TOKENS, D)
            code, scale = block_code(result.astype(jnp.float32) - base_out.astype(jnp.float32))
            value = block_value(code, scale)
            fresh_out = (base_out.astype(jnp.float32) + value).astype(jnp.bfloat16)
            table_out = table_out.at[s, rows, sample_ids].set(fresh_out.reshape(N_DP, MICRO, SEQ, D))
            base_in = table_in[s + 1][rows, sample_ids].reshape(TOKENS, D)
            height = (base_in.astype(jnp.float32) + value).astype(jnp.bfloat16)
            table_in = table_in.at[s + 1, rows, sample_ids].set(height.reshape(N_DP, MICRO, SEQ, D))
    grad = cotangent
    ingrad_list = [None] * SECTIONS
    gin_list = [None] * SECTIONS
    gout_list = [None] * SECTIONS
    for s in range(SECTIONS - 1, -1, -1):
        height, normed, pre, act, rstd = saved[s]
        dh, dpre = backward_layer(grad, height, rstd, pre, gains[s], proj_in[s], proj_out[s])
        ingrad_list[s] = dh.astype(jnp.bfloat16)
        gin_list[s] = lax.dot_general(normed, dpre, (((0,), (0,)), ((), ())), preferred_element_type=jnp.float32)
        gout_list[s] = lax.dot_general(grad, act, (((0,), (0,)), ((), ())), preferred_element_type=jnp.float32)
        if s > 0:
            gcode, gscale = block_code(dh)
            grad = block_value(gcode, gscale).astype(jnp.bfloat16)
    return (jnp.stack(acts_list), jnp.stack(ingrad_list), table_out.reshape(SECTIONS, ALLSAMPLES, SEQ, D), table_in.reshape(SECTIONS, ALLSAMPLES, SEQ, D), jnp.stack(gin_list), jnp.stack(gout_list))
```

```python
import functools

import jax
import jax.numpy as jnp
from jax import lax
from jax.experimental import pallas as pl
from jax.experimental.pallas import tpu as pltpu
from jax.sharding import PartitionSpec as P

D = 8192
RANK = 256
BLOCK = 128
SEQ = 32
MICRO = 4
SECTIONS = 4
NZ, NY, NX = 4, 2, 4
PIECE = 256
PER = 8
WIDE = D + BLOCK
F32 = jnp.float32
BF16 = jnp.bfloat16
VM = pl.BlockSpec(memory_space=pltpu.VMEM)
SM = pl.BlockSpec(memory_space=pltpu.SMEM)
HB = pl.BlockSpec(memory_space=pltpu.HBM)
NN = (((1,), (0,)), ((), ()))
NT = (((1,), (1,)), ((), ()))


def vmem(value):
    return pltpu.with_memory_space_constraint(value, pltpu.VMEM)


def vshape(shape, dtype):
    return pltpu.VMEM(shape, dtype)


def mm(a, b, dims):
    return lax.dot_general(a, b, dims, preferred_element_type=F32)


def in_offset(meta, r, q, p):
    z = lax.rem(meta[0] + r, NZ)
    x = lax.rem(meta[2] + q, NX)
    y = lax.rem(meta[1] + p, NY)
    return pl.multiple_of((z * NY * NX + y * NX + x) * PIECE, PIECE)


def out_offset(meta, r, q, p):
    x = lax.rem(meta[2] + r, NX)
    z = lax.rem(meta[0] + q, NZ)
    y = lax.rem(meta[1] + p, NY)
    return pl.multiple_of((z * NY * NX + y * NX + x) * PIECE, PIECE)


def scale_at(scales, block):
    lane = lax.broadcasted_iota(jnp.int32, scales.shape, 1)
    return jnp.sum(jnp.where(lane == block, scales, 0.0), axis=1, keepdims=True)


def coded(values):
    top = jnp.max(jnp.abs(values), axis=1, keepdims=True) + 1e-06
    scale = top.astype(BF16).astype(F32)
    code = (values * (1.0 / scale)).astype(BF16)
    return code, scale


def forward_kernel(
    tick, meta, code, base_in, base_out, gain, wi0, wi1, wi2, wi3, wo0, wo1, wo2, wo3,
    heights_, pres_, rstds_, acts_, results_, new_in_, new_out_,
    code_new, heights, pres, rstds, acts, results, new_in, new_out,
    result_buf, fresh_buf, sems,
):
    w_in = (wi0, wi1, wi2, wi3)
    w_out = (wo0, wo1, wo2, wo3)
    section = meta[3]
    slot = tick - section

    @pl.when((slot >= 0) & (slot < MICRO))
    def _():
        sample = meta[4 + slot]
        rows = pl.ds(pl.multiple_of(slot * SEQ, SEQ), SEQ)

        @pl.when(section > 0)
        def _():
            scales = code[:, D:].astype(F32)

            def decode(b, _):
                lanes = pl.ds(pl.multiple_of(b * BLOCK, BLOCK), BLOCK)
                value = code[:, lanes].astype(F32) * scale_at(scales, b)
                heights[rows, lanes] = (base_in[slot, :, lanes].astype(F32) + value).astype(BF16)
                return 0

            lax.fori_loop(0, D // BLOCK, decode, 0, unroll=8)
            pltpu.make_async_copy(heights.at[rows], new_in.at[sample], sems.at[0]).start()

        pre = jnp.zeros((SEQ, RANK), F32)
        square = jnp.zeros((SEQ, PIECE), F32)
        for r in range(NZ):
            for q in range(NX):
                for p in range(NY):
                    lanes = pl.ds(in_offset(meta, r, q, p), PIECE)
                    h = heights[rows, lanes].astype(F32)
                    square += h * h
                    scaled = (h * gain[:, lanes]).astype(BF16)
                    k = (q * NY + p) * PIECE
                    pre += mm(scaled, w_in[r][k : k + PIECE, :], NN)
        rstd = lax.rsqrt(jnp.sum(square, axis=1, keepdims=True) * (1.0 / D) + 1e-05)
        pre = pre * rstd
        act = (pre / (1.0 + jnp.exp(-pre))).astype(BF16)
        pres[rows, :] = pre
        rstds[rows, :] = jnp.broadcast_to(rstd, (SEQ, BLOCK))
        acts[rows, :] = act
        lane = lax.broadcasted_iota(jnp.int32, (SEQ, BLOCK), 1)
        scales_new = jnp.zeros((SEQ, BLOCK), F32)
        for r in range(NX):
            for q in range(NZ):
                for p in range(NY):
                    k = (q * NY + p) * PIECE
                    offset = out_offset(meta, r, q, p)
                    branch = mm(act, w_out[r][k : k + PIECE, :], NT)
                    for half in range(PIECE // BLOCK):
                        at = pl.multiple_of(offset + half * BLOCK, BLOCK)
                        lanes = pl.ds(at, BLOCK)
                        part = branch[:, half * BLOCK : (half + 1) * BLOCK]
                        result = (heights[rows, lanes].astype(F32) + part).astype(BF16)
                        result_buf[:, lanes] = result
                        base = base_out[slot, :, lanes].astype(F32)
                        new, scale = coded(result.astype(F32) - base)
                        code_new[:, lanes] = new
                        fresh_buf[:, lanes] = (base + new.astype(F32) * scale).astype(BF16)
                        scales_new = jnp.where(lane == at // BLOCK, scale, scales_new)
        code_new[:, D:] = scales_new.astype(BF16)
        pltpu.make_async_copy(result_buf, results.at[rows], sems.at[1]).start()

        @pl.when(section < SECTIONS - 1)
        def _():
            copy = pltpu.make_async_copy(fresh_buf, new_out.at[sample], sems.at[2])
            copy.start()
            copy.wait()

        @pl.when(section > 0)
        def _():
            pltpu.make_async_copy(heights.at[rows], new_in.at[sample], sems.at[0]).wait()

        pltpu.make_async_copy(result_buf, results.at[rows], sems.at[1]).wait()


def forward_tick(tick, meta, code, base_in, base_out, gain, w_in, w_out, state):
    heights, pres, rstds, acts, results, new_in, new_out = state
    out = pl.pallas_call(
        functools.partial(forward_kernel, tick),
        out_shape=(
            vshape((SEQ, WIDE), BF16),
            vshape(heights.shape, BF16),
            vshape(pres.shape, F32),
            vshape(rstds.shape, F32),
            vshape(acts.shape, BF16),
            jax.ShapeDtypeStruct(results.shape, BF16),
            jax.ShapeDtypeStruct(new_in.shape, BF16),
            jax.ShapeDtypeStruct(new_out.shape, BF16),
        ),
        in_specs=[SM] + [VM] * 12 + [VM] * 4 + [HB] * 3,
        out_specs=(VM,) * 5 + (HB,) * 3,
        scratch_shapes=[
            pltpu.VMEM((SEQ, D), BF16),
            pltpu.VMEM((SEQ, D), BF16),
            pltpu.SemaphoreType.DMA((3,)),
        ],
        input_output_aliases={13: 1, 14: 2, 15: 3, 16: 4, 17: 5, 18: 6, 19: 7},
        compiler_params=pltpu.CompilerParams(vmem_limit_bytes=20 * 2**20),
        cost_estimate=pl.CostEstimate(flops=2 * 2 * SEQ * D * RANK, bytes_accessed=10 * 2**20, transcendentals=0),
        name="forward_tick",
    )(
        meta, vmem(code), vmem(base_in), vmem(base_out), vmem(gain),
        *[vmem(w) for w in w_in], *[vmem(w) for w in w_out],
        vmem(heights), vmem(pres), vmem(rstds), vmem(acts), results, new_in, new_out,
    )
    return out[0], out[1:]


def backward_kernel(
    tick, meta, code, heights, pres, rstds, gain, wi0, wi1, wi2, wi3, wo0, wo1, wo2, wo3,
    grads_, dpres_, ingrads_,
    code_new, grads, dpres, ingrads,
    dh_buf, sems,
):
    w_in = (wi0, wi1, wi2, wi3)
    w_out = (wo0, wo1, wo2, wo3)
    section = meta[3]
    slot = tick - (SECTIONS - 1 - section)

    @pl.when((slot >= 0) & (slot < MICRO))
    def _():
        rows = pl.ds(pl.multiple_of(slot * SEQ, SEQ), SEQ)

        @pl.when(section < SECTIONS - 1)
        def _():
            scales = code[:, D:].astype(F32)

            def decode(b, _):
                lanes = pl.ds(pl.multiple_of(b * BLOCK, BLOCK), BLOCK)
                value = code[:, lanes].astype(F32) * scale_at(scales, b)
                grads[rows, lanes] = value.astype(BF16)
                return 0

            lax.fori_loop(0, D // BLOCK, decode, 0, unroll=8)

        down = jnp.zeros((SEQ, RANK), F32)
        for r in range(NX):
            for q in range(NZ):
                for p in range(NY):
                    k = (q * NY + p) * PIECE
                    lanes = pl.ds(out_offset(meta, r, q, p), PIECE)
                    down += mm(grads[rows, lanes], w_out[r][k : k + PIECE, :], NN)
        pre = pres[rows, :]
        rstd = rstds[rows, :]
        sig = 1.0 / (1.0 + jnp.exp(-pre))
        dpre = (down * sig * (1.0 + pre * (1.0 - sig))).astype(BF16)
        dpres[rows, :] = dpre
        inner = jnp.sum(dpre.astype(F32) * pre, axis=1, keepdims=True) * (1.0 / D)
        pull = rstd * rstd * inner
        lane = lax.broadcasted_iota(jnp.int32, (SEQ, BLOCK), 1)
        scales_new = jnp.zeros((SEQ, BLOCK), F32)
        for r in range(NZ):
            for q in range(NX):
                for p in range(NY):
                    k = (q * NY + p) * PIECE
                    offset = in_offset(meta, r, q, p)
                    dnorm = mm(dpre, w_in[r][k : k + PIECE, :], NT)
                    for half in range(PIECE // BLOCK):
                        at = pl.multiple_of(offset + half * BLOCK, BLOCK)
                        lanes = pl.ds(at, BLOCK)
                        extra = dnorm[:, half * BLOCK : (half + 1) * BLOCK] * gain[:, lanes]
                        dh = (
                            grads[rows, lanes].astype(F32)
                            + rstd * extra
                            - heights[rows, lanes].astype(F32) * pull
                        )
                        dh_buf[:, lanes] = dh.astype(BF16)
                        new, scale = coded(dh)
                        code_new[:, lanes] = new
                        scales_new = jnp.where(lane == at // BLOCK, scale, scales_new)
        code_new[:, D:] = scales_new.astype(BF16)
        copy = pltpu.make_async_copy(dh_buf, ingrads.at[rows], sems.at[0])
        copy.start()
        copy.wait()


def backward_tick(tick, meta, code, heights, pres, rstds, gain, w_in, w_out, state):
    grads, dpres, ingrads = state
    out = pl.pallas_call(
        functools.partial(backward_kernel, tick),
        out_shape=(
            vshape((SEQ, WIDE), BF16),
            vshape(grads.shape, BF16),
            vshape(dpres.shape, BF16),
            jax.ShapeDtypeStruct(ingrads.shape, BF16),
        ),
        in_specs=[SM] + [VM] * 13 + [VM] * 2 + [HB],
        out_specs=(VM,) * 3 + (HB,),
        scratch_shapes=[pltpu.VMEM((SEQ, D), BF16), pltpu.SemaphoreType.DMA((1,))],
        input_output_aliases={14: 1, 15: 2, 16: 3},
        compiler_params=pltpu.CompilerParams(vmem_limit_bytes=20 * 2**20),
        cost_estimate=pl.CostEstimate(flops=2 * 2 * SEQ * D * RANK, bytes_accessed=10 * 2**20, transcendentals=0),
        name="backward_tick",
    )(
        meta, vmem(code), vmem(heights), vmem(pres), vmem(rstds), vmem(gain),
        *[vmem(w) for w in w_in], *[vmem(w) for w in w_out],
        vmem(grads), vmem(dpres), ingrads,
    )
    return out[0], out[1:]


def weight_grad_kernel(meta, heights, grads, rstds, dpres, acts, gain, *outs):
    gin, gout = outs[:NZ], outs[NZ:]
    left_in = (dpres[...].astype(F32) * rstds[:, :1]).T.astype(BF16)
    left_out = acts[...].astype(F32).T.astype(BF16)
    for r in range(NZ):
        for i in range(PER):
            z = lax.rem(meta[0] + r, NZ)
            lanes = pl.ds(pl.multiple_of((z * PER + i) * PIECE, PIECE), PIECE)
            scaled = (heights[:, lanes].astype(F32) * gain[:, lanes]).astype(BF16)
            gin[r][:, i * PIECE : (i + 1) * PIECE] = mm(left_in, scaled, NN).astype(BF16)
    for r in range(NX):
        for i in range(PER):
            x = lax.rem(meta[2] + r, NX)
            lanes = pl.ds(pl.multiple_of((i * NX + x) * PIECE, PIECE), PIECE)
            gout[r][:, i * PIECE : (i + 1) * PIECE] = mm(left_out, grads[:, lanes], NN).astype(BF16)


def weight_grads(meta, heights, grads, rstds, dpres, acts, gain):
    return pl.pallas_call(
        weight_grad_kernel,
        out_shape=tuple(vshape((RANK, PER * PIECE), BF16) for _ in range(NZ + NX)),
        in_specs=[SM] + [VM] * 6,
        out_specs=(VM,) * (NZ + NX),
        compiler_params=pltpu.CompilerParams(vmem_limit_bytes=20 * 2**20),
        cost_estimate=pl.CostEstimate(flops=4 * 128 * D * RANK, bytes_accessed=12 * 2**20, transcendentals=0),
        name="weight_grads",
    )(meta, *[vmem(v) for v in (heights, grads, rstds, dpres, acts, gain)])


def sum_one_kernel(meta, *refs):
    gin, gout, outs = refs[:NZ], refs[NZ : NZ + NX], refs[NZ + NX :]
    for r in range(NX):
        for y in range(NY):
            x = lax.rem(meta[2] + r, NX)
            lanes = pl.ds(pl.multiple_of((y * NX + x) * PIECE, PIECE), PIECE)
            total = sum(ref[:, lanes].astype(F32) for ref in gin)
            outs[r][:, y * PIECE : (y + 1) * PIECE] = total.astype(BF16)
    for r in range(NZ):
        for y in range(NY):
            z = lax.rem(meta[0] + r, NZ)
            lanes = pl.ds(pl.multiple_of((z * NY + y) * PIECE, PIECE), PIECE)
            total = sum(ref[:, lanes].astype(F32) for ref in gout)
            outs[NX + r][:, y * PIECE : (y + 1) * PIECE] = total.astype(BF16)


def sum_two_kernel(meta, *refs):
    gin, gout, (keep, send) = refs[:NX], refs[NX : NX + NZ], refs[NX + NZ :]
    for which, group in enumerate((gin, gout)):
        for p, out in enumerate((keep, send)):
            y = lax.rem(meta[1] + p, NY)
            lanes = pl.ds(pl.multiple_of(y * PIECE, PIECE), PIECE)
            out[which] = sum(ref[:, lanes].astype(F32) for ref in group).astype(BF16)


def sum_three_kernel(keep, got, gin, gout):
    gin[...] = (keep[0].astype(F32) + got[0].astype(F32)).T
    gout[...] = (keep[1].astype(F32) + got[1].astype(F32)).T


def small_call(kernel, name, shapes, *args, smem_first=True):
    return pl.pallas_call(
        kernel,
        out_shape=shapes,
        in_specs=([SM] if smem_first else []) + [VM] * (len(args) - smem_first),
        out_specs=(VM,) * len(shapes),
        compiler_params=pltpu.CompilerParams(vmem_limit_bytes=20 * 2**20),
        name=name,
    )(*[a if smem_first and i == 0 else vmem(a) for i, a in enumerate(args)])


def place(z, y, x):
    return (z * NY + y) * NX + x


def moved(value, shift):
    dz, dy, dx = shift
    pairs = []
    for z in range(NZ):
        for y in range(NY):
            for x in range(NX):
                source = place((z + dz) % NZ, (y + dy) % NY, (x + dx) % NX)
                pairs.append((source, place(z, y, x)))
    return lax.ppermute(value, "dp", pairs)


def gathered(shard_in, shard_out):
    both = jnp.concatenate([shard_in, shard_out], axis=0)
    other = moved(both, (0, 1, 0))
    pair_in = jnp.concatenate([shard_in, other[:PIECE]], axis=0)
    pair_out = jnp.concatenate([shard_out, other[PIECE:]], axis=0)
    four_in = jnp.concatenate([pair_in] + [moved(pair_in, (0, 0, r)) for r in (1, 2, 3)], axis=0)
    four_out = jnp.concatenate([pair_out] + [moved(pair_out, (r, 0, 0)) for r in (1, 2, 3)], axis=0)
    w_in = [four_in] + [moved(four_in, (r, 0, 0)) for r in (1, 2, 3)]
    w_out = [four_out] + [moved(four_out, (0, 0, r)) for r in (1, 2, 3)]
    return w_in, w_out


def reduced(meta, parts):
    gin, gout = parts[:NZ], parts[NZ:]
    gin = [gin[0]] + [moved(gin[r], (-r, 0, 0)) for r in (1, 2, 3)]
    gout = [gout[0]] + [moved(gout[r], (0, 0, -r)) for r in (1, 2, 3)]
    shapes = tuple(vshape((RANK, NY * PIECE), BF16) for _ in range(NX + NZ))
    two = small_call(sum_one_kernel, "sum_one", shapes, meta, *gin, *gout)
    gin, gout = two[:NX], two[NX:]
    gin = [gin[0]] + [moved(gin[r], (0, 0, -r)) for r in (1, 2, 3)]
    gout = [gout[0]] + [moved(gout[r], (-r, 0, 0)) for r in (1, 2, 3)]
    shapes = (vshape((2, RANK, PIECE), BF16),) * 2
    keep, send = small_call(sum_two_kernel, "sum_two", shapes, meta, *gin, *gout)
    got = moved(send, (0, 1, 0))
    shapes = (jax.ShapeDtypeStruct((PIECE, RANK), F32),) * 2
    return small_call(sum_three_kernel, "sum_three", shapes, keep, got, smem_first=False)


def body(inputs, cotangent, sample_ids, out_bases, in_bases, proj_in, proj_out, gains):
    section = lax.axis_index("section")
    dp = lax.axis_index("dp")
    chosen = sample_ids[0]
    meta = jnp.concatenate(
        [
            jnp.stack([dp // (NY * NX), (dp // NX) % NY, dp % NX, section]).astype(jnp.int32),
            chosen,
        ]
    )
    table_out = out_bases[0]
    table_in = in_bases[0]
    base_out = jnp.stack([lax.dynamic_index_in_dim(table_out, chosen[j], 0, False) for j in range(MICRO)])
    base_in = jnp.stack([lax.dynamic_index_in_dim(table_in, chosen[j], 0, False) for j in range(MICRO)])
    w_in, w_out = gathered(proj_in[0], proj_out[0])
    tokens = MICRO * SEQ
    state = (
        inputs,
        jnp.zeros((tokens, RANK), F32),
        jnp.zeros((tokens, BLOCK), F32),
        jnp.zeros((tokens, RANK), BF16),
        jnp.zeros((tokens, D), BF16),
        table_in,
        table_out,
    )
    code = jnp.zeros((SEQ, WIDE), BF16)
    for tick in range(MICRO + SECTIONS - 1):
        code, state = forward_tick(tick, meta, code, base_in, base_out, gains, w_in, w_out, state)
        pairs = [(s, s + 1) for s in range(SECTIONS - 1) if 0 <= tick - s < MICRO]
        if pairs:
            code = lax.ppermute(code, "section", pairs)
    heights, pres, rstds, acts, results, new_in, new_out = state
    state = (cotangent, jnp.zeros((tokens, RANK), BF16), jnp.zeros((tokens, D), BF16))
    code = jnp.zeros((SEQ, WIDE), BF16)
    for tick in range(MICRO + SECTIONS - 1):
        code, state = backward_tick(tick, meta, code, heights, pres, rstds, gains, w_in, w_out, state)
        pairs = [(s, s - 1) for s in range(1, SECTIONS) if 0 <= tick - (SECTIONS - 1 - s) < MICRO]
        if pairs:
            code = lax.ppermute(code, "section", pairs)
    grads, dpres, ingrads = state
    parts = weight_grads(meta, heights, grads, rstds, dpres, acts, gains)
    grad_in, grad_out = reduced(meta, parts)
    return results[None], ingrads[None], new_out[None], new_in[None], grad_in[None], grad_out[None]


def solution(mesh):
    in_specs = (
        P("dp", None),
        P("dp", None),
        P("dp", None),
        P("section", "dp", None, None),
        P("section", "dp", None, None),
        P("section", "dp", None),
        P("section", "dp", None),
        P("section", None),
    )
    out_specs = (
        P("section", "dp", None),
        P("section", "dp", None),
        P("section", "dp", None, None),
        P("section", "dp", None, None),
        P("section", "dp", None),
        P("section", "dp", None),
    )
    return jax.shard_map(body, mesh=mesh, in_specs=in_specs, out_specs=out_specs, check_vma=False)
```

```python
import functools

import jax
import jax.numpy as jnp
from jax import lax
from jax.experimental import pallas as pl
from jax.experimental.pallas import tpu as pltpu
from jax.sharding import PartitionSpec as P

D = 8192
RANK = 256
BLOCK = 128
SEQ = 32
MICRO = 4
SECTIONS = 4
TOKENS = MICRO * SEQ
NZ, NY, NX = 4, 2, 4
PIECE = 256
WIDE = D + BLOCK
F32 = jnp.float32
BF16 = jnp.bfloat16
VM = pl.BlockSpec(memory_space=pltpu.VMEM)
SM = pl.BlockSpec(memory_space=pltpu.SMEM)
HB = pl.BlockSpec(memory_space=pltpu.HBM)
ANY = pl.BlockSpec(memory_space=pl.ANY)
NN = (((1,), (0,)), ((), ()))
NT = (((1,), (1,)), ((), ()))
FORWARD_AT = (0, 1, 3, 4)
BACKWARD_AT = (4, 3, 1, 0)
TICKS = MICRO + 4
SLOW = (1, 2)


def vmem(value):
    return pltpu.with_memory_space_constraint(value, pltpu.VMEM)


def vshape(shape, dtype):
    return pltpu.VMEM(shape, dtype)


def hshape(shape, dtype):
    return jax.ShapeDtypeStruct(shape, dtype)


def params():
    return pltpu.CompilerParams(vmem_limit_bytes=12 * 2**20)


def mm(a, b, dims):
    return lax.dot_general(a, b, dims, preferred_element_type=F32)


def coded(values):
    top = jnp.max(jnp.abs(values), axis=1, keepdims=True) + 1e-06
    scale = top.astype(BF16).astype(F32)
    code = (values * (1.0 / scale)).astype(BF16)
    return code, scale


def received(codes, section, lanes):
    if len(codes) == 1:
        return codes[0][:, lanes]
    fast, slow, here = codes[0], codes[1], section
    return jnp.where(here, slow[:, lanes], fast[:, lanes])


def fetch_kernel(meta, table_in, table_out, base_in, base_out, *rest):
    sems = rest[-1]
    copies = []
    for j in range(MICRO):
        copies.append(pltpu.make_async_copy(table_in.at[meta[4 + j]], base_in.at[j], sems.at[2 * j]))
        copies.append(pltpu.make_async_copy(table_out.at[meta[4 + j]], base_out.at[j], sems.at[2 * j + 1]))
    for copy in copies:
        copy.start()
    for copy in copies:
        copy.wait()


def fetch(meta, table_in, table_out):
    shape = (MICRO, SEQ, D)
    return pl.pallas_call(
        fetch_kernel,
        out_shape=(
            vshape(shape, BF16),
            vshape(shape, BF16),
            vshape((TOKENS, RANK), F32),
            vshape((TOKENS, BLOCK), F32),
            vshape((TOKENS, RANK), BF16),
            vshape((TOKENS, RANK), BF16),
            hshape((TOKENS, D), BF16),
            hshape((TOKENS, D), BF16),
        ),
        in_specs=[SM, ANY, ANY],
        out_specs=(VM,) * 6 + (HB,) * 2,
        scratch_shapes=[pltpu.SemaphoreType.DMA((2 * MICRO,))],
        compiler_params=params(),
        name="fetch",
    )(meta, table_in, table_out)


def assemble_kernel(meta, *refs):
    parts_in, parts_out, full_in, full_out, sems = refs[:5], refs[5:10], refs[10], refs[11], refs[12]
    copies = []
    for parts, full, first in ((parts_in, full_in, True), (parts_out, full_out, False)):
        blocks = [(parts[0], 0, 0, 4), (parts[1], 1, 0, 4), (parts[2], 3, 0, 4), (parts[3], 2, 0, 2), (parts[4], 2, 2, 4)]
        for ref, r, start, stop in blocks:
            for q in range(start, stop):
                for p in range(NY):
                    z = lax.rem(meta[0] + (r if first else q), NZ)
                    x = lax.rem(meta[2] + (q if first else r), NX)
                    y = lax.rem(meta[1] + p, NY)
                    at = pl.multiple_of((z * NY * NX + y * NX + x) * PIECE, PIECE)
                    k = ((q - start) * NY + p) * PIECE
                    copies.append(
                        pltpu.make_async_copy(ref.at[pl.ds(k, PIECE)], full.at[pl.ds(at, PIECE)], sems.at[len(copies)])
                    )
    for copy in copies:
        copy.start()
    for copy in copies:
        copy.wait()


def assemble(meta, parts_in, parts_out):
    return pl.pallas_call(
        assemble_kernel,
        out_shape=(vshape((D, RANK), BF16),) * 2,
        in_specs=[SM] + [ANY] * 10,
        out_specs=(VM,) * 2,
        scratch_shapes=[pltpu.SemaphoreType.DMA((64,))],
        compiler_params=params(),
        name="assemble",
    )(meta, *parts_in, *parts_out)


def pack_kernel(*refs):
    parts, out, sems = refs[:-2], refs[-2], refs[-1]
    copies, at = [], 0
    for i, ref in enumerate(parts):
        copies.append(pltpu.make_async_copy(ref, out.at[pl.ds(at, ref.shape[0])], sems.at[i]))
        at += ref.shape[0]
    for copy in copies:
        copy.start()
    for copy in copies:
        copy.wait()


def pack(*parts):
    rows = sum(part.shape[0] for part in parts)
    return pl.pallas_call(
        pack_kernel,
        out_shape=vshape((rows,) + parts[0].shape[1:], parts[0].dtype),
        in_specs=[ANY] * len(parts),
        out_specs=VM,
        scratch_shapes=[pltpu.SemaphoreType.DMA((len(parts),))],
        compiler_params=params(),
        name="pack",
    )(*parts)


def forward_kernel(tick, n_codes, meta, *refs):
    codes, refs = refs[:n_codes], refs[n_codes:]
    (
        base_in, base_out, gain, w_in, w_out, heights_, pres_, rstds_, acts_, results_, new_in_, new_out_,
        code_new, heights, pres, rstds, acts, results, new_in, new_out,
        result_buf, fresh_buf, sum_buf, square_buf, sems,
    ) = refs
    section = meta[3]
    slot = tick - (section + (section >= SLOW[1]).astype(jnp.int32))

    @pl.when((slot >= 0) & (slot < MICRO))
    def _():
        sample = meta[4 + slot]
        rows = pl.ds(pl.multiple_of(slot * SEQ, SEQ), SEQ)

        def project(decode):
            if decode:
                scales = received(codes, section == SLOW[1], slice(D, WIDE)).astype(F32)
            pre = jnp.zeros((SEQ, RANK), F32)
            square = jnp.zeros((SEQ, BLOCK), F32)
            for i in range(D // PIECE):
                scaled = []
                for half in range(PIECE // BLOCK):
                    b = i * (PIECE // BLOCK) + half
                    lanes = slice(b * BLOCK, (b + 1) * BLOCK)
                    if decode:
                        value = received(codes, section == SLOW[1], lanes).astype(F32) * scales[:, b : b + 1]
                        height = (base_in[slot, :, lanes].astype(F32) + value).astype(BF16)
                        heights[rows, lanes] = height
                    else:
                        height = heights[rows, lanes]
                    h = height.astype(F32)
                    square += h * h
                    scaled.append((h * gain[:, lanes]).astype(BF16))
                pre += mm(jnp.concatenate(scaled, axis=1), w_in[i * PIECE : (i + 1) * PIECE, :], NN)
            sum_buf[...] = pre
            square_buf[...] = square

        if codes:

            @pl.when(section > 0)
            def _():
                project(True)
                pltpu.make_async_copy(heights.at[rows], new_in.at[sample], sems.at[0]).start()

        @pl.when(section == 0)
        def _():
            project(False)

        rstd = lax.rsqrt(jnp.sum(square_buf[...], axis=1, keepdims=True) * (1.0 / D) + 1e-05)
        pre = sum_buf[...] * rstd
        act = (pre / (1.0 + jnp.exp(-pre))).astype(BF16)
        pres[rows, :] = pre
        rstds[rows, :] = jnp.broadcast_to(rstd, (SEQ, BLOCK))
        acts[rows, :] = act
        lane = lax.broadcasted_iota(jnp.int32, (SEQ, BLOCK), 1)
        scales_new = jnp.zeros((SEQ, BLOCK), F32)
        for i in range(D // PIECE):
            branch = mm(act, w_out[i * PIECE : (i + 1) * PIECE, :], NT)
            for half in range(PIECE // BLOCK):
                b = i * (PIECE // BLOCK) + half
                lanes = slice(b * BLOCK, (b + 1) * BLOCK)
                part = branch[:, half * BLOCK : (half + 1) * BLOCK]
                result = (heights[rows, lanes].astype(F32) + part).astype(BF16)
                result_buf[:, lanes] = result
                base = base_out[slot, :, lanes].astype(F32)
                new, scale = coded(result.astype(F32) - base)
                code_new[:, lanes] = new
                fresh_buf[:, lanes] = (base + new.astype(F32) * scale).astype(BF16)
                scales_new = jnp.where(lane == b, scale, scales_new)
        code_new[:, D:] = scales_new.astype(BF16)
        pltpu.make_async_copy(result_buf, results.at[rows], sems.at[1]).start()

        @pl.when(section < SECTIONS - 1)
        def _():
            copy = pltpu.make_async_copy(fresh_buf, new_out.at[sample], sems.at[2])
            copy.start()
            copy.wait()

        if codes:

            @pl.when(section > 0)
            def _():
                pltpu.make_async_copy(heights.at[rows], new_in.at[sample], sems.at[0]).wait()

        pltpu.make_async_copy(result_buf, results.at[rows], sems.at[1]).wait()


def forward_tick(tick, meta, codes, base_in, base_out, gain, w_in, w_out, state):
    heights, pres, rstds, acts, results, new_in, new_out = state
    first = 1 + len(codes) + 5
    out = pl.pallas_call(
        functools.partial(forward_kernel, tick, len(codes)),
        out_shape=(
            vshape((SEQ, WIDE), BF16),
            vshape(heights.shape, BF16),
            vshape(pres.shape, F32),
            vshape(rstds.shape, F32),
            vshape(acts.shape, BF16),
            hshape(results.shape, BF16),
            hshape(new_in.shape, BF16),
            hshape(new_out.shape, BF16),
        ),
        in_specs=[SM] + [VM] * (len(codes) + 5 + 4) + [HB] * 3,
        out_specs=(VM,) * 5 + (HB,) * 3,
        scratch_shapes=[
            pltpu.VMEM((SEQ, D), BF16),
            pltpu.VMEM((SEQ, D), BF16),
            pltpu.VMEM((SEQ, RANK), F32),
            pltpu.VMEM((SEQ, BLOCK), F32),
            pltpu.SemaphoreType.DMA((3,)),
        ],
        input_output_aliases={first + i: 1 + i for i in range(7)},
        compiler_params=params(),
        cost_estimate=pl.CostEstimate(flops=2 * 2 * SEQ * D * RANK, bytes_accessed=16 * 2**20, transcendentals=0),
        name="forward_tick",
    )(
        meta, *map(vmem, codes), vmem(base_in), vmem(base_out), vmem(gain), vmem(w_in), vmem(w_out),
        vmem(heights), vmem(pres), vmem(rstds), vmem(acts), results, new_in, new_out,
    )
    return out[0], out[1:]


def backward_kernel(tick, n_codes, meta, *refs):
    codes, refs = refs[:n_codes], refs[n_codes:]
    (
        heights, pres, rstds, gain, w_in, w_out, grads_, dpres_, ingrads_,
        code_new, grads, dpres, ingrads,
        dh_buf, sum_buf, sems,
    ) = refs
    section = meta[3]
    slot = tick - (SECTIONS - 1 - section + (section <= SLOW[0]).astype(jnp.int32))

    @pl.when((slot >= 0) & (slot < MICRO))
    def _():
        rows = pl.ds(pl.multiple_of(slot * SEQ, SEQ), SEQ)

        def project(decode):
            if decode:
                scales = received(codes, section == SLOW[0], slice(D, WIDE)).astype(F32)
            down = jnp.zeros((SEQ, RANK), F32)
            for i in range(D // PIECE):
                if decode:
                    for half in range(PIECE // BLOCK):
                        b = i * (PIECE // BLOCK) + half
                        lanes = slice(b * BLOCK, (b + 1) * BLOCK)
                        value = received(codes, section == SLOW[0], lanes).astype(F32) * scales[:, b : b + 1]
                        grads[rows, lanes] = value.astype(BF16)
                piece = slice(i * PIECE, (i + 1) * PIECE)
                down += mm(grads[rows, piece], w_out[piece, :], NN)
            sum_buf[...] = down

        if codes:

            @pl.when(section < SECTIONS - 1)
            def _():
                project(True)

        @pl.when(section == SECTIONS - 1)
        def _():
            project(False)

        pre = pres[rows, :]
        rstd = rstds[rows, :]
        sig = 1.0 / (1.0 + jnp.exp(-pre))
        dpre = (sum_buf[...] * sig * (1.0 + pre * (1.0 - sig))).astype(BF16)
        dpres[rows, :] = dpre
        inner = jnp.sum(dpre.astype(F32) * pre, axis=1, keepdims=True) * (1.0 / D)
        pull = rstd * rstd * inner
        lane = lax.broadcasted_iota(jnp.int32, (SEQ, BLOCK), 1)
        scales_new = jnp.zeros((SEQ, BLOCK), F32)
        for i in range(D // PIECE):
            dnorm = mm(dpre, w_in[i * PIECE : (i + 1) * PIECE, :], NT)
            for half in range(PIECE // BLOCK):
                b = i * (PIECE // BLOCK) + half
                lanes = slice(b * BLOCK, (b + 1) * BLOCK)
                extra = dnorm[:, half * BLOCK : (half + 1) * BLOCK] * gain[:, lanes]
                dh = (
                    grads[rows, lanes].astype(F32)
                    + rstd * extra
                    - heights[rows, lanes].astype(F32) * pull
                )
                dh_buf[:, lanes] = dh.astype(BF16)
                new, scale = coded(dh)
                code_new[:, lanes] = new
                scales_new = jnp.where(lane == b, scale, scales_new)
        code_new[:, D:] = scales_new.astype(BF16)
        copy = pltpu.make_async_copy(dh_buf, ingrads.at[rows], sems.at[0])
        copy.start()
        copy.wait()


def backward_tick(tick, meta, codes, heights, pres, rstds, gain, w_in, w_out, state):
    grads, dpres, ingrads = state
    first = 1 + len(codes) + 6
    out = pl.pallas_call(
        functools.partial(backward_kernel, tick, len(codes)),
        out_shape=(
            vshape((SEQ, WIDE), BF16),
            vshape(grads.shape, BF16),
            vshape(dpres.shape, BF16),
            hshape(ingrads.shape, BF16),
        ),
        in_specs=[SM] + [VM] * (len(codes) + 6 + 2) + [HB],
        out_specs=(VM,) * 3 + (HB,),
        scratch_shapes=[
            pltpu.VMEM((SEQ, D), BF16),
            pltpu.VMEM((SEQ, RANK), F32),
            pltpu.SemaphoreType.DMA((1,)),
        ],
        input_output_aliases={first + i: 1 + i for i in range(3)},
        compiler_params=params(),
        cost_estimate=pl.CostEstimate(flops=2 * 2 * SEQ * D * RANK, bytes_accessed=16 * 2**20, transcendentals=0),
        name="backward_tick",
    )(
        meta, *map(vmem, codes), vmem(heights), vmem(pres), vmem(rstds), vmem(gain), vmem(w_in), vmem(w_out),
        vmem(grads), vmem(dpres), ingrads,
    )
    return out[0], out[1:]


def grad_lanes(meta, which, r, i):
    if which == 0:
        z = lax.rem(meta[0] + r, NZ)
        return pl.ds(pl.multiple_of((z * NY * NX + i) * PIECE, PIECE), PIECE)
    x = lax.rem(meta[2] + r, NX)
    return pl.ds(pl.multiple_of((i * NX + x) * PIECE, PIECE), PIECE)


def left_sides(rstds, dpres, acts):
    return (dpres[...].astype(F32) * rstds[:, :1]).T.astype(BF16), acts[...].astype(F32).T.astype(BF16)


def right_side(which, lanes, heights, grads, gain):
    if which == 0:
        return (heights[:, lanes].astype(F32) * gain[:, lanes]).astype(BF16)
    return grads[:, lanes]


def far_grad_kernel(meta, heights, grads, rstds, dpres, acts, gain, *outs):
    left = left_sides(rstds, dpres, acts)
    for which in range(2):
        for i in range(NY * 4):
            product = mm(left[which], right_side(which, grad_lanes(meta, which, 2, i), heights, grads, gain), NN)
            product = product.astype(BF16)
            for half in range(2):
                outs[2 * which + half][:, i * PIECE : (i + 1) * PIECE] = product[half * 128 : (half + 1) * 128]


def near_grad_kernel(meta, heights, grads, rstds, dpres, acts, gain, *outs):
    left = left_sides(rstds, dpres, acts)
    for which in range(2):
        for k, r in enumerate((1, 3, 0)):
            for i in range(NY * 4):
                product = mm(left[which], right_side(which, grad_lanes(meta, which, r, i), heights, grads, gain), NN)
                outs[3 * which + k][:, i * PIECE : (i + 1) * PIECE] = product.astype(BF16)


def add_kernel(*refs):
    for which in range(2):
        ahead, behind, top, bottom = refs[4 * which : 4 * which + 4]
        ahead_new, behind_new = refs[8 + 2 * which : 10 + 2 * which]
        for i in range(4):
            lanes = slice(i * 512, (i + 1) * 512)
            ahead_new[:128, lanes] = (ahead[:128, lanes].astype(F32) + top[:, lanes].astype(F32)).astype(BF16)
            ahead_new[128:, lanes] = ahead[128:, lanes]
            behind_new[:128, lanes] = behind[:128, lanes]
            behind_new[128:, lanes] = (behind[128:, lanes].astype(F32) + bottom[:, lanes].astype(F32)).astype(BF16)


def sum_one_kernel(meta, *refs):
    gin, gout, outs = refs[:3], refs[3:6], refs[6:]
    for r in range(NX):
        for y in range(NY):
            x = lax.rem(meta[2] + r, NX)
            lanes = pl.ds(pl.multiple_of((y * NX + x) * PIECE, PIECE), PIECE)
            total = sum(ref[:, lanes].astype(F32) for ref in gin)
            outs[r][:, y * PIECE : (y + 1) * PIECE] = total.astype(BF16)
    for r in range(NZ):
        for y in range(NY):
            z = lax.rem(meta[0] + r, NZ)
            lanes = pl.ds(pl.multiple_of((z * NY + y) * PIECE, PIECE), PIECE)
            total = sum(ref[:, lanes].astype(F32) for ref in gout)
            outs[NX + r][:, y * PIECE : (y + 1) * PIECE] = total.astype(BF16)


def sum_two_kernel(meta, *refs):
    gin, gout, (keep, send) = refs[:NX], refs[NX : NX + NZ], refs[NX + NZ :]
    for which, group in enumerate((gin, gout)):
        for p, out in enumerate((keep, send)):
            y = lax.rem(meta[1] + p, NY)
            lanes = pl.ds(pl.multiple_of(y * PIECE, PIECE), PIECE)
            out[which] = sum(ref[:, lanes].astype(F32) for ref in group).astype(BF16)


def sum_three_kernel(keep, got, gin, gout):
    gin[...] = (keep[0].astype(F32) + got[0].astype(F32)).T
    gout[...] = (keep[1].astype(F32) + got[1].astype(F32)).T


def small_call(kernel, name, shapes, *args, meta=None):
    scalars = [] if meta is None else [meta]
    return pl.pallas_call(
        kernel,
        out_shape=shapes,
        in_specs=[SM] * len(scalars) + [VM] * len(args),
        out_specs=(VM,) * len(shapes),
        compiler_params=params(),
        name=name,
    )(*scalars, *map(vmem, args))


def place(z, y, x):
    return (z * NY + y) * NX + x


def moved(value, shift):
    dz, dy, dx = shift
    pairs = []
    for z in range(NZ):
        for y in range(NY):
            for x in range(NX):
                source = place((z + dz) % NZ, (y + dy) % NY, (x + dx) % NX)
                pairs.append((source, place(z, y, x)))
    return lax.ppermute(value, "dp", pairs)


def along(axis, steps):
    return (steps, 0, 0) if axis == 0 else (0, 0, steps)


def ring(block, axis):
    after, before = moved(block, along(axis, 1)), moved(block, along(axis, -1))
    half = block.shape[0] // 2
    return [block, after, before, moved(before[:half], along(axis, -1)), moved(after[half:], along(axis, 1))]


def gathered(meta, shard_in, other_in, shard_out, other_out):
    pair_in, pair_out = pack(shard_in, other_in), pack(shard_out, other_out)
    four_in = pack(pair_in, *[moved(pair_in, along(2, r)) for r in (1, 2, 3)])
    four_out = pack(pair_out, *[moved(pair_out, along(0, r)) for r in (1, 2, 3)])
    return assemble(meta, ring(four_in, 0), ring(four_out, 2))


def reduced(meta, operands):
    rows = RANK // 2
    far = small_call(far_grad_kernel, "far_grads", (vshape((rows, 2048), BF16),) * 4, *operands, meta=meta)
    near = small_call(near_grad_kernel, "near_grads", (vshape((RANK, 2048), BF16),) * 6, *operands, meta=meta)
    args, own = [], []
    for which, axis in ((0, 0), (1, 2)):
        top, bottom = far[2 * which : 2 * which + 2]
        ahead, behind, here = near[3 * which : 3 * which + 3]
        args += [ahead, behind, moved(top, along(axis, -1)), moved(bottom, along(axis, 1))]
        own.append(here)
    added = small_call(add_kernel, "add_far", (vshape((RANK, 2048), BF16),) * 4, *args)
    args = []
    for which, axis in ((0, 0), (1, 2)):
        ahead, behind = added[2 * which : 2 * which + 2]
        args += [own[which], moved(ahead, along(axis, -1)), moved(behind, along(axis, 1))]
    shapes = tuple(vshape((RANK, NY * PIECE), BF16) for _ in range(NX + NZ))
    two = small_call(sum_one_kernel, "sum_one", shapes, *args, meta=meta)
    gin, gout = two[:NX], two[NX:]
    gin = [gin[0]] + [moved(gin[r], along(2, -r)) for r in (1, 2, 3)]
    gout = [gout[0]] + [moved(gout[r], along(0, -r)) for r in (1, 2, 3)]
    shapes = (vshape((2, RANK, PIECE), BF16),) * 2
    keep, send = small_call(sum_two_kernel, "sum_two", shapes, *gin, *gout, meta=meta)
    got = moved(send, (0, 1, 0))
    return small_call(sum_three_kernel, "sum_three", (hshape((PIECE, RANK), F32),) * 2, keep, got)


def handed_on(tick, code, sent, at, pairs):
    live = [pair for pair in pairs if 0 <= tick - at[pair[0]] < MICRO]
    quick = [pair for pair in live if set(pair) != set(SLOW)]
    slow = [pair for pair in live if set(pair) == set(SLOW)]
    codes = [lax.ppermute(code, "section", quick)] if quick else []
    if sent is not None:
        codes.append(sent)
    return codes, lax.ppermute(code, "section", slow) if slow else None


def body(inputs, cotangent, sample_ids, out_bases, in_bases, proj_in, proj_out, gains):
    section = lax.axis_index("section")
    dp = lax.axis_index("dp")
    shard_in, shard_out = proj_in[0], proj_out[0]
    other_in, other_out = moved(shard_in, (0, 1, 0)), moved(shard_out, (0, 1, 0))
    other_in, inputs, cotangent, chosen, table_out, table_in = lax.optimization_barrier(
        (other_in, inputs, cotangent, sample_ids[0], out_bases[0], in_bases[0])
    )
    place_ids = jnp.stack([dp // (NY * NX), (dp // NX) % NY, dp % NX, section])
    meta = jnp.concatenate([place_ids.astype(jnp.int32), chosen])
    base_in, base_out, pres, rstds, acts, dpres, results, ingrads = fetch(meta, table_in, table_out)
    w_in, w_out = gathered(meta, shard_in, other_in, shard_out, other_out)
    state = (inputs, pres, rstds, acts, results, table_in, table_out)
    codes, sent = [], None
    for tick in range(TICKS):
        code, state = forward_tick(tick, meta, codes, base_in, base_out, gains, w_in, w_out, state)
        codes, sent = handed_on(tick, code, sent, FORWARD_AT, [(s, s + 1) for s in range(SECTIONS - 1)])
    heights, pres, rstds, acts, results, new_in, new_out = state
    state = (cotangent, dpres, ingrads)
    codes, sent = [], None
    for tick in range(TICKS):
        code, state = backward_tick(tick, meta, codes, heights, pres, rstds, gains, w_in, w_out, state)
        codes, sent = handed_on(tick, code, sent, BACKWARD_AT, [(s, s - 1) for s in range(1, SECTIONS)])
    grads, dpres, ingrads = state
    grad_in, grad_out = reduced(meta, (heights, grads, rstds, dpres, acts, gains))
    return results[None], ingrads[None], new_out[None], new_in[None], grad_in[None], grad_out[None]


def solution(mesh):
    in_specs = (
        P("dp", None),
        P("dp", None),
        P("dp", None),
        P("section", "dp", None, None),
        P("section", "dp", None, None),
        P("section", "dp", None),
        P("section", "dp", None),
        P("section", None),
    )
    out_specs = (
        P("section", "dp", None),
        P("section", "dp", None),
        P("section", "dp", None, None),
        P("section", "dp", None, None),
        P("section", "dp", None),
        P("section", "dp", None),
    )
    return jax.shard_map(body, mesh=mesh, in_specs=in_specs, out_specs=out_specs, check_vma=False)
```

```python
import functools

import jax
import jax.numpy as jnp
from jax import lax
from jax.experimental import pallas as pl
from jax.experimental.pallas import tpu as pltpu
from jax.sharding import PartitionSpec as P

D = 8192
RANK = 256
BLOCK = 128
SEQ = 32
MICRO = 4
SECTIONS = 4
TOKENS = MICRO * SEQ
NZ, NY, NX = 4, 2, 4
PIECE = 256
WIDE = D + BLOCK
F32 = jnp.float32
BF16 = jnp.bfloat16
VM = pl.BlockSpec(memory_space=pltpu.VMEM)
SM = pl.BlockSpec(memory_space=pltpu.SMEM)
HB = pl.BlockSpec(memory_space=pltpu.HBM)
ANY = pl.BlockSpec(memory_space=pl.ANY)
NN = (((1,), (0,)), ((), ()))
NT = (((1,), (1,)), ((), ()))
FORWARD_AT = (0, 1, 3, 4)
BACKWARD_AT = (4, 3, 1, 0)
TICKS = MICRO + 4
SLOW = (1, 2)


def vmem(value):
    return pltpu.with_memory_space_constraint(value, pltpu.VMEM)


def hbm(value):
    return pltpu.with_memory_space_constraint(value, pltpu.HBM)


def vshape(shape, dtype):
    return pltpu.VMEM(shape, dtype)


def hshape(shape, dtype):
    return jax.ShapeDtypeStruct(shape, dtype)


def params():
    return pltpu.CompilerParams(vmem_limit_bytes=12 * 2**20)


def mm(a, b, dims):
    return lax.dot_general(a, b, dims, preferred_element_type=F32)


def coded(values):
    top = jnp.max(jnp.abs(values), axis=1, keepdims=True) + 1e-06
    scale = top.astype(BF16).astype(F32)
    code = (values * (1.0 / scale)).astype(BF16)
    return code, scale


def received(codes, section, lanes):
    if len(codes) == 1:
        return codes[0][:, lanes]
    fast, slow, here = codes[0], codes[1], section
    return jnp.where(here, slow[:, lanes], fast[:, lanes])


def fetch_kernel(inputs, cotangent, table_in, table_out, after, heights, grads, base_in, base_out, *rest):
    sems = rest[-1]
    moves = [(inputs, heights), (cotangent, grads), (table_in, base_in), (table_out, base_out)]
    copies = [pltpu.make_async_copy(source, target, sems.at[i]) for i, (source, target) in enumerate(moves)]
    for copy in copies:
        copy.start()
    for copy in copies:
        copy.wait()


def fetch(inputs, cotangent, table_in, table_out, after):
    return pl.pallas_call(
        fetch_kernel,
        out_shape=(
            vshape(inputs.shape, BF16),
            vshape(cotangent.shape, BF16),
            vshape(table_in.shape, BF16),
            vshape(table_out.shape, BF16),
            vshape((TOKENS, RANK), F32),
            vshape((TOKENS, BLOCK), F32),
            vshape((TOKENS, RANK), BF16),
            vshape((TOKENS, RANK), BF16),
            vshape((TOKENS, D), BF16),
            vshape((TOKENS, D), BF16),
            vshape((TOKENS, D), BF16),
        ),
        in_specs=[HB] * 4 + [ANY],
        out_specs=(VM,) * 11,
        scratch_shapes=[pltpu.SemaphoreType.DMA((4,))],
        compiler_params=params(),
        cost_estimate=pl.CostEstimate(flops=0, bytes_accessed=20 * 2**20, transcendentals=0),
        name="fetch",
    )(hbm(inputs), hbm(cotangent), hbm(table_in), hbm(table_out), after)


def settle(meta, first, full, ref, r, start, stop):
    for q in range(start, stop):
        for p in range(NY):
            z = lax.rem(meta[0] + (r if first else q), NZ)
            x = lax.rem(meta[2] + (q if first else r), NX)
            y = lax.rem(meta[1] + p, NY)
            at = pl.multiple_of((z * NY * NX + y * NX + x) * PIECE, PIECE)
            k = ((q - start) * NY + p) * PIECE
            full[pl.ds(at, PIECE), :] = ref[k : k + PIECE, :]


def near_kernel(meta, *refs):
    for which in range(2):
        own, after, before = refs[3 * which : 3 * which + 3]
        full = refs[6 + which]
        settle(meta, which == 0, full, own, 0, 0, 4)
        settle(meta, which == 0, full, after, 1, 0, 4)
        settle(meta, which == 0, full, before, 3, 0, 4)


def far_kernel(meta, *refs):
    for which in range(2):
        top, bottom = refs[2 * which : 2 * which + 2]
        full = refs[6 + which]
        settle(meta, which == 0, full, top, 2, 0, 2)
        settle(meta, which == 0, full, bottom, 2, 2, 4)


def assemble(meta, parts_in, parts_out):
    shapes = (vshape((D, RANK), BF16),) * 2
    near = parts_in[:3] + parts_out[:3]
    full = small_call(near_kernel, "assemble_near", shapes, *near, meta=meta)
    far = parts_in[3:] + parts_out[3:]
    return small_call(far_kernel, "assemble_far", shapes, *far, *full, meta=meta, aliases={5: 0, 6: 1})


def both_kernel(one, two, out, sems):
    copies = [
        pltpu.make_async_copy(ref, out.at[pl.ds(i * PIECE, PIECE)], sems.at[i]) for i, ref in enumerate((one, two))
    ]
    for copy in copies:
        copy.start()
    for copy in copies:
        copy.wait()


def stacked(one, two):
    return pl.pallas_call(
        both_kernel,
        out_shape=vshape((2 * PIECE, RANK), BF16),
        in_specs=[HB] * 2,
        out_specs=VM,
        scratch_shapes=[pltpu.SemaphoreType.DMA((2,))],
        compiler_params=params(),
        name="both",
    )(hbm(one), hbm(two))


def rows_kernel(plan, n_in, *refs):
    for source, at, rows, target, to in plan:
        refs[n_in + target][to : to + rows, :] = refs[source][at : at + rows, :]


def arranged(name, args, *outs):
    plan, sizes = [], []
    for target, pieces in enumerate(outs):
        to = 0
        for source, at, rows in pieces:
            plan.append((source, at, rows, target, to))
            to += rows
        sizes.append(to)
    shapes = tuple(vshape((size,) + args[0].shape[1:], args[0].dtype) for size in sizes)
    return small_call(functools.partial(rows_kernel, plan, len(args)), name, shapes, *args)


def forward_kernel(tick, n_codes, meta, *refs):
    codes, refs = refs[:n_codes], refs[n_codes:]
    (
        base_in, base_out, gain, w_in, w_out, heights_, pres_, rstds_, acts_, results_, fresh_,
        code_new, heights, pres, rstds, acts, results, fresh,
        sum_buf, square_buf,
    ) = refs
    section = meta[3]
    slot = tick - (section + (section >= SLOW[1]).astype(jnp.int32))

    @pl.when((slot >= 0) & (slot < MICRO))
    def _():
        sample = meta[4 + slot]
        rows = pl.ds(pl.multiple_of(slot * SEQ, SEQ), SEQ)

        def project(decode):
            if decode:
                scales = received(codes, section == SLOW[1], slice(D, WIDE)).astype(F32)
            pre = jnp.zeros((SEQ, RANK), F32)
            square = jnp.zeros((SEQ, BLOCK), F32)
            for i in range(D // PIECE):
                scaled = []
                for half in range(PIECE // BLOCK):
                    b = i * (PIECE // BLOCK) + half
                    lanes = slice(b * BLOCK, (b + 1) * BLOCK)
                    if decode:
                        value = received(codes, section == SLOW[1], lanes).astype(F32) * scales[:, b : b + 1]
                        height = (base_in[sample, :, lanes].astype(F32) + value).astype(BF16)
                        heights[rows, lanes] = height
                    else:
                        height = heights[rows, lanes]
                    h = height.astype(F32)
                    square += h * h
                    scaled.append((h * gain[:, lanes]).astype(BF16))
                pre += mm(jnp.concatenate(scaled, axis=1), w_in[i * PIECE : (i + 1) * PIECE, :], NN)
            sum_buf[...] = pre
            square_buf[...] = square

        if codes:

            @pl.when(section > 0)
            def _():
                project(True)

        @pl.when(section == 0)
        def _():
            project(False)

        rstd = lax.rsqrt(jnp.sum(square_buf[...], axis=1, keepdims=True) * (1.0 / D) + 1e-05)
        pre = sum_buf[...] * rstd
        act = (pre / (1.0 + jnp.exp(-pre))).astype(BF16)
        pres[rows, :] = pre
        rstds[rows, :] = jnp.broadcast_to(rstd, (SEQ, BLOCK))
        acts[rows, :] = act
        lane = lax.broadcasted_iota(jnp.int32, (SEQ, BLOCK), 1)
        scales_new = jnp.zeros((SEQ, BLOCK), F32)
        for i in range(D // PIECE):
            branch = mm(act, w_out[i * PIECE : (i + 1) * PIECE, :], NT)
            for half in range(PIECE // BLOCK):
                b = i * (PIECE // BLOCK) + half
                lanes = slice(b * BLOCK, (b + 1) * BLOCK)
                part = branch[:, half * BLOCK : (half + 1) * BLOCK]
                result = (heights[rows, lanes].astype(F32) + part).astype(BF16)
                results[rows, lanes] = result
                base = base_out[sample, :, lanes].astype(F32)
                new, scale = coded(result.astype(F32) - base)
                code_new[:, lanes] = new
                fresh[rows, lanes] = (base + new.astype(F32) * scale).astype(BF16)
                scales_new = jnp.where(lane == b, scale, scales_new)
        code_new[:, D:] = scales_new.astype(BF16)


def forward_tick(tick, meta, codes, base_in, base_out, gain, w_in, w_out, state):
    heights, pres, rstds, acts, results, fresh = state
    first = 1 + len(codes) + 5
    out = pl.pallas_call(
        functools.partial(forward_kernel, tick, len(codes)),
        out_shape=(
            vshape((SEQ, WIDE), BF16),
            vshape(heights.shape, BF16),
            vshape(pres.shape, F32),
            vshape(rstds.shape, F32),
            vshape(acts.shape, BF16),
            vshape(results.shape, BF16),
            vshape(fresh.shape, BF16),
        ),
        in_specs=[SM] + [VM] * (len(codes) + 5 + 6),
        out_specs=(VM,) * 7,
        scratch_shapes=[
            pltpu.VMEM((SEQ, RANK), F32),
            pltpu.VMEM((SEQ, BLOCK), F32),
        ],
        input_output_aliases={first + i: 1 + i for i in range(6)},
        compiler_params=params(),
        cost_estimate=pl.CostEstimate(flops=2 * 2 * SEQ * D * RANK, bytes_accessed=16 * 2**20, transcendentals=0),
        name="forward_tick",
    )(
        meta, *map(vmem, codes), vmem(base_in), vmem(base_out), vmem(gain), vmem(w_in), vmem(w_out),
        vmem(heights), vmem(pres), vmem(rstds), vmem(acts), vmem(results), vmem(fresh),
    )
    return out[0], out[1:]


def backward_kernel(tick, n_codes, meta, *refs):
    codes, refs = refs[:n_codes], refs[n_codes:]
    (
        heights, pres, rstds, gain, w_in, w_out, grads_, dpres_, ingrads_,
        code_new, grads, dpres, ingrads,
        sum_buf,
    ) = refs
    section = meta[3]
    slot = tick - (SECTIONS - 1 - section + (section <= SLOW[0]).astype(jnp.int32))

    @pl.when((slot >= 0) & (slot < MICRO))
    def _():
        rows = pl.ds(pl.multiple_of(slot * SEQ, SEQ), SEQ)

        def project(decode):
            if decode:
                scales = received(codes, section == SLOW[0], slice(D, WIDE)).astype(F32)
            down = jnp.zeros((SEQ, RANK), F32)
            for i in range(D // PIECE):
                if decode:
                    for half in range(PIECE // BLOCK):
                        b = i * (PIECE // BLOCK) + half
                        lanes = slice(b * BLOCK, (b + 1) * BLOCK)
                        value = received(codes, section == SLOW[0], lanes).astype(F32) * scales[:, b : b + 1]
                        grads[rows, lanes] = value.astype(BF16)
                piece = slice(i * PIECE, (i + 1) * PIECE)
                down += mm(grads[rows, piece], w_out[piece, :], NN)
            sum_buf[...] = down

        if codes:

            @pl.when(section < SECTIONS - 1)
            def _():
                project(True)

        @pl.when(section == SECTIONS - 1)
        def _():
            project(False)

        pre = pres[rows, :]
        rstd = rstds[rows, :]
        sig = 1.0 / (1.0 + jnp.exp(-pre))
        dpre = (sum_buf[...] * sig * (1.0 + pre * (1.0 - sig))).astype(BF16)
        dpres[rows, :] = dpre
        inner = jnp.sum(dpre.astype(F32) * pre, axis=1, keepdims=True) * (1.0 / D)
        pull = rstd * rstd * inner
        lane = lax.broadcasted_iota(jnp.int32, (SEQ, BLOCK), 1)
        scales_new = jnp.zeros((SEQ, BLOCK), F32)
        for i in range(D // PIECE):
            dnorm = mm(dpre, w_in[i * PIECE : (i + 1) * PIECE, :], NT)
            for half in range(PIECE // BLOCK):
                b = i * (PIECE // BLOCK) + half
                lanes = slice(b * BLOCK, (b + 1) * BLOCK)
                extra = dnorm[:, half * BLOCK : (half + 1) * BLOCK] * gain[:, lanes]
                dh = (
                    grads[rows, lanes].astype(F32)
                    + rstd * extra
                    - heights[rows, lanes].astype(F32) * pull
                )
                ingrads[rows, lanes] = dh.astype(BF16)
                new, scale = coded(dh)
                code_new[:, lanes] = new
                scales_new = jnp.where(lane == b, scale, scales_new)
        code_new[:, D:] = scales_new.astype(BF16)


def backward_tick(tick, meta, codes, heights, pres, rstds, gain, w_in, w_out, state):
    grads, dpres, ingrads = state
    first = 1 + len(codes) + 6
    out = pl.pallas_call(
        functools.partial(backward_kernel, tick, len(codes)),
        out_shape=(
            vshape((SEQ, WIDE), BF16),
            vshape(grads.shape, BF16),
            vshape(dpres.shape, BF16),
            vshape(ingrads.shape, BF16),
        ),
        in_specs=[SM] + [VM] * (len(codes) + 6 + 3),
        out_specs=(VM,) * 4,
        scratch_shapes=[pltpu.VMEM((SEQ, RANK), F32)],
        input_output_aliases={first + i: 1 + i for i in range(3)},
        compiler_params=params(),
        cost_estimate=pl.CostEstimate(flops=2 * 2 * SEQ * D * RANK, bytes_accessed=16 * 2**20, transcendentals=0),
        name="backward_tick",
    )(
        meta, *map(vmem, codes), vmem(heights), vmem(pres), vmem(rstds), vmem(gain), vmem(w_in), vmem(w_out),
        vmem(grads), vmem(dpres), vmem(ingrads),
    )
    return out[0], out[1:]


def flush_kernel(
    meta, heights, results, fresh, ingrads, base_in, base_out, after, results_out, ingrads_out, new_in, new_out, sems
):
    section = meta[3]
    unused = 10 - (meta[4] + meta[5] + meta[6] + meta[7])
    always = [(results, results_out), (ingrads, ingrads_out), (base_in.at[unused], new_in.at[unused])]
    always.append((base_out.at[unused], new_out.at[unused]))
    copies = [pltpu.make_async_copy(source, target, sems.at[i]) for i, (source, target) in enumerate(always)]

    def table(rows_of, base, new, first):
        fresh_ones, old_ones = [], []
        for j in range(MICRO):
            target, sem = new.at[meta[4 + j]], sems.at[first + j]
            fresh_ones.append(pltpu.make_async_copy(rows_of.at[pl.ds(j * SEQ, SEQ)], target, sem))
            old_ones.append(pltpu.make_async_copy(base.at[meta[4 + j]], target, sem))
        return fresh_ones, old_ones

    received, kept_in = table(heights, base_in, new_in, 4)
    sent, kept_out = table(fresh, base_out, new_out, 4 + MICRO)
    groups = [
        (section > 0, received),
        (section == 0, kept_in),
        (section < SECTIONS - 1, sent),
        (section == SECTIONS - 1, kept_out),
    ]

    def run(act):
        for copy in copies:
            act(copy)
        for condition, group in groups:

            @pl.when(condition)
            def _(group=group):
                for copy in group:
                    act(copy)

    run(lambda copy: copy.start())
    run(lambda copy: copy.wait())


def flush(meta, heights, results, fresh, ingrads, base_in, base_out, after):
    return pl.pallas_call(
        flush_kernel,
        out_shape=(
            hshape(results.shape, BF16),
            hshape(ingrads.shape, BF16),
            hshape(base_in.shape, BF16),
            hshape(base_out.shape, BF16),
        ),
        in_specs=[SM] + [VM] * 6 + [ANY],
        out_specs=(HB,) * 4,
        scratch_shapes=[pltpu.SemaphoreType.DMA((4 + 2 * MICRO,))],
        compiler_params=params(),
        cost_estimate=pl.CostEstimate(flops=0, bytes_accessed=16 * 2**20, transcendentals=0),
        name="flush",
    )(meta, *map(vmem, (heights, results, fresh, ingrads, base_in, base_out)), after)


def grad_lanes(meta, which, r, i):
    if which == 0:
        z = lax.rem(meta[0] + r, NZ)
        return pl.ds(pl.multiple_of((z * NY * NX + i) * PIECE, PIECE), PIECE)
    x = lax.rem(meta[2] + r, NX)
    return pl.ds(pl.multiple_of((i * NX + x) * PIECE, PIECE), PIECE)


def left_sides(rstds, dpres, acts):
    return (dpres[...].astype(F32) * rstds[:, :1]).T.astype(BF16), acts[...].astype(F32).T.astype(BF16)


def right_side(which, lanes, heights, grads, gain):
    if which == 0:
        return (heights[:, lanes].astype(F32) * gain[:, lanes]).astype(BF16)
    return grads[:, lanes]


def far_grad_kernel(meta, heights, grads, rstds, dpres, acts, gain, *outs):
    left = left_sides(rstds, dpres, acts)
    for which in range(2):
        for i in range(NY * 4):
            product = mm(left[which], right_side(which, grad_lanes(meta, which, 2, i), heights, grads, gain), NN)
            product = product.astype(BF16)
            for half in range(2):
                outs[2 * which + half][:, i * PIECE : (i + 1) * PIECE] = product[half * 128 : (half + 1) * 128]


def near_grad_kernel(meta, heights, grads, rstds, dpres, acts, gain, *outs):
    left = left_sides(rstds, dpres, acts)
    for which in range(2):
        for k, r in enumerate((1, 3, 0)):
            for i in range(NY * 4):
                product = mm(left[which], right_side(which, grad_lanes(meta, which, r, i), heights, grads, gain), NN)
                outs[3 * which + k][:, i * PIECE : (i + 1) * PIECE] = product.astype(BF16)


def add_kernel(*refs):
    for which in range(2):
        ahead, behind, top, bottom = refs[4 * which : 4 * which + 4]
        ahead_new, behind_new = refs[8 + 2 * which : 10 + 2 * which]
        for i in range(4):
            lanes = slice(i * 512, (i + 1) * 512)
            ahead_new[:128, lanes] = (ahead[:128, lanes].astype(F32) + top[:, lanes].astype(F32)).astype(BF16)
            ahead_new[128:, lanes] = ahead[128:, lanes]
            behind_new[:128, lanes] = behind[:128, lanes]
            behind_new[128:, lanes] = (behind[128:, lanes].astype(F32) + bottom[:, lanes].astype(F32)).astype(BF16)


def sum_one_kernel(meta, *refs):
    gin, gout, outs = refs[:3], refs[3:6], refs[6:]
    for r in range(NX):
        for y in range(NY):
            x = lax.rem(meta[2] + r, NX)
            lanes = pl.ds(pl.multiple_of((y * NX + x) * PIECE, PIECE), PIECE)
            total = sum(ref[:, lanes].astype(F32) for ref in gin)
            outs[r][:, y * PIECE : (y + 1) * PIECE] = total.astype(BF16)
    for r in range(NZ):
        for y in range(NY):
            z = lax.rem(meta[0] + r, NZ)
            lanes = pl.ds(pl.multiple_of((z * NY + y) * PIECE, PIECE), PIECE)
            total = sum(ref[:, lanes].astype(F32) for ref in gout)
            outs[NX + r][:, y * PIECE : (y + 1) * PIECE] = total.astype(BF16)


def sum_two_kernel(meta, *refs):
    gin, gout, (keep, send) = refs[:NX], refs[NX : NX + NZ], refs[NX + NZ :]
    for which, group in enumerate((gin, gout)):
        for p, out in enumerate((keep, send)):
            y = lax.rem(meta[1] + p, NY)
            lanes = pl.ds(pl.multiple_of(y * PIECE, PIECE), PIECE)
            out[which] = sum(ref[:, lanes].astype(F32) for ref in group).astype(BF16)


def sum_three_kernel(keep, got, gin, gout):
    gin[...] = (keep[0].astype(F32) + got[0].astype(F32)).T
    gout[...] = (keep[1].astype(F32) + got[1].astype(F32)).T


def small_call(kernel, name, shapes, *args, meta=None, aliases={}):
    scalars = [] if meta is None else [meta]
    return pl.pallas_call(
        kernel,
        out_shape=shapes,
        in_specs=[SM] * len(scalars) + [VM] * len(args),
        out_specs=(VM,) * len(shapes),
        input_output_aliases=aliases,
        compiler_params=params(),
        cost_estimate=pl.CostEstimate(flops=0, bytes_accessed=8 * 2**20, transcendentals=0),
        name=name,
    )(*scalars, *map(vmem, args))


def place(z, y, x):
    return (z * NY + y) * NX + x


def moved(value, shift):
    dz, dy, dx = shift
    pairs = []
    for z in range(NZ):
        for y in range(NY):
            for x in range(NX):
                source = place((z + dz) % NZ, (y + dy) % NY, (x + dx) % NX)
                pairs.append((source, place(z, y, x)))
    return lax.ppermute(value, "dp", pairs)


def along(axis, steps):
    return (steps, 0, 0) if axis == 0 else (0, 0, steps)


def gathered(meta, shard_in, shard_out):
    both = stacked(shard_in, shard_out)
    other = moved(both, (0, 1, 0))
    rows, half = 2 * PIECE, 4 * PIECE
    pair_in, pair_out = arranged(
        "pairs", (both, other), [(0, 0, PIECE), (1, 0, PIECE)], [(0, PIECE, PIECE), (1, PIECE, PIECE)]
    )
    parts = [pair_in, pair_out]
    for r in (1, 3, 2):
        parts += [moved(pair_in, along(2, r)), moved(pair_out, along(0, r))]
    four_in, four_out = arranged(
        "fours", parts, [(i, 0, rows) for i in (0, 2, 6, 4)], [(i, 0, rows) for i in (1, 3, 7, 5)]
    )
    near_in = [four_in, moved(four_in, along(0, 1)), moved(four_in, along(0, -1))]
    near_out = [four_out, moved(four_out, along(2, 1)), moved(four_out, along(2, -1))]
    came = (near_in[2], near_in[1], near_out[2], near_out[1])
    cuts = arranged("cuts", came, *[[(i, half * (i % 2), half)] for i in range(4)])
    far_in = [moved(cuts[0], along(0, -1)), moved(cuts[1], along(0, 1))]
    far_out = [moved(cuts[2], along(2, -1)), moved(cuts[3], along(2, 1))]
    return assemble(meta, near_in + far_in, near_out + far_out), pair_in


def reduced(meta, operands):
    rows = RANK // 2
    far = small_call(far_grad_kernel, "far_grads", (vshape((rows, 2048), BF16),) * 4, *operands, meta=meta)
    near = small_call(near_grad_kernel, "near_grads", (vshape((RANK, 2048), BF16),) * 6, *operands, meta=meta)
    args, own = [], []
    for which, axis in ((0, 0), (1, 2)):
        top, bottom = far[2 * which : 2 * which + 2]
        ahead, behind, here = near[3 * which : 3 * which + 3]
        args += [ahead, behind, moved(top, along(axis, -1)), moved(bottom, along(axis, 1))]
        own.append(here)
    added = small_call(add_kernel, "add_far", (vshape((RANK, 2048), BF16),) * 4, *args)
    args = []
    for which, axis in ((0, 0), (1, 2)):
        ahead, behind = added[2 * which : 2 * which + 2]
        args += [own[which], moved(ahead, along(axis, -1)), moved(behind, along(axis, 1))]
    shapes = tuple(vshape((RANK, NY * PIECE), BF16) for _ in range(NX + NZ))
    two = small_call(sum_one_kernel, "sum_one", shapes, *args, meta=meta)
    gin, gout = two[:NX], two[NX:]
    gin = [gin[0]] + [moved(gin[r], along(2, -r)) for r in (1, 2, 3)]
    gout = [gout[0]] + [moved(gout[r], along(0, -r)) for r in (1, 2, 3)]
    shapes = (vshape((2, RANK, PIECE), BF16),) * 2
    keep, send = small_call(sum_two_kernel, "sum_two", shapes, *gin, *gout, meta=meta)
    got = moved(send, (0, 1, 0))
    return (*small_call(sum_three_kernel, "sum_three", (hshape((PIECE, RANK), F32),) * 2, keep, got), far[0])


def handed_on(tick, code, sent, at, pairs):
    live = [pair for pair in pairs if 0 <= tick - at[pair[0]] < MICRO]
    quick = [pair for pair in live if set(pair) != set(SLOW)]
    slow = [pair for pair in live if set(pair) == set(SLOW)]
    sending = lax.ppermute(code, "section", slow) if slow else None
    codes = [lax.ppermute(code, "section", quick)] if quick else []
    if sent is not None:
        codes.append(sent)
    return codes, sending


def body(inputs, cotangent, sample_ids, out_bases, in_bases, proj_in, proj_out, gains):
    section = lax.axis_index("section")
    dp = lax.axis_index("dp")
    place_ids = jnp.stack([dp // (NY * NX), (dp // NX) % NY, dp % NX, section])
    meta = jnp.concatenate([place_ids.astype(jnp.int32), sample_ids[0]])
    (w_in, w_out), after = gathered(meta, proj_in[0], proj_out[0])
    heights, grads, base_in, base_out, pres, rstds, acts, dpres, results, fresh, ingrads = fetch(
        inputs, cotangent, in_bases[0], out_bases[0], after
    )
    state = (heights, pres, rstds, acts, results, fresh)
    codes, sent = [], None
    for tick in range(TICKS):
        code, state = forward_tick(tick, meta, codes, base_in, base_out, gains, w_in, w_out, state)
        codes, sent = handed_on(tick, code, sent, FORWARD_AT, [(s, s + 1) for s in range(SECTIONS - 1)])
    heights, pres, rstds, acts, results, fresh = state
    state = (grads, dpres, ingrads)
    codes, sent = [], None
    for tick in range(TICKS):
        code, state = backward_tick(tick, meta, codes, heights, pres, rstds, gains, w_in, w_out, state)
        codes, sent = handed_on(tick, code, sent, BACKWARD_AT, [(s, s - 1) for s in range(1, SECTIONS)])
    grads, dpres, ingrads = state
    grad_in, grad_out, after = reduced(meta, (heights, grads, rstds, dpres, acts, gains))
    results, ingrads, new_in, new_out = flush(meta, heights, results, fresh, ingrads, base_in, base_out, after)
    return results[None], ingrads[None], new_out[None], new_in[None], grad_in[None], grad_out[None]


def solution(mesh):
    in_specs = (
        P("dp", None),
        P("dp", None),
        P("dp", None),
        P("section", "dp", None, None),
        P("section", "dp", None, None),
        P("section", "dp", None),
        P("section", "dp", None),
        P("section", None),
    )
    out_specs = (
        P("section", "dp", None),
        P("section", "dp", None),
        P("section", "dp", None, None),
        P("section", "dp", None, None),
        P("section", "dp", None),
        P("section", "dp", None),
    )
    return jax.shard_map(body, mesh=mesh, in_specs=in_specs, out_specs=out_specs, check_vma=False)
```

```python
import functools

import jax
import jax.numpy as jnp
from jax import lax
from jax.experimental import pallas as pl
from jax.experimental.pallas import tpu as pltpu
from jax.sharding import PartitionSpec as P

D = 8192
RANK = 256
BLOCK = 128
SEQ = 32
MICRO = 4
SECTIONS = 4
TOKENS = MICRO * SEQ
NZ, NY, NX = 4, 2, 4
PIECE = 256
WIDE = D + BLOCK
F32 = jnp.float32
BF16 = jnp.bfloat16
VM = pl.BlockSpec(memory_space=pltpu.VMEM)
SM = pl.BlockSpec(memory_space=pltpu.SMEM)
HB = pl.BlockSpec(memory_space=pltpu.HBM)
ANY = pl.BlockSpec(memory_space=pl.ANY)
NN = (((1,), (0,)), ((), ()))
NT = (((1,), (1,)), ((), ()))
FORWARD_AT = (0, 1, 3, 4)
BACKWARD_AT = (8, 7, 5, 4)
TICKS = MICRO + 8
SLOW = (1, 2)


def vmem(value):
    return pltpu.with_memory_space_constraint(value, pltpu.VMEM)


def hbm(value):
    return pltpu.with_memory_space_constraint(value, pltpu.HBM)


def vshape(shape, dtype):
    return pltpu.VMEM(shape, dtype)


def hshape(shape, dtype):
    return jax.ShapeDtypeStruct(shape, dtype)


def params():
    return pltpu.CompilerParams(vmem_limit_bytes=12 * 2**20)


def mm(a, b, dims):
    return lax.dot_general(a, b, dims, preferred_element_type=F32)


def coded(values):
    top = jnp.max(jnp.abs(values), axis=1, keepdims=True) + 1e-06
    scale = top.astype(BF16).astype(F32)
    code = (values * (1.0 / scale)).astype(BF16)
    return code, scale


def received(codes, slow_here, lanes):
    if len(codes) == 1:
        return codes[0][:, lanes]
    return jnp.where(slow_here, codes[1][:, lanes], codes[0][:, lanes])


def hand_out(wires, outs, code, slow_here):
    for wire, out in zip(wires, outs):

        @pl.when(slow_here if wire == "slow" else jnp.logical_not(slow_here))
        def _(out=out):
            out[...] = code[...]


FORWARD_PAIRS = [(s, s + 1) for s in range(SECTIONS - 1)]
BACKWARD_PAIRS = [(s, s - 1) for s in range(1, SECTIONS)]


def live(tick, pairs, at, wire):
    return [
        pair for pair in pairs if 0 <= tick - at[pair[0]] < MICRO and (set(pair) == set(SLOW)) == (wire == "slow")
    ]


def fetch_kernel(inputs, cotangent, table_in, table_out, after, heights, grads, base_in, base_out, *rest):
    sems = rest[-1]
    moves = [(inputs, heights), (cotangent, grads), (table_in, base_in), (table_out, base_out)]
    copies = [pltpu.make_async_copy(source, target, sems.at[i]) for i, (source, target) in enumerate(moves)]
    for copy in copies:
        copy.start()
    for copy in copies:
        copy.wait()


def fetch(inputs, cotangent, table_in, table_out, after):
    return pl.pallas_call(
        fetch_kernel,
        out_shape=(
            vshape(inputs.shape, BF16),
            vshape(cotangent.shape, BF16),
            vshape(table_in.shape, BF16),
            vshape(table_out.shape, BF16),
            vshape((TOKENS, RANK), F32),
            vshape((TOKENS, BLOCK), F32),
            vshape((TOKENS, RANK), BF16),
            vshape((TOKENS, RANK), BF16),
            vshape((TOKENS, D), BF16),
            vshape((TOKENS, D), BF16),
            vshape((TOKENS, D), BF16),
        ),
        in_specs=[HB] * 4 + [ANY],
        out_specs=(VM,) * 11,
        scratch_shapes=[pltpu.SemaphoreType.DMA((4,))],
        compiler_params=params(),
        cost_estimate=pl.CostEstimate(flops=0, bytes_accessed=20 * 2**20, transcendentals=0),
        name="fetch",
    )(hbm(inputs), hbm(cotangent), hbm(table_in), hbm(table_out), after)


def settle(meta, first, full, ref, r, start, stop):
    for q in range(start, stop):
        for p in range(NY):
            z = lax.rem(meta[0] + (r if first else q), NZ)
            x = lax.rem(meta[2] + (q if first else r), NX)
            y = lax.rem(meta[1] + p, NY)
            at = pl.multiple_of((z * NY * NX + y * NX + x) * PIECE, PIECE)
            k = ((q - start) * NY + p) * PIECE
            full[pl.ds(at, PIECE), :] = ref[k : k + PIECE, :]


def near_kernel(meta, *refs):
    for which in range(2):
        own, after, before = refs[3 * which : 3 * which + 3]
        full = refs[6 + which]
        settle(meta, which == 0, full, own, 0, 0, 4)
        settle(meta, which == 0, full, after, 1, 0, 4)
        settle(meta, which == 0, full, before, 3, 0, 4)


def far_kernel(meta, *refs):
    for which in range(2):
        top, bottom = refs[2 * which : 2 * which + 2]
        full = refs[6 + which]
        settle(meta, which == 0, full, top, 2, 0, 2)
        settle(meta, which == 0, full, bottom, 2, 2, 4)


def assemble(meta, parts_in, parts_out):
    shapes = (vshape((D, RANK), BF16),) * 2
    near = parts_in[:3] + parts_out[:3]
    full = small_call(near_kernel, "assemble_near", shapes, *near, meta=meta)
    far = parts_in[3:] + parts_out[3:]
    return small_call(far_kernel, "assemble_far", shapes, *far, *full, meta=meta, aliases={5: 0, 6: 1})


def both_kernel(one, two, out, sems):
    copies = [
        pltpu.make_async_copy(ref, out.at[pl.ds(i * PIECE, PIECE)], sems.at[i]) for i, ref in enumerate((one, two))
    ]
    for copy in copies:
        copy.start()
    for copy in copies:
        copy.wait()


def stacked(one, two):
    return pl.pallas_call(
        both_kernel,
        out_shape=vshape((2 * PIECE, RANK), BF16),
        in_specs=[HB] * 2,
        out_specs=VM,
        scratch_shapes=[pltpu.SemaphoreType.DMA((2,))],
        compiler_params=params(),
        name="both",
    )(hbm(one), hbm(two))


def rows_kernel(plan, n_in, *refs):
    for source, at, rows, target, to in plan:
        refs[n_in + target][to : to + rows, :] = refs[source][at : at + rows, :]


def arranged(name, args, *outs):
    plan, sizes = [], []
    for target, pieces in enumerate(outs):
        to = 0
        for source, at, rows in pieces:
            plan.append((source, at, rows, target, to))
            to += rows
        sizes.append(to)
    shapes = tuple(vshape((size,) + args[0].shape[1:], args[0].dtype) for size in sizes)
    return small_call(functools.partial(rows_kernel, plan, len(args)), name, shapes, *args)


def forward_kernel(tick, n_codes, wires, meta, *refs):
    codes, refs = refs[:n_codes], refs[n_codes:]
    (
        base_in, base_out, gain, w_in, w_out, heights_, pres_, rstds_, acts_, results_, fresh_,
        *code_out, heights, pres, rstds, acts, results, fresh,
        sum_buf, square_buf, code_new,
    ) = refs
    section = meta[3]
    slot = tick - (section + (section >= SLOW[1]).astype(jnp.int32))

    @pl.when((slot >= 0) & (slot < MICRO))
    def _():
        sample = meta[4 + slot]
        rows = pl.ds(pl.multiple_of(slot * SEQ, SEQ), SEQ)

        def project(decode):
            if decode:
                scales = received(codes, section == SLOW[1], slice(D, WIDE)).astype(F32)
            pre = jnp.zeros((SEQ, RANK), F32)
            square = jnp.zeros((SEQ, BLOCK), F32)
            for i in range(D // PIECE):
                scaled = []
                for half in range(PIECE // BLOCK):
                    b = i * (PIECE // BLOCK) + half
                    lanes = slice(b * BLOCK, (b + 1) * BLOCK)
                    if decode:
                        value = received(codes, section == SLOW[1], lanes).astype(F32) * scales[:, b : b + 1]
                        height = (base_in[sample, :, lanes].astype(F32) + value).astype(BF16)
                        heights[rows, lanes] = height
                    else:
                        height = heights[rows, lanes]
                    h = height.astype(F32)
                    square += h * h
                    scaled.append((h * gain[:, lanes]).astype(BF16))
                pre += mm(jnp.concatenate(scaled, axis=1), w_in[i * PIECE : (i + 1) * PIECE, :], NN)
            sum_buf[...] = pre
            square_buf[...] = square

        if codes:

            @pl.when(section > 0)
            def _():
                project(True)

        @pl.when(section == 0)
        def _():
            project(False)

        rstd = lax.rsqrt(jnp.sum(square_buf[...], axis=1, keepdims=True) * (1.0 / D) + 1e-05)
        pre = sum_buf[...] * rstd
        act = (pre / (1.0 + jnp.exp(-pre))).astype(BF16)
        pres[rows, :] = pre
        rstds[rows, :] = jnp.broadcast_to(rstd, (SEQ, BLOCK))
        acts[rows, :] = act
        lane = lax.broadcasted_iota(jnp.int32, (SEQ, BLOCK), 1)
        scales_new = jnp.zeros((SEQ, BLOCK), F32)
        for i in range(D // PIECE):
            branch = mm(act, w_out[i * PIECE : (i + 1) * PIECE, :], NT)
            for half in range(PIECE // BLOCK):
                b = i * (PIECE // BLOCK) + half
                lanes = slice(b * BLOCK, (b + 1) * BLOCK)
                part = branch[:, half * BLOCK : (half + 1) * BLOCK]
                result = (heights[rows, lanes].astype(F32) + part).astype(BF16)
                results[rows, lanes] = result
                if not code_out:
                    continue
                base = base_out[sample, :, lanes].astype(F32)
                new, scale = coded(result.astype(F32) - base)
                code_new[:, lanes] = new
                fresh[rows, lanes] = (base + new.astype(F32) * scale).astype(BF16)
                scales_new = jnp.where(lane == b, scale, scales_new)
        if code_out:
            code_new[:, D:] = scales_new.astype(BF16)
            hand_out(wires, code_out, code_new, section == SLOW[0])


def forward_tick(tick, meta, codes, base_in, base_out, gain, w_in, w_out, state):
    heights, pres, rstds, acts, results, fresh = state
    first = 1 + len(codes) + 5
    wires = [wire for wire in ("fast", "slow") if live(tick, FORWARD_PAIRS, FORWARD_AT, wire)]
    made = [vshape((SEQ, WIDE), BF16)] * len(wires)
    out = pl.pallas_call(
        functools.partial(forward_kernel, tick, len(codes), wires),
        out_shape=(
            *made,
            vshape(heights.shape, BF16),
            vshape(pres.shape, F32),
            vshape(rstds.shape, F32),
            vshape(acts.shape, BF16),
            vshape(results.shape, BF16),
            vshape(fresh.shape, BF16),
        ),
        in_specs=[SM] + [VM] * (len(codes) + 5 + 6),
        out_specs=(VM,) * (6 + len(made)),
        scratch_shapes=[
            pltpu.VMEM((SEQ, RANK), F32),
            pltpu.VMEM((SEQ, BLOCK), F32),
            pltpu.VMEM((SEQ, WIDE), BF16),
        ],
        input_output_aliases={first + i: len(made) + i for i in range(6)},
        compiler_params=params(),
        cost_estimate=pl.CostEstimate(flops=2 * 2 * SEQ * D * RANK, bytes_accessed=16 * 2**20, transcendentals=0),
        name="forward_tick",
    )(
        meta, *map(vmem, codes), vmem(base_in), vmem(base_out), vmem(gain), vmem(w_in), vmem(w_out),
        vmem(heights), vmem(pres), vmem(rstds), vmem(acts), vmem(results), vmem(fresh),
    )
    return dict(zip(wires, out)), out[len(made) :]


def backward_kernel(tick, n_codes, n_started, wires, meta, *refs):
    codes, refs = refs[:n_codes], refs[n_codes + n_started :]
    (
        heights, pres, rstds, gain, w_in, w_out, grads_, dpres_, ingrads_,
        *code_out, grads, dpres, ingrads,
        sum_buf, code_new,
    ) = refs
    section = meta[3]
    slot = tick - BACKWARD_AT[-1] - (SECTIONS - 1 - section + (section <= SLOW[0]).astype(jnp.int32))

    @pl.when((slot >= 0) & (slot < MICRO))
    def _():
        rows = pl.ds(pl.multiple_of(slot * SEQ, SEQ), SEQ)

        def project(decode):
            if decode:
                scales = received(codes, section == SLOW[0], slice(D, WIDE)).astype(F32)
            down = jnp.zeros((SEQ, RANK), F32)
            for i in range(D // PIECE):
                if decode:
                    for half in range(PIECE // BLOCK):
                        b = i * (PIECE // BLOCK) + half
                        lanes = slice(b * BLOCK, (b + 1) * BLOCK)
                        value = received(codes, section == SLOW[0], lanes).astype(F32) * scales[:, b : b + 1]
                        grads[rows, lanes] = value.astype(BF16)
                piece = slice(i * PIECE, (i + 1) * PIECE)
                down += mm(grads[rows, piece], w_out[piece, :], NN)
            sum_buf[...] = down

        if codes:

            @pl.when(section < SECTIONS - 1)
            def _():
                project(True)

        @pl.when(section == SECTIONS - 1)
        def _():
            project(False)

        pre = pres[rows, :]
        rstd = rstds[rows, :]
        sig = 1.0 / (1.0 + jnp.exp(-pre))
        dpre = (sum_buf[...] * sig * (1.0 + pre * (1.0 - sig))).astype(BF16)
        dpres[rows, :] = dpre
        inner = jnp.sum(dpre.astype(F32) * pre, axis=1, keepdims=True) * (1.0 / D)
        pull = rstd * rstd * inner
        lane = lax.broadcasted_iota(jnp.int32, (SEQ, BLOCK), 1)
        scales_new = jnp.zeros((SEQ, BLOCK), F32)
        for i in range(D // PIECE):
            dnorm = mm(dpre, w_in[i * PIECE : (i + 1) * PIECE, :], NT)
            for half in range(PIECE // BLOCK):
                b = i * (PIECE // BLOCK) + half
                lanes = slice(b * BLOCK, (b + 1) * BLOCK)
                extra = dnorm[:, half * BLOCK : (half + 1) * BLOCK] * gain[:, lanes]
                dh = (
                    grads[rows, lanes].astype(F32)
                    + rstd * extra
                    - heights[rows, lanes].astype(F32) * pull
                )
                ingrads[rows, lanes] = dh.astype(BF16)
                if code_out:
                    new, scale = coded(dh)
                    code_new[:, lanes] = new
                    scales_new = jnp.where(lane == b, scale, scales_new)
        if code_out:
            code_new[:, D:] = scales_new.astype(BF16)
            hand_out(wires, code_out, code_new, section == SLOW[1])


def backward_tick(tick, meta, codes, begun, heights, pres, rstds, gain, w_in, w_out, state):
    grads, dpres, ingrads = state
    wires = [wire for wire in ("fast", "slow") if live(tick, BACKWARD_PAIRS, BACKWARD_AT, wire)]
    made = [vshape((SEQ, WIDE), BF16)] * len(wires)
    shared = [wire for wire in wires if wire in begun]
    first = 1 + len(codes) + len(shared) + 6
    aliases = {1 + len(codes) + i: wires.index(wire) for i, wire in enumerate(shared)}
    out = pl.pallas_call(
        functools.partial(backward_kernel, tick, len(codes), len(shared), wires),
        out_shape=(
            *made,
            vshape(grads.shape, BF16),
            vshape(dpres.shape, BF16),
            vshape(ingrads.shape, BF16),
        ),
        in_specs=[SM] + [VM] * (len(codes) + len(shared) + 6 + 3),
        out_specs=(VM,) * (3 + len(made)),
        scratch_shapes=[pltpu.VMEM((SEQ, RANK), F32), pltpu.VMEM((SEQ, WIDE), BF16)],
        input_output_aliases=aliases | {first + i: len(made) + i for i in range(3)},
        compiler_params=params(),
        cost_estimate=pl.CostEstimate(flops=2 * 2 * SEQ * D * RANK, bytes_accessed=16 * 2**20, transcendentals=0),
        name="backward_tick",
    )(
        meta, *map(vmem, codes), *[vmem(begun[wire]) for wire in shared],
        vmem(heights), vmem(pres), vmem(rstds), vmem(gain), vmem(w_in), vmem(w_out),
        vmem(grads), vmem(dpres), vmem(ingrads),
    )
    return begun | dict(zip(wires, out)), out[len(made) :]


def flush_kernel(
    meta, heights, results, fresh, ingrads, base_in, base_out, after, results_out, ingrads_out, new_in, new_out, sems
):
    section = meta[3]
    unused = 10 - (meta[4] + meta[5] + meta[6] + meta[7])
    always = [(results, results_out), (ingrads, ingrads_out), (base_in.at[unused], new_in.at[unused])]
    always.append((base_out.at[unused], new_out.at[unused]))
    copies = [pltpu.make_async_copy(source, target, sems.at[i]) for i, (source, target) in enumerate(always)]

    def table(rows_of, base, new, first):
        fresh_ones, old_ones = [], []
        for j in range(MICRO):
            target, sem = new.at[meta[4 + j]], sems.at[first + j]
            fresh_ones.append(pltpu.make_async_copy(rows_of.at[pl.ds(j * SEQ, SEQ)], target, sem))
            old_ones.append(pltpu.make_async_copy(base.at[meta[4 + j]], target, sem))
        return fresh_ones, old_ones

    received, kept_in = table(heights, base_in, new_in, 4)
    sent, kept_out = table(fresh, base_out, new_out, 4 + MICRO)
    groups = [
        (section > 0, received),
        (section == 0, kept_in),
        (section < SECTIONS - 1, sent),
        (section == SECTIONS - 1, kept_out),
    ]

    def run(act):
        for copy in copies:
            act(copy)
        for condition, group in groups:

            @pl.when(condition)
            def _(group=group):
                for copy in group:
                    act(copy)

    run(lambda copy: copy.start())
    run(lambda copy: copy.wait())


def flush(meta, heights, results, fresh, ingrads, base_in, base_out, after):
    return pl.pallas_call(
        flush_kernel,
        out_shape=(
            hshape(results.shape, BF16),
            hshape(ingrads.shape, BF16),
            hshape(base_in.shape, BF16),
            hshape(base_out.shape, BF16),
        ),
        in_specs=[SM] + [VM] * 6 + [ANY],
        out_specs=(HB,) * 4,
        scratch_shapes=[pltpu.SemaphoreType.DMA((4 + 2 * MICRO,))],
        compiler_params=params(),
        cost_estimate=pl.CostEstimate(flops=0, bytes_accessed=16 * 2**20, transcendentals=0),
        name="flush",
    )(meta, *map(vmem, (heights, results, fresh, ingrads, base_in, base_out)), after)


def grad_lanes(meta, which, r, i):
    if which == 0:
        z = lax.rem(meta[0] + r, NZ)
        return pl.ds(pl.multiple_of((z * NY * NX + i) * PIECE, PIECE), PIECE)
    x = lax.rem(meta[2] + r, NX)
    return pl.ds(pl.multiple_of((i * NX + x) * PIECE, PIECE), PIECE)


def left_sides(rstds, dpres, acts):
    return (dpres[...].astype(F32) * rstds[:, :1]).T.astype(BF16), acts[...].astype(F32).T.astype(BF16)


def right_side(which, lanes, heights, grads, gain):
    if which == 0:
        return (heights[:, lanes].astype(F32) * gain[:, lanes]).astype(BF16)
    return grads[:, lanes]


def far_grad_kernel(meta, heights, grads, rstds, dpres, acts, gain, *outs):
    left = left_sides(rstds, dpres, acts)
    for which in range(2):
        for i in range(NY * 4):
            product = mm(left[which], right_side(which, grad_lanes(meta, which, 2, i), heights, grads, gain), NN)
            product = product.astype(BF16)
            for half in range(2):
                outs[2 * which + half][:, i * PIECE : (i + 1) * PIECE] = product[half * 128 : (half + 1) * 128]


def near_grad_kernel(meta, heights, grads, rstds, dpres, acts, gain, *outs):
    left = left_sides(rstds, dpres, acts)
    for which in range(2):
        for k, r in enumerate((1, 3, 0)):
            for i in range(NY * 4):
                product = mm(left[which], right_side(which, grad_lanes(meta, which, r, i), heights, grads, gain), NN)
                outs[3 * which + k][:, i * PIECE : (i + 1) * PIECE] = product.astype(BF16)


def add_kernel(*refs):
    for which in range(2):
        ahead, behind, top, bottom = refs[4 * which : 4 * which + 4]
        ahead_new, behind_new = refs[8 + 2 * which : 10 + 2 * which]
        for i in range(4):
            lanes = slice(i * 512, (i + 1) * 512)
            ahead_new[:128, lanes] = (ahead[:128, lanes].astype(F32) + top[:, lanes].astype(F32)).astype(BF16)
            ahead_new[128:, lanes] = ahead[128:, lanes]
            behind_new[:128, lanes] = behind[:128, lanes]
            behind_new[128:, lanes] = (behind[128:, lanes].astype(F32) + bottom[:, lanes].astype(F32)).astype(BF16)


def sum_one_kernel(meta, *refs):
    gin, gout, outs = refs[:3], refs[3:6], refs[6:]
    for r in range(NX):
        for y in range(NY):
            x = lax.rem(meta[2] + r, NX)
            lanes = pl.ds(pl.multiple_of((y * NX + x) * PIECE, PIECE), PIECE)
            total = sum(ref[:, lanes].astype(F32) for ref in gin)
            outs[r][:, y * PIECE : (y + 1) * PIECE] = total.astype(BF16)
    for r in range(NZ):
        for y in range(NY):
            z = lax.rem(meta[0] + r, NZ)
            lanes = pl.ds(pl.multiple_of((z * NY + y) * PIECE, PIECE), PIECE)
            total = sum(ref[:, lanes].astype(F32) for ref in gout)
            outs[NX + r][:, y * PIECE : (y + 1) * PIECE] = total.astype(BF16)


def sum_two_kernel(meta, *refs):
    gin, gout, (keep, send) = refs[:NX], refs[NX : NX + NZ], refs[NX + NZ :]
    for which, group in enumerate((gin, gout)):
        for p, out in enumerate((keep, send)):
            y = lax.rem(meta[1] + p, NY)
            lanes = pl.ds(pl.multiple_of(y * PIECE, PIECE), PIECE)
            out[which] = sum(ref[:, lanes].astype(F32) for ref in group).astype(BF16)


def sum_three_kernel(keep, got, gin, gout):
    gin[...] = (keep[0].astype(F32) + got[0].astype(F32)).T
    gout[...] = (keep[1].astype(F32) + got[1].astype(F32)).T


def small_call(kernel, name, shapes, *args, meta=None, aliases={}):
    scalars = [] if meta is None else [meta]
    return pl.pallas_call(
        kernel,
        out_shape=shapes,
        in_specs=[SM] * len(scalars) + [VM] * len(args),
        out_specs=(VM,) * len(shapes),
        input_output_aliases=aliases,
        compiler_params=params(),
        cost_estimate=pl.CostEstimate(flops=0, bytes_accessed=8 * 2**20, transcendentals=0),
        name=name,
    )(*scalars, *map(vmem, args))


def place(z, y, x):
    return (z * NY + y) * NX + x


def moved(value, shift):
    dz, dy, dx = shift
    pairs = []
    for z in range(NZ):
        for y in range(NY):
            for x in range(NX):
                source = place((z + dz) % NZ, (y + dy) % NY, (x + dx) % NX)
                pairs.append((source, place(z, y, x)))
    return lax.ppermute(value, "dp", pairs)


def along(axis, steps):
    return (steps, 0, 0) if axis == 0 else (0, 0, steps)


def gathered(meta, shard_in, shard_out):
    both = stacked(shard_in, shard_out)
    other = moved(both, (0, 1, 0))
    rows, half = 2 * PIECE, 4 * PIECE
    pair_in, pair_out = arranged(
        "pairs", (both, other), [(0, 0, PIECE), (1, 0, PIECE)], [(0, PIECE, PIECE), (1, PIECE, PIECE)]
    )
    parts = [pair_in, pair_out]
    for r in (1, 3, 2):
        parts += [moved(pair_in, along(2, r)), moved(pair_out, along(0, r))]
    four_in, four_out = arranged(
        "fours", parts, [(i, 0, rows) for i in (0, 2, 6, 4)], [(i, 0, rows) for i in (1, 3, 7, 5)]
    )
    near_in = [four_in, moved(four_in, along(0, 1)), moved(four_in, along(0, -1))]
    near_out = [four_out, moved(four_out, along(2, 1)), moved(four_out, along(2, -1))]
    came = (near_in[2], near_in[1], near_out[2], near_out[1])
    cuts = arranged("cuts", came, *[[(i, half * (i % 2), half)] for i in range(4)])
    far_in = [moved(cuts[0], along(0, -1)), moved(cuts[1], along(0, 1))]
    far_out = [moved(cuts[2], along(2, -1)), moved(cuts[3], along(2, 1))]
    return assemble(meta, near_in + far_in, near_out + far_out), pair_in


def reduced(meta, operands):
    rows = RANK // 2
    far = small_call(far_grad_kernel, "far_grads", (vshape((rows, 2048), BF16),) * 4, *operands, meta=meta)
    near = small_call(near_grad_kernel, "near_grads", (vshape((RANK, 2048), BF16),) * 6, *operands, meta=meta)
    args, own = [], []
    for which, axis in ((0, 0), (1, 2)):
        top, bottom = far[2 * which : 2 * which + 2]
        ahead, behind, here = near[3 * which : 3 * which + 3]
        args += [ahead, behind, moved(top, along(axis, -1)), moved(bottom, along(axis, 1))]
        own.append(here)
    added = small_call(add_kernel, "add_far", (vshape((RANK, 2048), BF16),) * 4, *args)
    args = []
    for which, axis in ((0, 0), (1, 2)):
        ahead, behind = added[2 * which : 2 * which + 2]
        args += [own[which], moved(ahead, along(axis, -1)), moved(behind, along(axis, 1))]
    shapes = tuple(vshape((RANK, NY * PIECE), BF16) for _ in range(NX + NZ))
    two = small_call(sum_one_kernel, "sum_one", shapes, *args, meta=meta)
    gin, gout = two[:NX], two[NX:]
    gin = [gin[0]] + [moved(gin[r], along(2, -r)) for r in (1, 2, 3)]
    gout = [gout[0]] + [moved(gout[r], along(0, -r)) for r in (1, 2, 3)]
    shapes = (vshape((2, RANK, PIECE), BF16),) * 2
    keep, send = small_call(sum_two_kernel, "sum_two", shapes, *gin, *gout, meta=meta)
    got = moved(send, (0, 1, 0))
    return (*small_call(sum_three_kernel, "sum_three", (hshape((PIECE, RANK), F32),) * 2, keep, got), far[0])


def body(inputs, cotangent, sample_ids, out_bases, in_bases, proj_in, proj_out, gains):
    section = lax.axis_index("section")
    dp = lax.axis_index("dp")
    place_ids = jnp.stack([dp // (NY * NX), (dp // NX) % NY, dp % NX, section])
    meta = jnp.concatenate([place_ids.astype(jnp.int32), sample_ids[0]])
    (w_in, w_out), after = gathered(meta, proj_in[0], proj_out[0])
    heights, grads, base_in, base_out, pres, rstds, acts, dpres, results, fresh, ingrads = fetch(
        inputs, cotangent, in_bases[0], out_bases[0], after
    )
    state = (heights, pres, rstds, acts, results, fresh)
    back = (grads, dpres, ingrads)
    fast, slow, sent = None, None, None
    for tick in range(TICKS):
        out = {}

        def arrived(pairs, at):
            codes = [fast] if live(tick - 1, pairs, at, "fast") else []
            return codes + ([slow] if live(tick - 2, pairs, at, "slow") else [])

        if tick < FORWARD_AT[-1] + MICRO:
            codes = arrived(FORWARD_PAIRS, FORWARD_AT)
            out, state = forward_tick(tick, meta, codes, base_in, base_out, gains, w_in, w_out, state)
        if tick >= BACKWARD_AT[-1]:
            heights, pres, rstds = state[:3]
            codes = arrived(BACKWARD_PAIRS, BACKWARD_AT)
            out, back = backward_tick(tick, meta, codes, out, heights, pres, rstds, gains, w_in, w_out, back)

        def hop(wire):
            pairs = live(tick, FORWARD_PAIRS, FORWARD_AT, wire) + live(tick, BACKWARD_PAIRS, BACKWARD_AT, wire)
            return lax.ppermute(out[wire], "section", pairs) if pairs else None

        slow, sent = sent, hop("slow")
        fast = hop("fast")
    heights, pres, rstds, acts, results, fresh = state
    grads, dpres, ingrads = back
    grad_in, grad_out, after = reduced(meta, (heights, grads, rstds, dpres, acts, gains))
    results, ingrads, new_in, new_out = flush(meta, heights, results, fresh, ingrads, base_in, base_out, after)
    return results[None], ingrads[None], new_out[None], new_in[None], grad_in[None], grad_out[None]


def solution(mesh):
    in_specs = (
        P("dp", None),
        P("dp", None),
        P("dp", None),
        P("section", "dp", None, None),
        P("section", "dp", None, None),
        P("section", "dp", None),
        P("section", "dp", None),
        P("section", None),
    )
    out_specs = (
        P("section", "dp", None),
        P("section", "dp", None),
        P("section", "dp", None, None),
        P("section", "dp", None, None),
        P("section", "dp", None),
        P("section", "dp", None),
    )
    return jax.shard_map(body, mesh=mesh, in_specs=in_specs, out_specs=out_specs, check_vma=False)
```

```python
import functools

import jax
import jax.numpy as jnp
from jax import lax
from jax.experimental import pallas as pl
from jax.experimental.pallas import tpu as pltpu
from jax.sharding import PartitionSpec as P

D = 8192
RANK = 256
BLOCK = 128
SEQ = 32
MICRO = 4
SECTIONS = 4
TOKENS = MICRO * SEQ
NZ, NY, NX = 4, 2, 4
PIECE = 256
WIDE = D + BLOCK
F32 = jnp.float32
BF16 = jnp.bfloat16
VM = pl.BlockSpec(memory_space=pltpu.VMEM)
SM = pl.BlockSpec(memory_space=pltpu.SMEM)
HB = pl.BlockSpec(memory_space=pltpu.HBM)
ANY = pl.BlockSpec(memory_space=pl.ANY)
NN = (((1,), (0,)), ((), ()))
NT = (((1,), (1,)), ((), ()))
FORWARD_AT = (0, 1, 3, 4)
BACKWARD_AT = (8, 7, 5, 4)
TICKS = MICRO + 8
SLOW = (1, 2)


def vmem(value):
    return pltpu.with_memory_space_constraint(value, pltpu.VMEM)


def hbm(value):
    return pltpu.with_memory_space_constraint(value, pltpu.HBM)


def vshape(shape, dtype):
    return pltpu.VMEM(shape, dtype)


def hshape(shape, dtype):
    return jax.ShapeDtypeStruct(shape, dtype)


def params():
    return pltpu.CompilerParams(vmem_limit_bytes=12 * 2**20)


def mm(a, b, dims):
    return lax.dot_general(a, b, dims, preferred_element_type=F32)


def coded(values):
    top = jnp.max(jnp.abs(values), axis=1, keepdims=True) + 1e-06
    scale = top.astype(BF16).astype(F32)
    code = (values * (1.0 / scale)).astype(BF16)
    return code, scale


def received(codes, slow_here, lanes):
    if len(codes) == 1:
        return codes[0][:, lanes]
    return jnp.where(slow_here, codes[1][:, lanes], codes[0][:, lanes])


def hand_out(wires, outs, code, slow_here):
    for wire, out in zip(wires, outs):

        @pl.when(slow_here if wire == "slow" else jnp.logical_not(slow_here))
        def _(out=out):
            out[...] = code[...]


FORWARD_PAIRS = [(s, s + 1) for s in range(SECTIONS - 1)]
BACKWARD_PAIRS = [(s, s - 1) for s in range(1, SECTIONS)]


def live(tick, pairs, at, wire):
    return [
        pair for pair in pairs if 0 <= tick - at[pair[0]] < MICRO and (set(pair) == set(SLOW)) == (wire == "slow")
    ]


def fetch_kernel(inputs, cotangent, table_in, table_out, after, heights, grads, base_in, base_out, *rest):
    sems = rest[-1]
    moves = [(inputs, heights), (cotangent, grads), (table_in, base_in), (table_out, base_out)]
    copies = [pltpu.make_async_copy(source, target, sems.at[i]) for i, (source, target) in enumerate(moves)]
    for copy in copies:
        copy.start()
    for copy in copies:
        copy.wait()


def fetch(inputs, cotangent, table_in, table_out, after):
    return pl.pallas_call(
        fetch_kernel,
        out_shape=(
            vshape(inputs.shape, BF16),
            vshape(cotangent.shape, BF16),
            vshape(table_in.shape, BF16),
            vshape(table_out.shape, BF16),
            vshape((TOKENS, RANK), F32),
            vshape((TOKENS, BLOCK), F32),
            vshape((TOKENS, RANK), BF16),
            vshape((TOKENS, RANK), BF16),
            vshape((TOKENS, D), BF16),
            vshape((TOKENS, D), BF16),
            vshape((TOKENS, D), BF16),
        ),
        in_specs=[HB] * 4 + [ANY],
        out_specs=(VM,) * 11,
        scratch_shapes=[pltpu.SemaphoreType.DMA((4,))],
        compiler_params=params(),
        cost_estimate=pl.CostEstimate(flops=0, bytes_accessed=20 * 2**20, transcendentals=0),
        name="fetch",
    )(hbm(inputs), hbm(cotangent), hbm(table_in), hbm(table_out), after)


def settle(meta, first, full, ref, r, start, stop):
    for q in range(start, stop):
        for p in range(NY):
            z = lax.rem(meta[0] + (r if first else q), NZ)
            x = lax.rem(meta[2] + (q if first else r), NX)
            y = lax.rem(meta[1] + p, NY)
            at = pl.multiple_of((z * NY * NX + y * NX + x) * PIECE, PIECE)
            k = ((q - start) * NY + p) * PIECE
            full[pl.ds(at, PIECE), :] = ref[k : k + PIECE, :]


def near_kernel(meta, *refs):
    for which in range(2):
        own, after, before = refs[3 * which : 3 * which + 3]
        full = refs[6 + which]
        settle(meta, which == 0, full, own, 0, 0, 4)
        settle(meta, which == 0, full, after, 1, 0, 4)
        settle(meta, which == 0, full, before, 3, 0, 4)


def far_kernel(meta, *refs):
    for which in range(2):
        top, bottom = refs[2 * which : 2 * which + 2]
        full = refs[6 + which]
        settle(meta, which == 0, full, top, 2, 0, 2)
        settle(meta, which == 0, full, bottom, 2, 2, 4)


def assemble(meta, parts_in, parts_out):
    shapes = (vshape((D, RANK), BF16),) * 2
    near = parts_in[:3] + parts_out[:3]
    full = small_call(near_kernel, "assemble_near", shapes, *near, meta=meta)
    far = parts_in[3:] + parts_out[3:]
    return small_call(far_kernel, "assemble_far", shapes, *far, *full, meta=meta, aliases={5: 0, 6: 1})


def both_kernel(one, two, out, sems):
    copies = [
        pltpu.make_async_copy(ref, out.at[pl.ds(i * PIECE, PIECE)], sems.at[i]) for i, ref in enumerate((one, two))
    ]
    for copy in copies:
        copy.start()
    for copy in copies:
        copy.wait()


def stacked(one, two):
    return pl.pallas_call(
        both_kernel,
        out_shape=vshape((2 * PIECE, RANK), BF16),
        in_specs=[HB] * 2,
        out_specs=VM,
        scratch_shapes=[pltpu.SemaphoreType.DMA((2,))],
        compiler_params=params(),
        name="both",
    )(hbm(one), hbm(two))


def rows_kernel(plan, n_in, *refs):
    for source, at, rows, target, to in plan:
        refs[n_in + target][to : to + rows, :] = refs[source][at : at + rows, :]


def arranged(name, args, *outs):
    plan, sizes = [], []
    for target, pieces in enumerate(outs):
        to = 0
        for source, at, rows in pieces:
            plan.append((source, at, rows, target, to))
            to += rows
        sizes.append(to)
    shapes = tuple(vshape((size,) + args[0].shape[1:], args[0].dtype) for size in sizes)
    return small_call(functools.partial(rows_kernel, plan, len(args)), name, shapes, *args)


def forward_kernel(tick, n_codes, wires, meta, *refs):
    codes, refs = refs[:n_codes], refs[n_codes:]
    (
        base_in, base_out, gain, w_in, w_out, heights_, pres_, rstds_, acts_, results_, fresh_,
        *code_out, heights, pres, rstds, acts, results, fresh,
        sum_buf, square_buf, code_new,
    ) = refs
    section = meta[3]
    slot = tick - (section + (section >= SLOW[1]).astype(jnp.int32))

    @pl.when((slot >= 0) & (slot < MICRO))
    def _():
        sample = meta[4 + slot]
        rows = pl.ds(pl.multiple_of(slot * SEQ, SEQ), SEQ)

        def project(decode):
            if decode:
                scales = received(codes, section == SLOW[1], slice(D, WIDE)).astype(F32)
            pre = jnp.zeros((SEQ, RANK), F32)
            square = jnp.zeros((SEQ, BLOCK), F32)
            for i in range(D // PIECE):
                scaled = []
                for half in range(PIECE // BLOCK):
                    b = i * (PIECE // BLOCK) + half
                    lanes = slice(b * BLOCK, (b + 1) * BLOCK)
                    if decode:
                        value = received(codes, section == SLOW[1], lanes).astype(F32) * scales[:, b : b + 1]
                        height = (base_in[sample, :, lanes].astype(F32) + value).astype(BF16)
                        heights[rows, lanes] = height
                    else:
                        height = heights[rows, lanes]
                    h = height.astype(F32)
                    square += h * h
                    scaled.append((h * gain[:, lanes]).astype(BF16))
                pre += mm(jnp.concatenate(scaled, axis=1), w_in[i * PIECE : (i + 1) * PIECE, :], NN)
            sum_buf[...] = pre
            square_buf[...] = square

        if codes:

            @pl.when(section > 0)
            def _():
                project(True)

        if 0 <= tick - FORWARD_AT[0] < MICRO:

            @pl.when(section == 0)
            def _():
                project(False)

        rstd = lax.rsqrt(jnp.sum(square_buf[...], axis=1, keepdims=True) * (1.0 / D) + 1e-05)
        pre = sum_buf[...] * rstd
        act = (pre / (1.0 + jnp.exp(-pre))).astype(BF16)
        pres[rows, :] = pre
        rstds[rows, :] = jnp.broadcast_to(rstd, (SEQ, BLOCK))
        acts[rows, :] = act
        lane = lax.broadcasted_iota(jnp.int32, (SEQ, BLOCK), 1)
        scales_new = jnp.zeros((SEQ, BLOCK), F32)
        for i in range(D // PIECE):
            branch = mm(act, w_out[i * PIECE : (i + 1) * PIECE, :], NT)
            for half in range(PIECE // BLOCK):
                b = i * (PIECE // BLOCK) + half
                lanes = slice(b * BLOCK, (b + 1) * BLOCK)
                part = branch[:, half * BLOCK : (half + 1) * BLOCK]
                result = (heights[rows, lanes].astype(F32) + part).astype(BF16)
                results[rows, lanes] = result
                if not code_out:
                    continue
                base = base_out[sample, :, lanes].astype(F32)
                new, scale = coded(result.astype(F32) - base)
                code_new[:, lanes] = new
                fresh[rows, lanes] = (base + new.astype(F32) * scale).astype(BF16)
                scales_new = jnp.where(lane == b, scale, scales_new)
        if code_out:
            code_new[:, D:] = scales_new.astype(BF16)
            hand_out(wires, code_out, code_new, section == SLOW[0])


def forward_tick(tick, meta, codes, base_in, base_out, gain, w_in, w_out, state):
    heights, pres, rstds, acts, results, fresh = state
    first = 1 + len(codes) + 5
    wires = [wire for wire in ("fast", "slow") if live(tick, FORWARD_PAIRS, FORWARD_AT, wire)]
    made = [vshape((SEQ, WIDE), BF16)] * len(wires)
    out = pl.pallas_call(
        functools.partial(forward_kernel, tick, len(codes), wires),
        out_shape=(
            *made,
            vshape(heights.shape, BF16),
            vshape(pres.shape, F32),
            vshape(rstds.shape, F32),
            vshape(acts.shape, BF16),
            vshape(results.shape, BF16),
            vshape(fresh.shape, BF16),
        ),
        in_specs=[SM] + [VM] * (len(codes) + 5 + 6),
        out_specs=(VM,) * (6 + len(made)),
        scratch_shapes=[
            pltpu.VMEM((SEQ, RANK), F32),
            pltpu.VMEM((SEQ, BLOCK), F32),
            pltpu.VMEM((SEQ, WIDE), BF16),
        ],
        input_output_aliases={first + i: len(made) + i for i in range(6)},
        compiler_params=params(),
        cost_estimate=pl.CostEstimate(flops=2 * 2 * SEQ * D * RANK, bytes_accessed=16 * 2**20, transcendentals=0),
        name="forward_tick",
    )(
        meta, *map(vmem, codes), vmem(base_in), vmem(base_out), vmem(gain), vmem(w_in), vmem(w_out),
        vmem(heights), vmem(pres), vmem(rstds), vmem(acts), vmem(results), vmem(fresh),
    )
    return dict(zip(wires, out)), out[len(made) :]


def backward_kernel(tick, n_codes, n_started, wires, meta, *refs):
    codes, refs = refs[:n_codes], refs[n_codes + n_started :]
    (
        heights, pres, rstds, gain, w_in, w_out, grads_, dpres_, ingrads_,
        *code_out, grads, dpres, ingrads,
        sum_buf, code_new,
    ) = refs
    section = meta[3]
    slot = tick - BACKWARD_AT[-1] - (SECTIONS - 1 - section + (section <= SLOW[0]).astype(jnp.int32))

    @pl.when((slot >= 0) & (slot < MICRO))
    def _():
        rows = pl.ds(pl.multiple_of(slot * SEQ, SEQ), SEQ)

        def project(decode):
            if decode:
                scales = received(codes, section == SLOW[0], slice(D, WIDE)).astype(F32)
            down = jnp.zeros((SEQ, RANK), F32)
            for i in range(D // PIECE):
                if decode:
                    for half in range(PIECE // BLOCK):
                        b = i * (PIECE // BLOCK) + half
                        lanes = slice(b * BLOCK, (b + 1) * BLOCK)
                        value = received(codes, section == SLOW[0], lanes).astype(F32) * scales[:, b : b + 1]
                        grads[rows, lanes] = value.astype(BF16)
                piece = slice(i * PIECE, (i + 1) * PIECE)
                down += mm(grads[rows, piece], w_out[piece, :], NN)
            sum_buf[...] = down

        if codes:

            @pl.when(section < SECTIONS - 1)
            def _():
                project(True)

        if 0 <= tick - BACKWARD_AT[-1] < MICRO:

            @pl.when(section == SECTIONS - 1)
            def _():
                project(False)

        pre = pres[rows, :]
        rstd = rstds[rows, :]
        sig = 1.0 / (1.0 + jnp.exp(-pre))
        dpre = (sum_buf[...] * sig * (1.0 + pre * (1.0 - sig))).astype(BF16)
        dpres[rows, :] = dpre
        inner = jnp.sum(dpre.astype(F32) * pre, axis=1, keepdims=True) * (1.0 / D)
        pull = rstd * rstd * inner
        lane = lax.broadcasted_iota(jnp.int32, (SEQ, BLOCK), 1)
        scales_new = jnp.zeros((SEQ, BLOCK), F32)
        for i in range(D // PIECE):
            dnorm = mm(dpre, w_in[i * PIECE : (i + 1) * PIECE, :], NT)
            for half in range(PIECE // BLOCK):
                b = i * (PIECE // BLOCK) + half
                lanes = slice(b * BLOCK, (b + 1) * BLOCK)
                extra = dnorm[:, half * BLOCK : (half + 1) * BLOCK] * gain[:, lanes]
                dh = (
                    grads[rows, lanes].astype(F32)
                    + rstd * extra
                    - heights[rows, lanes].astype(F32) * pull
                )
                ingrads[rows, lanes] = dh.astype(BF16)
                if code_out:
                    new, scale = coded(dh)
                    code_new[:, lanes] = new
                    scales_new = jnp.where(lane == b, scale, scales_new)
        if code_out:
            code_new[:, D:] = scales_new.astype(BF16)
            hand_out(wires, code_out, code_new, section == SLOW[1])


def backward_tick(tick, meta, codes, begun, heights, pres, rstds, gain, w_in, w_out, state):
    grads, dpres, ingrads = state
    wires = [wire for wire in ("fast", "slow") if live(tick, BACKWARD_PAIRS, BACKWARD_AT, wire)]
    made = [vshape((SEQ, WIDE), BF16)] * len(wires)
    shared = [wire for wire in wires if wire in begun]
    first = 1 + len(codes) + len(shared) + 6
    aliases = {1 + len(codes) + i: wires.index(wire) for i, wire in enumerate(shared)}
    out = pl.pallas_call(
        functools.partial(backward_kernel, tick, len(codes), len(shared), wires),
        out_shape=(
            *made,
            vshape(grads.shape, BF16),
            vshape(dpres.shape, BF16),
            vshape(ingrads.shape, BF16),
        ),
        in_specs=[SM] + [VM] * (len(codes) + len(shared) + 6 + 3),
        out_specs=(VM,) * (3 + len(made)),
        scratch_shapes=[pltpu.VMEM((SEQ, RANK), F32), pltpu.VMEM((SEQ, WIDE), BF16)],
        input_output_aliases=aliases | {first + i: len(made) + i for i in range(3)},
        compiler_params=params(),
        cost_estimate=pl.CostEstimate(flops=2 * 2 * SEQ * D * RANK, bytes_accessed=16 * 2**20, transcendentals=0),
        name="backward_tick",
    )(
        meta, *map(vmem, codes), *[vmem(begun[wire]) for wire in shared],
        vmem(heights), vmem(pres), vmem(rstds), vmem(gain), vmem(w_in), vmem(w_out),
        vmem(grads), vmem(dpres), vmem(ingrads),
    )
    return begun | dict(zip(wires, out)), out[len(made) :]


def flush_kernel(
    meta, heights, results, fresh, ingrads, base_in, base_out, after, results_out, ingrads_out, new_in, new_out, sems
):
    section = meta[3]
    unused = 10 - (meta[4] + meta[5] + meta[6] + meta[7])
    always = [(results, results_out), (ingrads, ingrads_out), (base_in.at[unused], new_in.at[unused])]
    always.append((base_out.at[unused], new_out.at[unused]))
    copies = [pltpu.make_async_copy(source, target, sems.at[i]) for i, (source, target) in enumerate(always)]

    def table(rows_of, base, new, first):
        fresh_ones, old_ones = [], []
        for j in range(MICRO):
            target, sem = new.at[meta[4 + j]], sems.at[first + j]
            fresh_ones.append(pltpu.make_async_copy(rows_of.at[pl.ds(j * SEQ, SEQ)], target, sem))
            old_ones.append(pltpu.make_async_copy(base.at[meta[4 + j]], target, sem))
        return fresh_ones, old_ones

    received, kept_in = table(heights, base_in, new_in, 4)
    sent, kept_out = table(fresh, base_out, new_out, 4 + MICRO)
    groups = [
        (section > 0, received),
        (section == 0, kept_in),
        (section < SECTIONS - 1, sent),
        (section == SECTIONS - 1, kept_out),
    ]

    def run(act):
        for copy in copies:
            act(copy)
        for condition, group in groups:

            @pl.when(condition)
            def _(group=group):
                for copy in group:
                    act(copy)

    run(lambda copy: copy.start())
    run(lambda copy: copy.wait())


def flush(meta, heights, results, fresh, ingrads, base_in, base_out, after):
    return pl.pallas_call(
        flush_kernel,
        out_shape=(
            hshape(results.shape, BF16),
            hshape(ingrads.shape, BF16),
            hshape(base_in.shape, BF16),
            hshape(base_out.shape, BF16),
        ),
        in_specs=[SM] + [VM] * 6 + [ANY],
        out_specs=(HB,) * 4,
        scratch_shapes=[pltpu.SemaphoreType.DMA((4 + 2 * MICRO,))],
        compiler_params=params(),
        cost_estimate=pl.CostEstimate(flops=0, bytes_accessed=16 * 2**20, transcendentals=0),
        name="flush",
    )(meta, *map(vmem, (heights, results, fresh, ingrads, base_in, base_out)), after)


def grad_lanes(meta, which, r, i):
    if which == 0:
        z = lax.rem(meta[0] + r, NZ)
        return pl.ds(pl.multiple_of((z * NY * NX + i) * PIECE, PIECE), PIECE)
    x = lax.rem(meta[2] + r, NX)
    return pl.ds(pl.multiple_of((i * NX + x) * PIECE, PIECE), PIECE)


def left_sides(rstds, dpres, acts):
    return (dpres[...].astype(F32) * rstds[:, :1]).T.astype(BF16), acts[...].astype(F32).T.astype(BF16)


def right_side(which, lanes, heights, grads, gain):
    if which == 0:
        return (heights[:, lanes].astype(F32) * gain[:, lanes]).astype(BF16)
    return grads[:, lanes]


def far_grad_kernel(meta, heights, grads, rstds, dpres, acts, gain, *outs):
    left = left_sides(rstds, dpres, acts)
    for which in range(2):
        for i in range(NY * 4):
            product = mm(left[which], right_side(which, grad_lanes(meta, which, 2, i), heights, grads, gain), NN)
            product = product.astype(BF16)
            for half in range(2):
                outs[2 * which + half][:, i * PIECE : (i + 1) * PIECE] = product[half * 128 : (half + 1) * 128]


def near_grad_kernel(meta, heights, grads, rstds, dpres, acts, gain, *outs):
    left = left_sides(rstds, dpres, acts)
    for which in range(2):
        for k, r in enumerate((1, 3, 0)):
            for i in range(NY * 4):
                product = mm(left[which], right_side(which, grad_lanes(meta, which, r, i), heights, grads, gain), NN)
                outs[3 * which + k][:, i * PIECE : (i + 1) * PIECE] = product.astype(BF16)


def add_kernel(*refs):
    for which in range(2):
        ahead, behind, top, bottom = refs[4 * which : 4 * which + 4]
        ahead_new, behind_new = refs[8 + 2 * which : 10 + 2 * which]
        for i in range(4):
            lanes = slice(i * 512, (i + 1) * 512)
            ahead_new[:128, lanes] = (ahead[:128, lanes].astype(F32) + top[:, lanes].astype(F32)).astype(BF16)
            ahead_new[128:, lanes] = ahead[128:, lanes]
            behind_new[:128, lanes] = behind[:128, lanes]
            behind_new[128:, lanes] = (behind[128:, lanes].astype(F32) + bottom[:, lanes].astype(F32)).astype(BF16)


def sum_one_kernel(meta, *refs):
    gin, gout, outs = refs[:3], refs[3:6], refs[6:]
    for r in range(NX):
        for y in range(NY):
            x = lax.rem(meta[2] + r, NX)
            lanes = pl.ds(pl.multiple_of((y * NX + x) * PIECE, PIECE), PIECE)
            total = sum(ref[:, lanes].astype(F32) for ref in gin)
            outs[r][:, y * PIECE : (y + 1) * PIECE] = total.astype(BF16)
    for r in range(NZ):
        for y in range(NY):
            z = lax.rem(meta[0] + r, NZ)
            lanes = pl.ds(pl.multiple_of((z * NY + y) * PIECE, PIECE), PIECE)
            total = sum(ref[:, lanes].astype(F32) for ref in gout)
            outs[NX + r][:, y * PIECE : (y + 1) * PIECE] = total.astype(BF16)


def sum_two_kernel(meta, *refs):
    gin, gout, (keep, send) = refs[:NX], refs[NX : NX + NZ], refs[NX + NZ :]
    for which, group in enumerate((gin, gout)):
        for p, out in enumerate((keep, send)):
            y = lax.rem(meta[1] + p, NY)
            lanes = pl.ds(pl.multiple_of(y * PIECE, PIECE), PIECE)
            out[which] = sum(ref[:, lanes].astype(F32) for ref in group).astype(BF16)


def sum_three_kernel(keep, got, gin, gout):
    gin[...] = (keep[0].astype(F32) + got[0].astype(F32)).T
    gout[...] = (keep[1].astype(F32) + got[1].astype(F32)).T


def small_call(kernel, name, shapes, *args, meta=None, aliases={}):
    scalars = [] if meta is None else [meta]
    return pl.pallas_call(
        kernel,
        out_shape=shapes,
        in_specs=[SM] * len(scalars) + [VM] * len(args),
        out_specs=(VM,) * len(shapes),
        input_output_aliases=aliases,
        compiler_params=params(),
        cost_estimate=pl.CostEstimate(flops=0, bytes_accessed=8 * 2**20, transcendentals=0),
        name=name,
    )(*scalars, *map(vmem, args))


def place(z, y, x):
    return (z * NY + y) * NX + x


def moved(value, shift):
    dz, dy, dx = shift
    pairs = []
    for z in range(NZ):
        for y in range(NY):
            for x in range(NX):
                source = place((z + dz) % NZ, (y + dy) % NY, (x + dx) % NX)
                pairs.append((source, place(z, y, x)))
    return lax.ppermute(value, "dp", pairs)


def along(axis, steps):
    return (steps, 0, 0) if axis == 0 else (0, 0, steps)


def gathered(meta, shard_in, shard_out):
    both = stacked(shard_in, shard_out)
    other = moved(both, (0, 1, 0))
    rows, half = 2 * PIECE, 4 * PIECE
    pair_in, pair_out = arranged(
        "pairs", (both, other), [(0, 0, PIECE), (1, 0, PIECE)], [(0, PIECE, PIECE), (1, PIECE, PIECE)]
    )
    parts = [pair_in, pair_out]
    for r in (1, 3, 2):
        parts += [moved(pair_in, along(2, r)), moved(pair_out, along(0, r))]
    four_in, four_out = arranged(
        "fours", parts, [(i, 0, rows) for i in (0, 2, 6, 4)], [(i, 0, rows) for i in (1, 3, 7, 5)]
    )
    near_in = [four_in, moved(four_in, along(0, 1)), moved(four_in, along(0, -1))]
    near_out = [four_out, moved(four_out, along(2, 1)), moved(four_out, along(2, -1))]
    came = (near_in[2], near_in[1], near_out[2], near_out[1])
    cuts = arranged("cuts", came, *[[(i, half * (i % 2), half)] for i in range(4)])
    far_in = [moved(cuts[0], along(0, -1)), moved(cuts[1], along(0, 1))]
    far_out = [moved(cuts[2], along(2, -1)), moved(cuts[3], along(2, 1))]
    return assemble(meta, near_in + far_in, near_out + far_out), pair_in


def reduced(meta, operands):
    rows = RANK // 2
    far = small_call(far_grad_kernel, "far_grads", (vshape((rows, 2048), BF16),) * 4, *operands, meta=meta)
    near = small_call(near_grad_kernel, "near_grads", (vshape((RANK, 2048), BF16),) * 6, *operands, meta=meta)
    args, own = [], []
    for which, axis in ((0, 0), (1, 2)):
        top, bottom = far[2 * which : 2 * which + 2]
        ahead, behind, here = near[3 * which : 3 * which + 3]
        args += [ahead, behind, moved(top, along(axis, -1)), moved(bottom, along(axis, 1))]
        own.append(here)
    added = small_call(add_kernel, "add_far", (vshape((RANK, 2048), BF16),) * 4, *args)
    args = []
    for which, axis in ((0, 0), (1, 2)):
        ahead, behind = added[2 * which : 2 * which + 2]
        args += [own[which], moved(ahead, along(axis, -1)), moved(behind, along(axis, 1))]
    shapes = tuple(vshape((RANK, NY * PIECE), BF16) for _ in range(NX + NZ))
    two = small_call(sum_one_kernel, "sum_one", shapes, *args, meta=meta)
    gin, gout = two[:NX], two[NX:]
    gin = [gin[0]] + [moved(gin[r], along(2, -r)) for r in (1, 2, 3)]
    gout = [gout[0]] + [moved(gout[r], along(0, -r)) for r in (1, 2, 3)]
    shapes = (vshape((2, RANK, PIECE), BF16),) * 2
    keep, send = small_call(sum_two_kernel, "sum_two", shapes, *gin, *gout, meta=meta)
    got = moved(send, (0, 1, 0))
    return (*small_call(sum_three_kernel, "sum_three", (hshape((PIECE, RANK), F32),) * 2, keep, got), far[0])


def body(inputs, cotangent, sample_ids, out_bases, in_bases, proj_in, proj_out, gains):
    section = lax.axis_index("section")
    dp = lax.axis_index("dp")
    place_ids = jnp.stack([dp // (NY * NX), (dp // NX) % NY, dp % NX, section])
    meta = jnp.concatenate([place_ids.astype(jnp.int32), sample_ids[0]])
    (w_in, w_out), after = gathered(meta, proj_in[0], proj_out[0])
    heights, grads, base_in, base_out, pres, rstds, acts, dpres, results, fresh, ingrads = fetch(
        inputs, cotangent, in_bases[0], out_bases[0], after
    )
    state = (heights, pres, rstds, acts, results, fresh)
    back = (grads, dpres, ingrads)
    fast, slow, sent = None, None, None
    for tick in range(TICKS):
        out = {}

        def arrived(pairs, at):
            codes = [fast] if live(tick - 1, pairs, at, "fast") else []
            return codes + ([slow] if live(tick - 2, pairs, at, "slow") else [])

        if tick < FORWARD_AT[-1] + MICRO:
            codes = arrived(FORWARD_PAIRS, FORWARD_AT)
            out, state = forward_tick(tick, meta, codes, base_in, base_out, gains, w_in, w_out, state)
        if tick >= BACKWARD_AT[-1]:
            heights, pres, rstds = state[:3]
            codes = arrived(BACKWARD_PAIRS, BACKWARD_AT)
            out, back = backward_tick(tick, meta, codes, out, heights, pres, rstds, gains, w_in, w_out, back)

        def hop(wire):
            pairs = live(tick, FORWARD_PAIRS, FORWARD_AT, wire) + live(tick, BACKWARD_PAIRS, BACKWARD_AT, wire)
            return lax.ppermute(out[wire], "section", pairs) if pairs else None

        slow, sent = sent, hop("slow")
        fast = hop("fast")
    heights, pres, rstds, acts, results, fresh = state
    grads, dpres, ingrads = back
    grad_in, grad_out, after = reduced(meta, (heights, grads, rstds, dpres, acts, gains))
    results, ingrads, new_in, new_out = flush(meta, heights, results, fresh, ingrads, base_in, base_out, after)
    return results[None], ingrads[None], new_out[None], new_in[None], grad_in[None], grad_out[None]


def solution(mesh):
    in_specs = (
        P("dp", None),
        P("dp", None),
        P("dp", None),
        P("section", "dp", None, None),
        P("section", "dp", None, None),
        P("section", "dp", None),
        P("section", "dp", None),
        P("section", None),
    )
    out_specs = (
        P("section", "dp", None),
        P("section", "dp", None),
        P("section", "dp", None, None),
        P("section", "dp", None, None),
        P("section", "dp", None),
        P("section", "dp", None),
    )
    return jax.shard_map(body, mesh=mesh, in_specs=in_specs, out_specs=out_specs, check_vma=False)
```

```python
import functools

import jax
import jax.numpy as jnp
from jax import lax
from jax.experimental import pallas as pl
from jax.experimental.pallas import tpu as pltpu
from jax.sharding import PartitionSpec as P

D = 8192
RANK = 256
BLOCK = 128
SEQ = 32
MICRO = 4
SECTIONS = 4
TOKENS = MICRO * SEQ
NZ, NY, NX = 4, 2, 4
PIECE = 256
WIDE = D + BLOCK
F32 = jnp.float32
BF16 = jnp.bfloat16
VM = pl.BlockSpec(memory_space=pltpu.VMEM)
SM = pl.BlockSpec(memory_space=pltpu.SMEM)
HB = pl.BlockSpec(memory_space=pltpu.HBM)
ANY = pl.BlockSpec(memory_space=pl.ANY)
NN = (((1,), (0,)), ((), ()))
NT = (((1,), (1,)), ((), ()))
FORWARD_AT = (0, 1, 3, 4)
BACKWARD_AT = (8, 7, 5, 4)
TICKS = MICRO + 8
SLOW = (1, 2)


def vmem(value):
    return pltpu.with_memory_space_constraint(value, pltpu.VMEM)


def hbm(value):
    return pltpu.with_memory_space_constraint(value, pltpu.HBM)


def vshape(shape, dtype):
    return pltpu.VMEM(shape, dtype)


def hshape(shape, dtype):
    return jax.ShapeDtypeStruct(shape, dtype)


def params():
    return pltpu.CompilerParams(vmem_limit_bytes=12 * 2**20)


def mm(a, b, dims):
    return lax.dot_general(a, b, dims, preferred_element_type=F32)


def coded(values):
    top = jnp.max(jnp.abs(values), axis=1, keepdims=True) + 1e-06
    scale = top.astype(BF16).astype(F32)
    code = (values * (1.0 / scale)).astype(BF16)
    return code, scale


def received(codes, slow_here, lanes):
    if len(codes) == 1:
        return codes[0][:, lanes]
    return jnp.where(slow_here, codes[1][:, lanes], codes[0][:, lanes])


def hand_out(wires, outs, code, slow_here):
    for wire, out in zip(wires, outs):

        @pl.when(slow_here if wire == "slow" else jnp.logical_not(slow_here))
        def _(out=out):
            out[...] = code[...]


FORWARD_PAIRS = [(s, s + 1) for s in range(SECTIONS - 1)]
BACKWARD_PAIRS = [(s, s - 1) for s in range(1, SECTIONS)]


def live(tick, pairs, at, wire):
    return [
        pair for pair in pairs if 0 <= tick - at[pair[0]] < MICRO and (set(pair) == set(SLOW)) == (wire == "slow")
    ]


def fetch_kernel(inputs, cotangent, table_in, table_out, after, heights, grads, base_in, base_out, *rest):
    sems = rest[-1]
    moves = [(inputs, heights), (cotangent, grads), (table_in, base_in), (table_out, base_out)]
    copies = [pltpu.make_async_copy(source, target, sems.at[i]) for i, (source, target) in enumerate(moves)]
    for copy in copies:
        copy.start()
    for copy in copies:
        copy.wait()


def fetch(inputs, cotangent, table_in, table_out, after):
    return pl.pallas_call(
        fetch_kernel,
        out_shape=(
            vshape(inputs.shape, BF16),
            vshape(cotangent.shape, BF16),
            vshape(table_in.shape, BF16),
            vshape(table_out.shape, BF16),
            vshape((TOKENS, RANK), F32),
            vshape((TOKENS, BLOCK), F32),
            vshape((TOKENS, RANK), BF16),
            vshape((TOKENS, RANK), BF16),
            vshape((TOKENS, D), BF16),
            vshape((TOKENS, D), BF16),
            vshape((TOKENS, D), BF16),
        ),
        in_specs=[HB] * 4 + [ANY],
        out_specs=(VM,) * 11,
        scratch_shapes=[pltpu.SemaphoreType.DMA((4,))],
        compiler_params=params(),
        cost_estimate=pl.CostEstimate(flops=0, bytes_accessed=20 * 2**20, transcendentals=0),
        name="fetch",
    )(hbm(inputs), hbm(cotangent), hbm(table_in), hbm(table_out), after)


def settle(meta, first, full, ref, r, start, stop):
    for q in range(start, stop):
        for p in range(NY):
            z = lax.rem(meta[0] + (r if first else q), NZ)
            x = lax.rem(meta[2] + (q if first else r), NX)
            y = lax.rem(meta[1] + p, NY)
            at = pl.multiple_of((z * NY * NX + y * NX + x) * PIECE, PIECE)
            k = ((q - start) * NY + p) * PIECE
            full[pl.ds(at, PIECE), :] = ref[k : k + PIECE, :]


def near_kernel(meta, *refs):
    for which in range(2):
        own, after, before = refs[3 * which : 3 * which + 3]
        full = refs[6 + which]
        settle(meta, which == 0, full, own, 0, 0, 4)
        settle(meta, which == 0, full, after, 1, 0, 4)
        settle(meta, which == 0, full, before, 3, 0, 4)


def far_kernel(meta, *refs):
    for which in range(2):
        top, bottom = refs[2 * which : 2 * which + 2]
        full = refs[6 + which]
        settle(meta, which == 0, full, top, 2, 0, 2)
        settle(meta, which == 0, full, bottom, 2, 2, 4)


def assemble(meta, parts_in, parts_out):
    shapes = (vshape((D, RANK), BF16),) * 2
    near = parts_in[:3] + parts_out[:3]
    full = small_call(near_kernel, "assemble_near", shapes, *near, meta=meta)
    far = parts_in[3:] + parts_out[3:]
    return small_call(far_kernel, "assemble_far", shapes, *far, *full, meta=meta, aliases={5: 0, 6: 1})


def both_kernel(one, two, out, sems):
    copies = [
        pltpu.make_async_copy(ref, out.at[pl.ds(i * PIECE, PIECE)], sems.at[i]) for i, ref in enumerate((one, two))
    ]
    for copy in copies:
        copy.start()
    for copy in copies:
        copy.wait()


def stacked(one, two):
    return pl.pallas_call(
        both_kernel,
        out_shape=vshape((2 * PIECE, RANK), BF16),
        in_specs=[HB] * 2,
        out_specs=VM,
        scratch_shapes=[pltpu.SemaphoreType.DMA((2,))],
        compiler_params=params(),
        name="both",
    )(hbm(one), hbm(two))


def rows_kernel(plan, n_in, *refs):
    for source, at, rows, target, to in plan:
        refs[n_in + target][to : to + rows, :] = refs[source][at : at + rows, :]


def arranged(name, args, *outs):
    plan, sizes = [], []
    for target, pieces in enumerate(outs):
        to = 0
        for source, at, rows in pieces:
            plan.append((source, at, rows, target, to))
            to += rows
        sizes.append(to)
    shapes = tuple(vshape((size,) + args[0].shape[1:], args[0].dtype) for size in sizes)
    return small_call(functools.partial(rows_kernel, plan, len(args)), name, shapes, *args)


def forward_kernel(tick, n_codes, wires, meta, *refs):
    codes, refs = refs[:n_codes], refs[n_codes:]
    (
        base_in, base_out, gain, w_in, w_out, heights_, pres_, rstds_, acts_, results_, fresh_,
        *code_out, heights, pres, rstds, acts, results, fresh,
        sum_buf, square_buf, code_new,
    ) = refs
    section = meta[3]
    slot = tick - (section + (section >= SLOW[1]).astype(jnp.int32))

    @pl.when((slot >= 0) & (slot < MICRO))
    def _():
        sample = meta[4 + slot]
        rows = pl.ds(pl.multiple_of(slot * SEQ, SEQ), SEQ)

        def project(decode):
            if decode:
                scales = received(codes, section == SLOW[1], slice(D, WIDE)).astype(F32)
            pre = jnp.zeros((SEQ, RANK), F32)
            square = jnp.zeros((SEQ, BLOCK), F32)
            for i in range(D // PIECE):
                scaled = []
                for half in range(PIECE // BLOCK):
                    b = i * (PIECE // BLOCK) + half
                    lanes = slice(b * BLOCK, (b + 1) * BLOCK)
                    if decode:
                        value = received(codes, section == SLOW[1], lanes).astype(F32) * scales[:, b : b + 1]
                        height = (base_in[sample, :, lanes].astype(F32) + value).astype(BF16)
                        heights[rows, lanes] = height
                    else:
                        height = heights[rows, lanes]
                    h = height.astype(F32)
                    square += h * h
                    scaled.append((h * gain[:, lanes]).astype(BF16))
                pre += mm(jnp.concatenate(scaled, axis=1), w_in[i * PIECE : (i + 1) * PIECE, :], NN)
            sum_buf[...] = pre
            square_buf[...] = square

        if codes:

            @pl.when(section > 0)
            def _():
                project(True)

        if 0 <= tick - FORWARD_AT[0] < MICRO:

            @pl.when(section == 0)
            def _():
                project(False)

        rstd = lax.rsqrt(jnp.sum(square_buf[...], axis=1, keepdims=True) * (1.0 / D) + 1e-05)
        pre = sum_buf[...] * rstd
        act = (pre / (1.0 + jnp.exp(-pre))).astype(BF16)
        pres[rows, :] = pre
        rstds[rows, :] = jnp.broadcast_to(rstd, (SEQ, BLOCK))
        acts[rows, :] = act
        lane = lax.broadcasted_iota(jnp.int32, (SEQ, BLOCK), 1)
        scales_new = jnp.zeros((SEQ, BLOCK), F32)
        for i in range(D // PIECE):
            branch = mm(act, w_out[i * PIECE : (i + 1) * PIECE, :], NT)
            for half in range(PIECE // BLOCK):
                b = i * (PIECE // BLOCK) + half
                lanes = slice(b * BLOCK, (b + 1) * BLOCK)
                part = branch[:, half * BLOCK : (half + 1) * BLOCK]
                result = (heights[rows, lanes].astype(F32) + part).astype(BF16)
                results[rows, lanes] = result
                if not code_out:
                    continue
                base = base_out[sample, :, lanes].astype(F32)
                new, scale = coded(result.astype(F32) - base)
                code_new[:, lanes] = new
                fresh[rows, lanes] = (base + new.astype(F32) * scale).astype(BF16)
                scales_new = jnp.where(lane == b, scale, scales_new)
        if code_out:
            code_new[:, D:] = scales_new.astype(BF16)
            hand_out(wires, code_out, code_new, section == SLOW[0])


def forward_tick(tick, meta, codes, base_in, base_out, gain, w_in, w_out, state):
    heights, pres, rstds, acts, results, fresh = state
    first = 1 + len(codes) + 5
    wires = [wire for wire in ("fast", "slow") if live(tick, FORWARD_PAIRS, FORWARD_AT, wire)]
    made = [vshape((SEQ, WIDE), BF16)] * len(wires)
    out = pl.pallas_call(
        functools.partial(forward_kernel, tick, len(codes), wires),
        out_shape=(
            *made,
            vshape(heights.shape, BF16),
            vshape(pres.shape, F32),
            vshape(rstds.shape, F32),
            vshape(acts.shape, BF16),
            vshape(results.shape, BF16),
            vshape(fresh.shape, BF16),
        ),
        in_specs=[SM] + [VM] * (len(codes) + 5 + 6),
        out_specs=(VM,) * (6 + len(made)),
        scratch_shapes=[
            pltpu.VMEM((SEQ, RANK), F32),
            pltpu.VMEM((SEQ, BLOCK), F32),
            pltpu.VMEM((SEQ, WIDE), BF16),
        ],
        input_output_aliases={first + i: len(made) + i for i in range(6)},
        compiler_params=params(),
        cost_estimate=pl.CostEstimate(flops=2 * 2 * SEQ * D * RANK, bytes_accessed=16 * 2**20, transcendentals=0),
        name="forward_tick",
    )(
        meta, *map(vmem, codes), vmem(base_in), vmem(base_out), vmem(gain), vmem(w_in), vmem(w_out),
        vmem(heights), vmem(pres), vmem(rstds), vmem(acts), vmem(results), vmem(fresh),
    )
    return dict(zip(wires, out)), out[len(made) :]


def backward_kernel(tick, n_codes, n_started, wires, meta, *refs):
    codes, refs = refs[:n_codes], refs[n_codes + n_started :]
    (
        heights, pres, rstds, gain, w_in, w_out, grads_, dpres_, ingrads_,
        *code_out, grads, dpres, ingrads,
        sum_buf, code_new,
    ) = refs
    section = meta[3]
    slot = tick - BACKWARD_AT[-1] - (SECTIONS - 1 - section + (section <= SLOW[0]).astype(jnp.int32))

    @pl.when((slot >= 0) & (slot < MICRO))
    def _():
        rows = pl.ds(pl.multiple_of(slot * SEQ, SEQ), SEQ)

        def project(decode):
            if decode:
                scales = received(codes, section == SLOW[0], slice(D, WIDE)).astype(F32)
            down = jnp.zeros((SEQ, RANK), F32)
            for i in range(D // PIECE):
                if decode:
                    for half in range(PIECE // BLOCK):
                        b = i * (PIECE // BLOCK) + half
                        lanes = slice(b * BLOCK, (b + 1) * BLOCK)
                        value = received(codes, section == SLOW[0], lanes).astype(F32) * scales[:, b : b + 1]
                        grads[rows, lanes] = value.astype(BF16)
                piece = slice(i * PIECE, (i + 1) * PIECE)
                down += mm(grads[rows, piece], w_out[piece, :], NN)
            sum_buf[...] = down

        if codes:

            @pl.when(section < SECTIONS - 1)
            def _():
                project(True)

        if 0 <= tick - BACKWARD_AT[-1] < MICRO:

            @pl.when(section == SECTIONS - 1)
            def _():
                project(False)

        pre = pres[rows, :]
        rstd = rstds[rows, :]
        sig = 1.0 / (1.0 + jnp.exp(-pre))
        dpre = (sum_buf[...] * sig * (1.0 + pre * (1.0 - sig))).astype(BF16)
        dpres[rows, :] = dpre
        inner = jnp.sum(dpre.astype(F32) * pre, axis=1, keepdims=True) * (1.0 / D)
        pull = rstd * rstd * inner
        lane = lax.broadcasted_iota(jnp.int32, (SEQ, BLOCK), 1)
        scales_new = jnp.zeros((SEQ, BLOCK), F32)
        for i in range(D // PIECE):
            dnorm = mm(dpre, w_in[i * PIECE : (i + 1) * PIECE, :], NT)
            for half in range(PIECE // BLOCK):
                b = i * (PIECE // BLOCK) + half
                lanes = slice(b * BLOCK, (b + 1) * BLOCK)
                extra = dnorm[:, half * BLOCK : (half + 1) * BLOCK] * gain[:, lanes]
                dh = (
                    grads[rows, lanes].astype(F32)
                    + rstd * extra
                    - heights[rows, lanes].astype(F32) * pull
                )
                ingrads[rows, lanes] = dh.astype(BF16)
                if code_out:
                    new, scale = coded(dh)
                    code_new[:, lanes] = new
                    scales_new = jnp.where(lane == b, scale, scales_new)
        if code_out:
            code_new[:, D:] = scales_new.astype(BF16)
            hand_out(wires, code_out, code_new, section == SLOW[1])


def backward_tick(tick, meta, codes, begun, heights, pres, rstds, gain, w_in, w_out, state):
    grads, dpres, ingrads = state
    wires = [wire for wire in ("fast", "slow") if live(tick, BACKWARD_PAIRS, BACKWARD_AT, wire)]
    made = [vshape((SEQ, WIDE), BF16)] * len(wires)
    shared = [wire for wire in wires if wire in begun]
    first = 1 + len(codes) + len(shared) + 6
    aliases = {1 + len(codes) + i: wires.index(wire) for i, wire in enumerate(shared)}
    out = pl.pallas_call(
        functools.partial(backward_kernel, tick, len(codes), len(shared), wires),
        out_shape=(
            *made,
            vshape(grads.shape, BF16),
            vshape(dpres.shape, BF16),
            vshape(ingrads.shape, BF16),
        ),
        in_specs=[SM] + [VM] * (len(codes) + len(shared) + 6 + 3),
        out_specs=(VM,) * (3 + len(made)),
        scratch_shapes=[pltpu.VMEM((SEQ, RANK), F32), pltpu.VMEM((SEQ, WIDE), BF16)],
        input_output_aliases=aliases | {first + i: len(made) + i for i in range(3)},
        compiler_params=params(),
        cost_estimate=pl.CostEstimate(flops=2 * 2 * SEQ * D * RANK, bytes_accessed=16 * 2**20, transcendentals=0),
        name="backward_tick",
    )(
        meta, *map(vmem, codes), *[vmem(begun[wire]) for wire in shared],
        vmem(heights), vmem(pres), vmem(rstds), vmem(gain), vmem(w_in), vmem(w_out),
        vmem(grads), vmem(dpres), vmem(ingrads),
    )
    return begun | dict(zip(wires, out)), out[len(made) :]


def double_kernel(tick, came, f_came, b_came, wires, f_wires, b_wires, meta, *refs):
    refs = list(refs)
    take = lambda n: [refs.pop(0) for _ in range(n)]
    codes = dict(zip(came, take(len(came))))
    bases, (gain, w_in, w_out), old = take(2), take(3), take(9)
    outs, new = dict(zip(wires, take(len(wires)))), take(9)
    sum_buf, square_buf, code_new = refs
    forward_kernel(
        tick, len(f_came), f_wires, meta, *[codes[wire] for wire in f_came], *bases, gain, w_in, w_out, *old[:6],
        *[outs[wire] for wire in f_wires], *new[:6], sum_buf, square_buf, code_new,
    )
    backward_kernel(
        tick, len(b_came), 0, b_wires, meta, *[codes[wire] for wire in b_came], *new[:3], gain, w_in, w_out, *old[6:],
        *[outs[wire] for wire in b_wires], *new[6:], sum_buf, code_new,
    )


def double_tick(tick, meta, codes, f_came, b_came, base_in, base_out, gain, w_in, w_out, state, back):
    came = [wire for wire in codes if wire in f_came or wire in b_came]
    f_wires = [wire for wire in ("fast", "slow") if live(tick, FORWARD_PAIRS, FORWARD_AT, wire)]
    b_wires = [wire for wire in ("fast", "slow") if live(tick, BACKWARD_PAIRS, BACKWARD_AT, wire)]
    wires = [wire for wire in ("fast", "slow") if wire in f_wires or wire in b_wires]
    kept = (*state, *back)
    first = 1 + len(came) + 5
    out = pl.pallas_call(
        functools.partial(double_kernel, tick, came, f_came, b_came, wires, f_wires, b_wires),
        out_shape=(*[vshape((SEQ, WIDE), BF16)] * len(wires), *[vshape(v.shape, v.dtype) for v in kept]),
        in_specs=[SM] + [VM] * (len(came) + 5 + 9),
        out_specs=(VM,) * (len(wires) + 9),
        scratch_shapes=[
            pltpu.VMEM((SEQ, RANK), F32),
            pltpu.VMEM((SEQ, BLOCK), F32),
            pltpu.VMEM((SEQ, WIDE), BF16),
        ],
        input_output_aliases={first + i: len(wires) + i for i in range(9)},
        compiler_params=params(),
        cost_estimate=pl.CostEstimate(flops=4 * 2 * SEQ * D * RANK, bytes_accessed=32 * 2**20, transcendentals=0),
        name="double_tick",
    )(
        meta, *[vmem(codes[wire]) for wire in came], vmem(base_in), vmem(base_out), vmem(gain), vmem(w_in), vmem(w_out),
        *map(vmem, kept),
    )
    return dict(zip(wires, out)), out[len(wires) : len(wires) + 6], out[len(wires) + 6 :]


def flush_kernel(
    meta, heights, results, fresh, ingrads, base_in, base_out, after, results_out, ingrads_out, new_in, new_out, sems
):
    section = meta[3]
    unused = 10 - (meta[4] + meta[5] + meta[6] + meta[7])
    always = [(results, results_out), (ingrads, ingrads_out), (base_in.at[unused], new_in.at[unused])]
    always.append((base_out.at[unused], new_out.at[unused]))
    copies = [pltpu.make_async_copy(source, target, sems.at[i]) for i, (source, target) in enumerate(always)]

    def table(rows_of, base, new, first):
        fresh_ones, old_ones = [], []
        for j in range(MICRO):
            target, sem = new.at[meta[4 + j]], sems.at[first + j]
            fresh_ones.append(pltpu.make_async_copy(rows_of.at[pl.ds(j * SEQ, SEQ)], target, sem))
            old_ones.append(pltpu.make_async_copy(base.at[meta[4 + j]], target, sem))
        return fresh_ones, old_ones

    received, kept_in = table(heights, base_in, new_in, 4)
    sent, kept_out = table(fresh, base_out, new_out, 4 + MICRO)
    groups = [
        (section > 0, received),
        (section == 0, kept_in),
        (section < SECTIONS - 1, sent),
        (section == SECTIONS - 1, kept_out),
    ]

    def run(act):
        for copy in copies:
            act(copy)
        for condition, group in groups:

            @pl.when(condition)
            def _(group=group):
                for copy in group:
                    act(copy)

    run(lambda copy: copy.start())
    run(lambda copy: copy.wait())


def flush(meta, heights, results, fresh, ingrads, base_in, base_out, after):
    return pl.pallas_call(
        flush_kernel,
        out_shape=(
            hshape(results.shape, BF16),
            hshape(ingrads.shape, BF16),
            hshape(base_in.shape, BF16),
            hshape(base_out.shape, BF16),
        ),
        in_specs=[SM] + [VM] * 6 + [ANY],
        out_specs=(HB,) * 4,
        scratch_shapes=[pltpu.SemaphoreType.DMA((4 + 2 * MICRO,))],
        compiler_params=params(),
        cost_estimate=pl.CostEstimate(flops=0, bytes_accessed=16 * 2**20, transcendentals=0),
        name="flush",
    )(meta, *map(vmem, (heights, results, fresh, ingrads, base_in, base_out)), after)


def grad_lanes(meta, which, r, i):
    if which == 0:
        z = lax.rem(meta[0] + r, NZ)
        return pl.ds(pl.multiple_of((z * NY * NX + i) * PIECE, PIECE), PIECE)
    x = lax.rem(meta[2] + r, NX)
    return pl.ds(pl.multiple_of((i * NX + x) * PIECE, PIECE), PIECE)


def left_sides(rstds, dpres, acts):
    return (dpres[...].astype(F32) * rstds[:, :1]).T.astype(BF16), acts[...].astype(F32).T.astype(BF16)


def right_side(which, lanes, heights, grads, gain):
    if which == 0:
        return (heights[:, lanes].astype(F32) * gain[:, lanes]).astype(BF16)
    return grads[:, lanes]


def far_grad_kernel(meta, heights, grads, rstds, dpres, acts, gain, *outs):
    left = left_sides(rstds, dpres, acts)
    for which in range(2):
        for i in range(NY * 4):
            product = mm(left[which], right_side(which, grad_lanes(meta, which, 2, i), heights, grads, gain), NN)
            product = product.astype(BF16)
            for half in range(2):
                outs[2 * which + half][:, i * PIECE : (i + 1) * PIECE] = product[half * 128 : (half + 1) * 128]


def near_grad_kernel(meta, heights, grads, rstds, dpres, acts, gain, *outs):
    left = left_sides(rstds, dpres, acts)
    for which in range(2):
        for k, r in enumerate((1, 3, 0)):
            for i in range(NY * 4):
                product = mm(left[which], right_side(which, grad_lanes(meta, which, r, i), heights, grads, gain), NN)
                outs[3 * which + k][:, i * PIECE : (i + 1) * PIECE] = product.astype(BF16)


def add_kernel(*refs):
    for which in range(2):
        ahead, behind, top, bottom = refs[4 * which : 4 * which + 4]
        ahead_new, behind_new = refs[8 + 2 * which : 10 + 2 * which]
        for i in range(4):
            lanes = slice(i * 512, (i + 1) * 512)
            ahead_new[:128, lanes] = (ahead[:128, lanes].astype(F32) + top[:, lanes].astype(F32)).astype(BF16)
            ahead_new[128:, lanes] = ahead[128:, lanes]
            behind_new[:128, lanes] = behind[:128, lanes]
            behind_new[128:, lanes] = (behind[128:, lanes].astype(F32) + bottom[:, lanes].astype(F32)).astype(BF16)


def sum_one_kernel(meta, *refs):
    gin, gout, outs = refs[:3], refs[3:6], refs[6:]
    for r in range(NX):
        for y in range(NY):
            x = lax.rem(meta[2] + r, NX)
            lanes = pl.ds(pl.multiple_of((y * NX + x) * PIECE, PIECE), PIECE)
            total = sum(ref[:, lanes].astype(F32) for ref in gin)
            outs[r][:, y * PIECE : (y + 1) * PIECE] = total.astype(BF16)
    for r in range(NZ):
        for y in range(NY):
            z = lax.rem(meta[0] + r, NZ)
            lanes = pl.ds(pl.multiple_of((z * NY + y) * PIECE, PIECE), PIECE)
            total = sum(ref[:, lanes].astype(F32) for ref in gout)
            outs[NX + r][:, y * PIECE : (y + 1) * PIECE] = total.astype(BF16)


def sum_two_kernel(meta, *refs):
    gin, gout, (keep, send) = refs[:NX], refs[NX : NX + NZ], refs[NX + NZ :]
    for which, group in enumerate((gin, gout)):
        for p, out in enumerate((keep, send)):
            y = lax.rem(meta[1] + p, NY)
            lanes = pl.ds(pl.multiple_of(y * PIECE, PIECE), PIECE)
            out[which] = sum(ref[:, lanes].astype(F32) for ref in group).astype(BF16)


def sum_three_kernel(keep, got, gin, gout):
    gin[...] = (keep[0].astype(F32) + got[0].astype(F32)).T
    gout[...] = (keep[1].astype(F32) + got[1].astype(F32)).T


def small_call(kernel, name, shapes, *args, meta=None, aliases={}):
    scalars = [] if meta is None else [meta]
    return pl.pallas_call(
        kernel,
        out_shape=shapes,
        in_specs=[SM] * len(scalars) + [VM] * len(args),
        out_specs=(VM,) * len(shapes),
        input_output_aliases=aliases,
        compiler_params=params(),
        cost_estimate=pl.CostEstimate(flops=0, bytes_accessed=8 * 2**20, transcendentals=0),
        name=name,
    )(*scalars, *map(vmem, args))


def place(z, y, x):
    return (z * NY + y) * NX + x


def moved(value, shift):
    dz, dy, dx = shift
    pairs = []
    for z in range(NZ):
        for y in range(NY):
            for x in range(NX):
                source = place((z + dz) % NZ, (y + dy) % NY, (x + dx) % NX)
                pairs.append((source, place(z, y, x)))
    return lax.ppermute(value, "dp", pairs)


def along(axis, steps):
    return (steps, 0, 0) if axis == 0 else (0, 0, steps)


def gathered(meta, shard_in, shard_out):
    both = stacked(shard_in, shard_out)
    other = moved(both, (0, 1, 0))
    rows, half = 2 * PIECE, 4 * PIECE
    pair_in, pair_out = arranged(
        "pairs", (both, other), [(0, 0, PIECE), (1, 0, PIECE)], [(0, PIECE, PIECE), (1, PIECE, PIECE)]
    )
    parts = [pair_in, pair_out]
    for r in (1, 3, 2):
        parts += [moved(pair_in, along(2, r)), moved(pair_out, along(0, r))]
    four_in, four_out = arranged(
        "fours", parts, [(i, 0, rows) for i in (0, 2, 6, 4)], [(i, 0, rows) for i in (1, 3, 7, 5)]
    )
    near_in = [four_in, moved(four_in, along(0, 1)), moved(four_in, along(0, -1))]
    near_out = [four_out, moved(four_out, along(2, 1)), moved(four_out, along(2, -1))]
    came = (near_in[2], near_in[1], near_out[2], near_out[1])
    cuts = arranged("cuts", came, *[[(i, half * (i % 2), half)] for i in range(4)])
    far_in = [moved(cuts[0], along(0, -1)), moved(cuts[1], along(0, 1))]
    far_out = [moved(cuts[2], along(2, -1)), moved(cuts[3], along(2, 1))]
    return assemble(meta, near_in + far_in, near_out + far_out), pair_in


def reduced(meta, operands):
    rows = RANK // 2
    far = small_call(far_grad_kernel, "far_grads", (vshape((rows, 2048), BF16),) * 4, *operands, meta=meta)
    near = small_call(near_grad_kernel, "near_grads", (vshape((RANK, 2048), BF16),) * 6, *operands, meta=meta)
    args, own = [], []
    for which, axis in ((0, 0), (1, 2)):
        top, bottom = far[2 * which : 2 * which + 2]
        ahead, behind, here = near[3 * which : 3 * which + 3]
        args += [ahead, behind, moved(top, along(axis, -1)), moved(bottom, along(axis, 1))]
        own.append(here)
    added = small_call(add_kernel, "add_far", (vshape((RANK, 2048), BF16),) * 4, *args)
    args = []
    for which, axis in ((0, 0), (1, 2)):
        ahead, behind = added[2 * which : 2 * which + 2]
        args += [own[which], moved(ahead, along(axis, -1)), moved(behind, along(axis, 1))]
    shapes = tuple(vshape((RANK, NY * PIECE), BF16) for _ in range(NX + NZ))
    two = small_call(sum_one_kernel, "sum_one", shapes, *args, meta=meta)
    gin, gout = two[:NX], two[NX:]
    gin = [gin[0]] + [moved(gin[r], along(2, -r)) for r in (1, 2, 3)]
    gout = [gout[0]] + [moved(gout[r], along(0, -r)) for r in (1, 2, 3)]
    shapes = (vshape((2, RANK, PIECE), BF16),) * 2
    keep, send = small_call(sum_two_kernel, "sum_two", shapes, *gin, *gout, meta=meta)
    got = moved(send, (0, 1, 0))
    return (*small_call(sum_three_kernel, "sum_three", (hshape((PIECE, RANK), F32),) * 2, keep, got), far[0])


def body(inputs, cotangent, sample_ids, out_bases, in_bases, proj_in, proj_out, gains):
    section = lax.axis_index("section")
    dp = lax.axis_index("dp")
    place_ids = jnp.stack([dp // (NY * NX), (dp // NX) % NY, dp % NX, section])
    meta = jnp.concatenate([place_ids.astype(jnp.int32), sample_ids[0]])
    (w_in, w_out), after = gathered(meta, proj_in[0], proj_out[0])
    heights, grads, base_in, base_out, pres, rstds, acts, dpres, results, fresh, ingrads = fetch(
        inputs, cotangent, in_bases[0], out_bases[0], after
    )
    state = (heights, pres, rstds, acts, results, fresh)
    back = (grads, dpres, ingrads)
    fast, slow, sent = None, None, None
    for tick in range(TICKS):
        codes = {"fast": fast, "slow": slow}

        def arrived(pairs, at):
            return [wire for wire, ago in (("fast", 1), ("slow", 2)) if live(tick - ago, pairs, at, wire)]

        f_came, b_came = arrived(FORWARD_PAIRS, FORWARD_AT), arrived(BACKWARD_PAIRS, BACKWARD_AT)
        bases = (base_in, base_out)
        if tick < BACKWARD_AT[-1]:
            came = [codes[wire] for wire in f_came]
            out, state = forward_tick(tick, meta, came, *bases, gains, w_in, w_out, state)
        elif tick < FORWARD_AT[-1] + MICRO:
            out, state, back = double_tick(tick, meta, codes, f_came, b_came, *bases, gains, w_in, w_out, state, back)
        else:
            came = [codes[wire] for wire in b_came]
            out, back = backward_tick(tick, meta, came, {}, *state[:3], gains, w_in, w_out, back)

        def hop(wire):
            pairs = live(tick, FORWARD_PAIRS, FORWARD_AT, wire) + live(tick, BACKWARD_PAIRS, BACKWARD_AT, wire)
            return lax.ppermute(out[wire], "section", pairs) if pairs else None

        slow, sent = sent, hop("slow")
        fast = hop("fast")
    heights, pres, rstds, acts, results, fresh = state
    grads, dpres, ingrads = back
    grad_in, grad_out, after = reduced(meta, (heights, grads, rstds, dpres, acts, gains))
    results, ingrads, new_in, new_out = flush(meta, heights, results, fresh, ingrads, base_in, base_out, after)
    return results[None], ingrads[None], new_out[None], new_in[None], grad_in[None], grad_out[None]


def solution(mesh):
    in_specs = (
        P("dp", None),
        P("dp", None),
        P("dp", None),
        P("section", "dp", None, None),
        P("section", "dp", None, None),
        P("section", "dp", None),
        P("section", "dp", None),
        P("section", None),
    )
    out_specs = (
        P("section", "dp", None),
        P("section", "dp", None),
        P("section", "dp", None, None),
        P("section", "dp", None, None),
        P("section", "dp", None),
        P("section", "dp", None),
    )
    return jax.shard_map(body, mesh=mesh, in_specs=in_specs, out_specs=out_specs, check_vma=False)
```

```python
import functools

import jax
import jax.numpy as jnp
from jax import lax
from jax.experimental import pallas as pl
from jax.experimental.pallas import tpu as pltpu
from jax.sharding import PartitionSpec as P

D = 8192
RANK = 256
BLOCK = 128
SEQ = 32
MICRO = 4
SECTIONS = 4
TOKENS = MICRO * SEQ
NZ, NY, NX = 4, 2, 4
PIECE = 256
WIDE = D + BLOCK
F32 = jnp.float32
BF16 = jnp.bfloat16
VM = pl.BlockSpec(memory_space=pltpu.VMEM)
SM = pl.BlockSpec(memory_space=pltpu.SMEM)
HB = pl.BlockSpec(memory_space=pltpu.HBM)
ANY = pl.BlockSpec(memory_space=pl.ANY)
NN = (((1,), (0,)), ((), ()))
NT = (((1,), (1,)), ((), ()))
FORWARD_AT = (0, 1, 3, 4)
BACKWARD_AT = (8, 7, 5, 4)
TICKS = MICRO + 8
SLOW = (1, 2)


def vmem(value):
    return pltpu.with_memory_space_constraint(value, pltpu.VMEM)


def hbm(value):
    return pltpu.with_memory_space_constraint(value, pltpu.HBM)


def vshape(shape, dtype):
    return pltpu.VMEM(shape, dtype)


def hshape(shape, dtype):
    return jax.ShapeDtypeStruct(shape, dtype)


def params():
    return pltpu.CompilerParams(vmem_limit_bytes=6 * 2**20)


def mm(a, b, dims):
    return lax.dot_general(a, b, dims, preferred_element_type=F32)


def coded(values):
    top = jnp.max(jnp.abs(values), axis=1, keepdims=True) + 1e-06
    scale = top.astype(BF16).astype(F32)
    code = (values * (1.0 / scale)).astype(BF16)
    return code, scale


def received(codes, slow_here, lanes):
    if len(codes) == 1:
        return codes[0][:, lanes]
    return jnp.where(slow_here, codes[1][:, lanes], codes[0][:, lanes])


def hand_out(wires, outs, code, slow_here):
    for wire, out in zip(wires, outs):

        @pl.when(slow_here if wire == "slow" else jnp.logical_not(slow_here))
        def _(out=out):
            out[...] = code[...]


FORWARD_PAIRS = [(s, s + 1) for s in range(SECTIONS - 1)]
BACKWARD_PAIRS = [(s, s - 1) for s in range(1, SECTIONS)]


def live(tick, pairs, at, wire):
    return [
        pair for pair in pairs if 0 <= tick - at[pair[0]] < MICRO and (set(pair) == set(SLOW)) == (wire == "slow")
    ]


def fetch_kernel(inputs, cotangent, table_in, table_out, after, heights, grads, base_in, base_out, *rest):
    sems = rest[-1]
    moves = [(inputs, heights), (cotangent, grads), (table_in, base_in), (table_out, base_out)]
    copies = [pltpu.make_async_copy(source, target, sems.at[i]) for i, (source, target) in enumerate(moves)]
    for copy in copies:
        copy.start()
    for copy in copies:
        copy.wait()


def fetch(inputs, cotangent, table_in, table_out, after):
    return pl.pallas_call(
        fetch_kernel,
        out_shape=(
            vshape(inputs.shape, BF16),
            vshape(cotangent.shape, BF16),
            vshape(table_in.shape, BF16),
            vshape(table_out.shape, BF16),
            vshape((TOKENS, RANK), F32),
            vshape((TOKENS, BLOCK), F32),
            vshape((TOKENS, RANK), BF16),
            vshape((TOKENS, RANK), BF16),
            vshape((TOKENS, D), BF16),
            vshape((TOKENS, D), BF16),
            vshape((TOKENS, D), BF16),
        ),
        in_specs=[HB] * 4 + [ANY],
        out_specs=(VM,) * 11,
        scratch_shapes=[pltpu.SemaphoreType.DMA((4,))],
        compiler_params=params(),
        cost_estimate=pl.CostEstimate(flops=0, bytes_accessed=20 * 2**20, transcendentals=0),
        name="fetch",
    )(hbm(inputs), hbm(cotangent), hbm(table_in), hbm(table_out), after)


def settle(meta, first, full, ref, r, start, stop):
    for q in range(start, stop):
        for p in range(NY):
            z = lax.rem(meta[0] + (r if first else q), NZ)
            x = lax.rem(meta[2] + (q if first else r), NX)
            y = lax.rem(meta[1] + p, NY)
            at = pl.multiple_of((z * NY * NX + y * NX + x) * PIECE, PIECE)
            k = ((q - start) * NY + p) * PIECE
            full[pl.ds(at, PIECE), :] = ref[k : k + PIECE, :]


def near_kernel(meta, *refs):
    for which in range(2):
        own, after, before = refs[3 * which : 3 * which + 3]
        full = refs[6 + which]
        settle(meta, which == 0, full, own, 0, 0, 4)
        settle(meta, which == 0, full, after, 1, 0, 4)
        settle(meta, which == 0, full, before, 3, 0, 4)


def far_kernel(meta, *refs):
    for which in range(2):
        top, bottom = refs[2 * which : 2 * which + 2]
        full = refs[6 + which]
        settle(meta, which == 0, full, top, 2, 0, 2)
        settle(meta, which == 0, full, bottom, 2, 2, 4)


def assemble(meta, parts_in, parts_out):
    shapes = (vshape((D, RANK), BF16),) * 2
    near = parts_in[:3] + parts_out[:3]
    full = small_call(near_kernel, "assemble_near", shapes, *near, meta=meta)
    far = parts_in[3:] + parts_out[3:]
    return small_call(far_kernel, "assemble_far", shapes, *far, *full, meta=meta, aliases={5: 0, 6: 1})


def both_kernel(one, two, out, sems):
    copies = [
        pltpu.make_async_copy(ref, out.at[pl.ds(i * PIECE, PIECE)], sems.at[i]) for i, ref in enumerate((one, two))
    ]
    for copy in copies:
        copy.start()
    for copy in copies:
        copy.wait()


def stacked(one, two):
    return pl.pallas_call(
        both_kernel,
        out_shape=vshape((2 * PIECE, RANK), BF16),
        in_specs=[HB] * 2,
        out_specs=VM,
        scratch_shapes=[pltpu.SemaphoreType.DMA((2,))],
        compiler_params=params(),
        name="both",
    )(hbm(one), hbm(two))


def rows_kernel(plan, n_in, *refs):
    for source, at, rows, target, to in plan:
        refs[n_in + target][to : to + rows, :] = refs[source][at : at + rows, :]


def arranged(name, args, *outs):
    plan, sizes = [], []
    for target, pieces in enumerate(outs):
        to = 0
        for source, at, rows in pieces:
            plan.append((source, at, rows, target, to))
            to += rows
        sizes.append(to)
    shapes = tuple(vshape((size,) + args[0].shape[1:], args[0].dtype) for size in sizes)
    return small_call(functools.partial(rows_kernel, plan, len(args)), name, shapes, *args)


def forward_kernel(tick, n_codes, wires, meta, *refs):
    codes, refs = refs[:n_codes], refs[n_codes:]
    (
        base_in, base_out, gain, w_in, w_out, heights_, pres_, rstds_, acts_, results_, fresh_,
        *code_out, heights, pres, rstds, acts, results, fresh,
        sum_buf, square_buf, code_new,
    ) = refs
    section = meta[3]
    slot = tick - (section + (section >= SLOW[1]).astype(jnp.int32))

    @pl.when((slot >= 0) & (slot < MICRO))
    def _():
        sample = meta[4 + slot]
        rows = pl.ds(pl.multiple_of(slot * SEQ, SEQ), SEQ)

        def project(decode):
            if decode:
                scales = received(codes, section == SLOW[1], slice(D, WIDE)).astype(F32)
            pre = jnp.zeros((SEQ, RANK), F32)
            square = jnp.zeros((SEQ, BLOCK), F32)
            for i in range(D // PIECE):
                scaled = []
                for half in range(PIECE // BLOCK):
                    b = i * (PIECE // BLOCK) + half
                    lanes = slice(b * BLOCK, (b + 1) * BLOCK)
                    if decode:
                        value = received(codes, section == SLOW[1], lanes).astype(F32) * scales[:, b : b + 1]
                        height = (base_in[sample, :, lanes].astype(F32) + value).astype(BF16)
                        heights[rows, lanes] = height
                    else:
                        height = heights[rows, lanes]
                    h = height.astype(F32)
                    square += h * h
                    scaled.append((h * gain[:, lanes]).astype(BF16))
                pre += mm(jnp.concatenate(scaled, axis=1), w_in[i * PIECE : (i + 1) * PIECE, :], NN)
            sum_buf[...] = pre
            square_buf[...] = square

        if codes:

            @pl.when(section > 0)
            def _():
                project(True)

        if 0 <= tick - FORWARD_AT[0] < MICRO:

            @pl.when(section == 0)
            def _():
                project(False)

        rstd = lax.rsqrt(jnp.sum(square_buf[...], axis=1, keepdims=True) * (1.0 / D) + 1e-05)
        pre = sum_buf[...] * rstd
        act = (pre / (1.0 + jnp.exp(-pre))).astype(BF16)
        pres[rows, :] = pre
        rstds[rows, :] = jnp.broadcast_to(rstd, (SEQ, BLOCK))
        acts[rows, :] = act
        lane = lax.broadcasted_iota(jnp.int32, (SEQ, BLOCK), 1)
        scales_new = jnp.zeros((SEQ, BLOCK), F32)
        for i in range(D // PIECE):
            branch = mm(act, w_out[i * PIECE : (i + 1) * PIECE, :], NT)
            for half in range(PIECE // BLOCK):
                b = i * (PIECE // BLOCK) + half
                lanes = slice(b * BLOCK, (b + 1) * BLOCK)
                part = branch[:, half * BLOCK : (half + 1) * BLOCK]
                result = (heights[rows, lanes].astype(F32) + part).astype(BF16)
                results[rows, lanes] = result
                if not code_out:
                    continue
                base = base_out[sample, :, lanes].astype(F32)
                new, scale = coded(result.astype(F32) - base)
                code_new[:, lanes] = new
                fresh[rows, lanes] = (base + new.astype(F32) * scale).astype(BF16)
                scales_new = jnp.where(lane == b, scale, scales_new)
        if code_out:
            code_new[:, D:] = scales_new.astype(BF16)
            hand_out(wires, code_out, code_new, section == SLOW[0])


def forward_tick(tick, meta, codes, base_in, base_out, gain, w_in, w_out, state):
    heights, pres, rstds, acts, results, fresh = state
    first = 1 + len(codes) + 5
    wires = [wire for wire in ("fast", "slow") if live(tick, FORWARD_PAIRS, FORWARD_AT, wire)]
    made = [vshape((SEQ, WIDE), BF16)] * len(wires)
    out = pl.pallas_call(
        functools.partial(forward_kernel, tick, len(codes), wires),
        out_shape=(
            *made,
            vshape(heights.shape, BF16),
            vshape(pres.shape, F32),
            vshape(rstds.shape, F32),
            vshape(acts.shape, BF16),
            vshape(results.shape, BF16),
            vshape(fresh.shape, BF16),
        ),
        in_specs=[SM] + [VM] * (len(codes) + 5 + 6),
        out_specs=(VM,) * (6 + len(made)),
        scratch_shapes=[
            pltpu.VMEM((SEQ, RANK), F32),
            pltpu.VMEM((SEQ, BLOCK), F32),
            pltpu.VMEM((SEQ, WIDE), BF16),
        ],
        input_output_aliases={first + i: len(made) + i for i in range(6)},
        compiler_params=params(),
        cost_estimate=pl.CostEstimate(flops=2 * 2 * SEQ * D * RANK, bytes_accessed=16 * 2**20, transcendentals=0),
        name="forward_tick",
    )(
        meta, *map(vmem, codes), vmem(base_in), vmem(base_out), vmem(gain), vmem(w_in), vmem(w_out),
        vmem(heights), vmem(pres), vmem(rstds), vmem(acts), vmem(results), vmem(fresh),
    )
    return dict(zip(wires, out)), out[len(made) :]


def backward_kernel(tick, n_codes, n_started, wires, meta, *refs):
    codes, refs = refs[:n_codes], refs[n_codes + n_started :]
    (
        heights, pres, rstds, gain, w_in, w_out, grads_, dpres_, ingrads_,
        *code_out, grads, dpres, ingrads,
        sum_buf, code_new,
    ) = refs
    section = meta[3]
    slot = tick - BACKWARD_AT[-1] - (SECTIONS - 1 - section + (section <= SLOW[0]).astype(jnp.int32))

    @pl.when((slot >= 0) & (slot < MICRO))
    def _():
        rows = pl.ds(pl.multiple_of(slot * SEQ, SEQ), SEQ)

        def project(decode):
            if decode:
                scales = received(codes, section == SLOW[0], slice(D, WIDE)).astype(F32)
            down = jnp.zeros((SEQ, RANK), F32)
            for i in range(D // PIECE):
                if decode:
                    for half in range(PIECE // BLOCK):
                        b = i * (PIECE // BLOCK) + half
                        lanes = slice(b * BLOCK, (b + 1) * BLOCK)
                        value = received(codes, section == SLOW[0], lanes).astype(F32) * scales[:, b : b + 1]
                        grads[rows, lanes] = value.astype(BF16)
                piece = slice(i * PIECE, (i + 1) * PIECE)
                down += mm(grads[rows, piece], w_out[piece, :], NN)
            sum_buf[...] = down

        if codes:

            @pl.when(section < SECTIONS - 1)
            def _():
                project(True)

        if 0 <= tick - BACKWARD_AT[-1] < MICRO:

            @pl.when(section == SECTIONS - 1)
            def _():
                project(False)

        pre = pres[rows, :]
        rstd = rstds[rows, :]
        sig = 1.0 / (1.0 + jnp.exp(-pre))
        dpre = (sum_buf[...] * sig * (1.0 + pre * (1.0 - sig))).astype(BF16)
        dpres[rows, :] = dpre
        inner = jnp.sum(dpre.astype(F32) * pre, axis=1, keepdims=True) * (1.0 / D)
        pull = rstd * rstd * inner
        lane = lax.broadcasted_iota(jnp.int32, (SEQ, BLOCK), 1)
        scales_new = jnp.zeros((SEQ, BLOCK), F32)
        for i in range(D // PIECE):
            dnorm = mm(dpre, w_in[i * PIECE : (i + 1) * PIECE, :], NT)
            for half in range(PIECE // BLOCK):
                b = i * (PIECE // BLOCK) + half
                lanes = slice(b * BLOCK, (b + 1) * BLOCK)
                extra = dnorm[:, half * BLOCK : (half + 1) * BLOCK] * gain[:, lanes]
                dh = (
                    grads[rows, lanes].astype(F32)
                    + rstd * extra
                    - heights[rows, lanes].astype(F32) * pull
                )
                ingrads[rows, lanes] = dh.astype(BF16)
                if code_out:
                    new, scale = coded(dh)
                    code_new[:, lanes] = new
                    scales_new = jnp.where(lane == b, scale, scales_new)
        if code_out:
            code_new[:, D:] = scales_new.astype(BF16)
            hand_out(wires, code_out, code_new, section == SLOW[1])


def backward_tick(tick, meta, codes, begun, heights, pres, rstds, gain, w_in, w_out, state):
    grads, dpres, ingrads = state
    wires = [wire for wire in ("fast", "slow") if live(tick, BACKWARD_PAIRS, BACKWARD_AT, wire)]
    made = [vshape((SEQ, WIDE), BF16)] * len(wires)
    shared = [wire for wire in wires if wire in begun]
    first = 1 + len(codes) + len(shared) + 6
    aliases = {1 + len(codes) + i: wires.index(wire) for i, wire in enumerate(shared)}
    out = pl.pallas_call(
        functools.partial(backward_kernel, tick, len(codes), len(shared), wires),
        out_shape=(
            *made,
            vshape(grads.shape, BF16),
            vshape(dpres.shape, BF16),
            vshape(ingrads.shape, BF16),
        ),
        in_specs=[SM] + [VM] * (len(codes) + len(shared) + 6 + 3),
        out_specs=(VM,) * (3 + len(made)),
        scratch_shapes=[pltpu.VMEM((SEQ, RANK), F32), pltpu.VMEM((SEQ, WIDE), BF16)],
        input_output_aliases=aliases | {first + i: len(made) + i for i in range(3)},
        compiler_params=params(),
        cost_estimate=pl.CostEstimate(flops=2 * 2 * SEQ * D * RANK, bytes_accessed=16 * 2**20, transcendentals=0),
        name="backward_tick",
    )(
        meta, *map(vmem, codes), *[vmem(begun[wire]) for wire in shared],
        vmem(heights), vmem(pres), vmem(rstds), vmem(gain), vmem(w_in), vmem(w_out),
        vmem(grads), vmem(dpres), vmem(ingrads),
    )
    return begun | dict(zip(wires, out)), out[len(made) :]


def double_kernel(tick, came, f_came, b_came, wires, f_wires, b_wires, meta, *refs):
    refs = list(refs)
    take = lambda n: [refs.pop(0) for _ in range(n)]
    codes = dict(zip(came, take(len(came))))
    bases, (gain, w_in, w_out), old = take(2), take(3), take(9)
    outs, new = dict(zip(wires, take(len(wires)))), take(9)
    sum_buf, square_buf, code_new = refs
    forward_kernel(
        tick, len(f_came), f_wires, meta, *[codes[wire] for wire in f_came], *bases, gain, w_in, w_out, *old[:6],
        *[outs[wire] for wire in f_wires], *new[:6], sum_buf, square_buf, code_new,
    )
    backward_kernel(
        tick, len(b_came), 0, b_wires, meta, *[codes[wire] for wire in b_came], *new[:3], gain, w_in, w_out, *old[6:],
        *[outs[wire] for wire in b_wires], *new[6:], sum_buf, code_new,
    )


def double_tick(tick, meta, codes, f_came, b_came, base_in, base_out, gain, w_in, w_out, state, back):
    came = [wire for wire in codes if wire in f_came or wire in b_came]
    f_wires = [wire for wire in ("fast", "slow") if live(tick, FORWARD_PAIRS, FORWARD_AT, wire)]
    b_wires = [wire for wire in ("fast", "slow") if live(tick, BACKWARD_PAIRS, BACKWARD_AT, wire)]
    wires = [wire for wire in ("fast", "slow") if wire in f_wires or wire in b_wires]
    kept = (*state, *back)
    first = 1 + len(came) + 5
    out = pl.pallas_call(
        functools.partial(double_kernel, tick, came, f_came, b_came, wires, f_wires, b_wires),
        out_shape=(*[vshape((SEQ, WIDE), BF16)] * len(wires), *[vshape(v.shape, v.dtype) for v in kept]),
        in_specs=[SM] + [VM] * (len(came) + 5 + 9),
        out_specs=(VM,) * (len(wires) + 9),
        scratch_shapes=[
            pltpu.VMEM((SEQ, RANK), F32),
            pltpu.VMEM((SEQ, BLOCK), F32),
            pltpu.VMEM((SEQ, WIDE), BF16),
        ],
        input_output_aliases={first + i: len(wires) + i for i in range(9)},
        compiler_params=params(),
        cost_estimate=pl.CostEstimate(flops=4 * 2 * SEQ * D * RANK, bytes_accessed=32 * 2**20, transcendentals=0),
        name="double_tick",
    )(
        meta, *[vmem(codes[wire]) for wire in came], vmem(base_in), vmem(base_out), vmem(gain), vmem(w_in), vmem(w_out),
        *map(vmem, kept),
    )
    return dict(zip(wires, out)), out[len(wires) : len(wires) + 6], out[len(wires) + 6 :]


def flush_kernel(
    meta, heights, results, fresh, ingrads, base_in, base_out, after, results_out, ingrads_out, new_in, new_out, sems
):
    section = meta[3]
    unused = 10 - (meta[4] + meta[5] + meta[6] + meta[7])
    always = [(results, results_out), (ingrads, ingrads_out), (base_in.at[unused], new_in.at[unused])]
    always.append((base_out.at[unused], new_out.at[unused]))
    copies = [pltpu.make_async_copy(source, target, sems.at[i]) for i, (source, target) in enumerate(always)]

    def table(rows_of, base, new, first):
        fresh_ones, old_ones = [], []
        for j in range(MICRO):
            target, sem = new.at[meta[4 + j]], sems.at[first + j]
            fresh_ones.append(pltpu.make_async_copy(rows_of.at[pl.ds(j * SEQ, SEQ)], target, sem))
            old_ones.append(pltpu.make_async_copy(base.at[meta[4 + j]], target, sem))
        return fresh_ones, old_ones

    received, kept_in = table(heights, base_in, new_in, 4)
    sent, kept_out = table(fresh, base_out, new_out, 4 + MICRO)
    groups = [
        (section > 0, received),
        (section == 0, kept_in),
        (section < SECTIONS - 1, sent),
        (section == SECTIONS - 1, kept_out),
    ]

    def run(act):
        for copy in copies:
            act(copy)
        for condition, group in groups:

            @pl.when(condition)
            def _(group=group):
                for copy in group:
                    act(copy)

    run(lambda copy: copy.start())
    run(lambda copy: copy.wait())


def flush(meta, heights, results, fresh, ingrads, base_in, base_out, after):
    return pl.pallas_call(
        flush_kernel,
        out_shape=(
            hshape(results.shape, BF16),
            hshape(ingrads.shape, BF16),
            hshape(base_in.shape, BF16),
            hshape(base_out.shape, BF16),
        ),
        in_specs=[SM] + [VM] * 6 + [ANY],
        out_specs=(HB,) * 4,
        scratch_shapes=[pltpu.SemaphoreType.DMA((4 + 2 * MICRO,))],
        compiler_params=params(),
        cost_estimate=pl.CostEstimate(flops=0, bytes_accessed=16 * 2**20, transcendentals=0),
        name="flush",
    )(meta, *map(vmem, (heights, results, fresh, ingrads, base_in, base_out)), after)


def grad_lanes(meta, which, r, i):
    if which == 0:
        z = lax.rem(meta[0] + r, NZ)
        return pl.ds(pl.multiple_of((z * NY * NX + i) * PIECE, PIECE), PIECE)
    x = lax.rem(meta[2] + r, NX)
    return pl.ds(pl.multiple_of((i * NX + x) * PIECE, PIECE), PIECE)


def left_sides(rstds, dpres, acts):
    return (dpres[...].astype(F32) * rstds[:, :1]).T.astype(BF16), acts[...].astype(F32).T.astype(BF16)


def right_side(which, lanes, heights, grads, gain):
    if which == 0:
        return (heights[:, lanes].astype(F32) * gain[:, lanes]).astype(BF16)
    return grads[:, lanes]


def far_grad_kernel(meta, heights, grads, rstds, dpres, acts, gain, *outs):
    left = left_sides(rstds, dpres, acts)
    for which in range(2):
        for i in range(NY * 4):
            product = mm(left[which], right_side(which, grad_lanes(meta, which, 2, i), heights, grads, gain), NN)
            product = product.astype(BF16)
            for half in range(2):
                outs[2 * which + half][:, i * PIECE : (i + 1) * PIECE] = product[half * 128 : (half + 1) * 128]


def near_grad_kernel(meta, heights, grads, rstds, dpres, acts, gain, *outs):
    left = left_sides(rstds, dpres, acts)
    for which in range(2):
        for k, r in enumerate((1, 3, 0)):
            for i in range(NY * 4):
                product = mm(left[which], right_side(which, grad_lanes(meta, which, r, i), heights, grads, gain), NN)
                outs[3 * which + k][:, i * PIECE : (i + 1) * PIECE] = product.astype(BF16)


def add_kernel(*refs):
    for which in range(2):
        ahead, behind, top, bottom = refs[4 * which : 4 * which + 4]
        ahead_new, behind_new = refs[8 + 2 * which : 10 + 2 * which]
        for i in range(4):
            lanes = slice(i * 512, (i + 1) * 512)
            ahead_new[:128, lanes] = (ahead[:128, lanes].astype(F32) + top[:, lanes].astype(F32)).astype(BF16)
            ahead_new[128:, lanes] = ahead[128:, lanes]
            behind_new[:128, lanes] = behind[:128, lanes]
            behind_new[128:, lanes] = (behind[128:, lanes].astype(F32) + bottom[:, lanes].astype(F32)).astype(BF16)


def sum_one_kernel(meta, *refs):
    gin, gout, outs = refs[:3], refs[3:6], refs[6:]
    for r in range(NX):
        for y in range(NY):
            x = lax.rem(meta[2] + r, NX)
            lanes = pl.ds(pl.multiple_of((y * NX + x) * PIECE, PIECE), PIECE)
            total = sum(ref[:, lanes].astype(F32) for ref in gin)
            outs[r][:, y * PIECE : (y + 1) * PIECE] = total.astype(BF16)
    for r in range(NZ):
        for y in range(NY):
            z = lax.rem(meta[0] + r, NZ)
            lanes = pl.ds(pl.multiple_of((z * NY + y) * PIECE, PIECE), PIECE)
            total = sum(ref[:, lanes].astype(F32) for ref in gout)
            outs[NX + r][:, y * PIECE : (y + 1) * PIECE] = total.astype(BF16)


def sum_two_kernel(meta, *refs):
    gin, gout, (keep, send) = refs[:NX], refs[NX : NX + NZ], refs[NX + NZ :]
    for which, group in enumerate((gin, gout)):
        for p, out in enumerate((keep, send)):
            y = lax.rem(meta[1] + p, NY)
            lanes = pl.ds(pl.multiple_of(y * PIECE, PIECE), PIECE)
            out[which] = sum(ref[:, lanes].astype(F32) for ref in group).astype(BF16)


def sum_three_kernel(keep, got, gin, gout):
    gin[...] = (keep[0].astype(F32) + got[0].astype(F32)).T
    gout[...] = (keep[1].astype(F32) + got[1].astype(F32)).T


def small_call(kernel, name, shapes, *args, meta=None, aliases={}):
    scalars = [] if meta is None else [meta]
    return pl.pallas_call(
        kernel,
        out_shape=shapes,
        in_specs=[SM] * len(scalars) + [VM] * len(args),
        out_specs=(VM,) * len(shapes),
        input_output_aliases=aliases,
        compiler_params=params(),
        cost_estimate=pl.CostEstimate(flops=0, bytes_accessed=8 * 2**20, transcendentals=0),
        name=name,
    )(*scalars, *map(vmem, args))


def place(z, y, x):
    return (z * NY + y) * NX + x


def moved(value, shift):
    dz, dy, dx = shift
    pairs = []
    for z in range(NZ):
        for y in range(NY):
            for x in range(NX):
                source = place((z + dz) % NZ, (y + dy) % NY, (x + dx) % NX)
                pairs.append((source, place(z, y, x)))
    return lax.ppermute(value, "dp", pairs)


def along(axis, steps):
    return (steps, 0, 0) if axis == 0 else (0, 0, steps)


def gathered(meta, shard_in, shard_out):
    both = stacked(shard_in, shard_out)
    other = moved(both, (0, 1, 0))
    rows, half = 2 * PIECE, 4 * PIECE
    pair_in, pair_out = arranged(
        "pairs", (both, other), [(0, 0, PIECE), (1, 0, PIECE)], [(0, PIECE, PIECE), (1, PIECE, PIECE)]
    )
    parts = [pair_in, pair_out]
    for r in (2, 1, 3):
        parts += [moved(pair_in, along(2, r)), moved(pair_out, along(0, r))]
    four_in, four_out = arranged(
        "fours", parts, [(i, 0, rows) for i in (0, 4, 2, 6)], [(i, 0, rows) for i in (1, 5, 3, 7)]
    )
    near_in = [four_in, moved(four_in, along(0, 1)), moved(four_in, along(0, -1))]
    near_out = [four_out, moved(four_out, along(2, 1)), moved(four_out, along(2, -1))]
    came = (near_in[2], near_in[1], near_out[2], near_out[1])
    cuts = arranged("cuts", came, *[[(i, half * (i % 2), half)] for i in range(4)])
    far_in = [moved(cuts[0], along(0, -1)), moved(cuts[1], along(0, 1))]
    far_out = [moved(cuts[2], along(2, -1)), moved(cuts[3], along(2, 1))]
    return assemble(meta, near_in + far_in, near_out + far_out), pair_in


def reduced(meta, operands):
    rows = RANK // 2
    far = small_call(far_grad_kernel, "far_grads", (vshape((rows, 2048), BF16),) * 4, *operands, meta=meta)
    near = small_call(near_grad_kernel, "near_grads", (vshape((RANK, 2048), BF16),) * 6, *operands, meta=meta)
    args, own = [], []
    for which, axis in ((0, 0), (1, 2)):
        top, bottom = far[2 * which : 2 * which + 2]
        ahead, behind, here = near[3 * which : 3 * which + 3]
        args += [ahead, behind, moved(top, along(axis, -1)), moved(bottom, along(axis, 1))]
        own.append(here)
    added = small_call(add_kernel, "add_far", (vshape((RANK, 2048), BF16),) * 4, *args)
    args = []
    for which, axis in ((0, 0), (1, 2)):
        ahead, behind = added[2 * which : 2 * which + 2]
        args += [own[which], moved(ahead, along(axis, -1)), moved(behind, along(axis, 1))]
    shapes = tuple(vshape((RANK, NY * PIECE), BF16) for _ in range(NX + NZ))
    two = small_call(sum_one_kernel, "sum_one", shapes, *args, meta=meta)
    gin, gout = two[:NX], two[NX:]
    gin = [gin[0]] + [moved(gin[r], along(2, -r)) for r in (1, 2, 3)]
    gout = [gout[0]] + [moved(gout[r], along(0, -r)) for r in (1, 2, 3)]
    shapes = (vshape((2, RANK, PIECE), BF16),) * 2
    keep, send = small_call(sum_two_kernel, "sum_two", shapes, *gin, *gout, meta=meta)
    got = moved(send, (0, 1, 0))
    return (*small_call(sum_three_kernel, "sum_three", (hshape((PIECE, RANK), F32),) * 2, keep, got), far[0])


def body(inputs, cotangent, sample_ids, out_bases, in_bases, proj_in, proj_out, gains):
    section = lax.axis_index("section")
    dp = lax.axis_index("dp")
    place_ids = jnp.stack([dp // (NY * NX), (dp // NX) % NY, dp % NX, section])
    meta = jnp.concatenate([place_ids.astype(jnp.int32), sample_ids[0]])
    (w_in, w_out), after = gathered(meta, proj_in[0], proj_out[0])
    heights, grads, base_in, base_out, pres, rstds, acts, dpres, results, fresh, ingrads = fetch(
        inputs, cotangent, in_bases[0], out_bases[0], after
    )
    state = (heights, pres, rstds, acts, results, fresh)
    back = (grads, dpres, ingrads)
    fast, slow, sent = None, None, None
    for tick in range(TICKS):
        codes = {"fast": fast, "slow": slow}

        def arrived(pairs, at):
            return [wire for wire, ago in (("fast", 1), ("slow", 2)) if live(tick - ago, pairs, at, wire)]

        f_came, b_came = arrived(FORWARD_PAIRS, FORWARD_AT), arrived(BACKWARD_PAIRS, BACKWARD_AT)
        bases = (base_in, base_out)
        if tick < BACKWARD_AT[-1]:
            came = [codes[wire] for wire in f_came]
            out, state = forward_tick(tick, meta, came, *bases, gains, w_in, w_out, state)
        elif tick < FORWARD_AT[-1] + MICRO:
            out, state, back = double_tick(tick, meta, codes, f_came, b_came, *bases, gains, w_in, w_out, state, back)
        else:
            came = [codes[wire] for wire in b_came]
            out, back = backward_tick(tick, meta, came, {}, *state[:3], gains, w_in, w_out, back)

        def hop(wire):
            pairs = live(tick, FORWARD_PAIRS, FORWARD_AT, wire) + live(tick, BACKWARD_PAIRS, BACKWARD_AT, wire)
            return lax.ppermute(out[wire], "section", pairs) if pairs else None

        slow, sent = sent, hop("slow")
        fast = hop("fast")
    heights, pres, rstds, acts, results, fresh = state
    grads, dpres, ingrads = back
    grad_in, grad_out, after = reduced(meta, (heights, grads, rstds, dpres, acts, gains))
    results, ingrads, new_in, new_out = flush(meta, heights, results, fresh, ingrads, base_in, base_out, after)
    return results[None], ingrads[None], new_out[None], new_in[None], grad_in[None], grad_out[None]


def solution(mesh):
    in_specs = (
        P("dp", None),
        P("dp", None),
        P("dp", None),
        P("section", "dp", None, None),
        P("section", "dp", None, None),
        P("section", "dp", None),
        P("section", "dp", None),
        P("section", None),
    )
    out_specs = (
        P("section", "dp", None),
        P("section", "dp", None),
        P("section", "dp", None, None),
        P("section", "dp", None, None),
        P("section", "dp", None),
        P("section", "dp", None),
    )
    return jax.shard_map(body, mesh=mesh, in_specs=in_specs, out_specs=out_specs, check_vma=False)
```
